32 devices in a mesh: lat: 4 (over y, core), lon: 8 (over z, x).
Axes of the slice: x: 2, y: 2, z: 4, core: 2. Of those that a mesh axis runs over, the one named last changes fastest.
Arguments:
- field: float32 [256, 4, 1024], P(None, 'lat', 'lon'), may hold values from -6 to 6
- cotangent: float32 [256, 4, 1024], P(None, 'lat', 'lon'), may hold values from -6 to 6
- conv_weight: float32 [3, 3, 256, 256], replicated, may hold values from -0.125 to 0.125
- spectral_filter: float32 [2, 256, 1024], P(None, None, 'lon'), may hold values from -6 to 6
Outputs:
- output: float32 [256, 4, 1024], P(None, 'lat', 'lon')
- input_grad: float32 [256, 4, 1024], P(None, 'lat', 'lon')
- filter_grad: float32 [2, 256, 1024], P(None, None, 'lon')
The draws below stay inside these ranges and needn't reach their ends.
All inputs are finite; a program needn't handle non-finite values.
Results may differ from the reference program's by a relative error of at most 0.00014.
Values sent between devices are 32-bit elements; how exact they have to be, the bound alone decides.
No kernel may reach another device: no remote copies, remote signals or barrier semaphores. Data moves between devices by JAX's collectives and lax.ppermute only.
A program may use at most 64 MiB of HBM per device.

```python
from functools import partial
import jax
import jax.numpy as jnp
from jax import lax

C = 256
LON_DEV = 128
NLAT = 4
NLON = 1024
N_LON = 8


def shard_levels(own_key, extent, shards, low, largest):
    loudness, own = 1.0, jax.random.fold_in(own_key, 6)
    for position, parts in shards:
        draws = jnp.exp(jax.random.uniform(jax.random.fold_in(own, position), (parts,), jnp.float32, low / len(shards), largest / len(shards)))
        loudness = loudness * jnp.repeat(draws, extent[position] // parts).reshape([-1 if axis == position else 1 for axis in range(len(extent))])
    return loudness


def bell_draw(key, dims, width, reach, split=(), kind=jnp.bfloat16):
    result = width * jax.random.normal(key, dims, jnp.float32)
    if split:
        result = result * shard_levels(key, dims, split, -0.22, 0.18)
    return jnp.clip(result, -reach, reach).astype(kind)


def setup_inputs(seed: int = 0) -> dict:
    splits = jax.random.split(jax.random.key(seed), 5)
    return {
        "field": bell_draw(splits[0], (C, NLAT, NLON), 1.0, 6.0, ((1, 4), (2, 8)), jnp.float32),
        "cotangent": bell_draw(splits[1], (C, NLAT, NLON), 1.0, 6.0, ((1, 4), (2, 8)), jnp.float32),
        "conv_weight": bell_draw(splits[2], (3, 3, C, C), (9 * C) ** -0.5, 0.125, (), jnp.float32),
        "spectral_filter": bell_draw(splits[3], (2, C, NLON), 1.0, 6.0, ((2, 8),), jnp.float32),
    }


precise = lax.Precision.HIGHEST

def pad_field(field):
    padded = jnp.pad(field, ((0, 0), (1, 1), (0, 0)))
    return jnp.concatenate([padded[:, :, -1:], padded, padded[:, :, :1]], axis=2)

def apply_taps(padded, taps, lat_rows, columns):
    total = jnp.zeros((taps.shape[2], lat_rows, columns), jnp.float32)
    for tap_row in range(3):
        for tap_col in range(3):
            window = padded[:, tap_row:tap_row + lat_rows, tap_col:tap_col + columns]
            total = total + jnp.einsum('oi,iab->oab', taps[tap_row, tap_col], window, precision=precise)
    return total

def natural_order(spectral_filter):
    places = jnp.arange(NLON, dtype=jnp.int32)
    residue = places % N_LON
    width_bits = N_LON.bit_length() - 1
    flipped = jnp.zeros((NLON,), jnp.int32)
    for bit_pos in range(width_bits):
        flipped = flipped + residue // 2 ** bit_pos % 2 * 2 ** (width_bits - 1 - bit_pos)
    column = (LON_DEV * flipped + places // N_LON).astype(jnp.int32)
    return (spectral_filter[0][:, column], spectral_filter[1][:, column])

def layer(conv_weight, field, spectral_filter):
    mixed = apply_taps(pad_field(field), conv_weight, NLAT, NLON)
    gain_real, gain_imag = natural_order(spectral_filter)
    gain = (gain_real + 1j * gain_imag)[:, None, :]
    spectrum = jnp.fft.fft(mixed, axis=-1)
    shaped = jnp.real(jnp.fft.ifft(gain * spectrum, axis=-1))
    return field + shaped

def reference(field, cotangent, conv_weight, spectral_filter):
    output, pullback = jax.vjp(partial(layer, conv_weight), field, spectral_filter)
    input_grad, filter_grad = pullback(cotangent)
    return (output, input_grad, filter_grad)
```

```python
from functools import partial

import jax
import jax.numpy as jnp
import numpy as np
from jax import lax
from jax.experimental import pallas as pl
from jax.experimental.pallas import tpu as pltpu
from jax.sharding import PartitionSpec as P

precise = lax.Precision.HIGHEST
three_pass = lax.Precision.HIGH
ROOT_HALF = 0.5**0.5


def padded_2(array, sides, width, wrap):
    for axis, dim in sides:
        peers, length = (lax.axis_size(axis), array.shape[dim])
        up = [(i, (i + 1) % peers) for i in range(peers if wrap else peers - 1)]
        down = [(j, i) for i, j in up]
        last = lax.slice_in_dim(array, length - width, length, axis=dim)
        leading = lax.slice_in_dim(array, 0, width, axis=dim)
        before = lax.ppermute(last, axis, up)
        after = lax.ppermute(leading, axis, down)
        array = jnp.concatenate([before, array, after], axis=dim)
    return array


def partner(array, axis, stride):
    return lax.ppermute(array, axis, [(i, i ^ 1 << stride) for i in range(lax.axis_size(axis))])


def angle_table(first, second, modulus):
    product = first[:, None] * second[None, :] % modulus
    return 2.0 * jnp.pi / modulus * product.astype(jnp.float32)


def apply_taps(padded, taps, lat_rows, columns):
    total = jnp.zeros((taps.shape[2], lat_rows, columns), jnp.float32)
    for tap_row in range(3):
        for tap_col in range(3):
            window = padded[:, tap_row : tap_row + lat_rows, tap_col : tap_col + columns]
            total = total + jnp.einsum(
                "oi,iab->oab", taps[tap_row, tap_col], window, precision=precise
            )
    return total


def with_rims(field):
    wider = padded_2(field, (("lon", 2),), 1, True)
    return padded_2(wider, (("lat", 1),), 1, False)


def local_forward(real_part, imag_part):
    columns = real_part.shape[-1]
    places = lax.iota(jnp.int32, columns)
    angles = angle_table(places, places, columns)
    cosine = jnp.cos(angles)
    sine = jnp.sin(angles)
    out_real = jnp.dot(real_part, cosine, precision=precise) + jnp.dot(
        imag_part, sine, precision=precise
    )
    out_imag = jnp.dot(imag_part, cosine, precision=precise) - jnp.dot(
        real_part, sine, precision=precise
    )
    return (out_real, out_imag)


def local_inverse(real_part, imag_part):
    columns = real_part.shape[-1]
    places = lax.iota(jnp.int32, columns)
    angles = angle_table(places, places, columns)
    cosine = jnp.cos(angles)
    sine = jnp.sin(angles)
    out_real = jnp.dot(real_part, cosine, precision=precise) - jnp.dot(
        imag_part, sine, precision=precise
    )
    out_imag = jnp.dot(imag_part, cosine, precision=precise) + jnp.dot(
        real_part, sine, precision=precise
    )
    return (out_real / columns, out_imag / columns)


def section_angles(place, bit_pos, columns):
    offsets = lax.iota(jnp.int32, columns)
    start = place % 2**bit_pos * columns
    span = 2 * columns * 2**bit_pos
    angles = 2.0 * jnp.pi / span * (start + offsets).astype(jnp.float32)
    upper = place // 2**bit_pos % 2 == 1
    return (jnp.cos(angles), jnp.sin(angles), upper)


def forward_pairs(field):
    extent = lax.axis_size("lon")
    width_bits = extent.bit_length() - 1
    place = lax.axis_index("lon")
    columns = field.shape[-1]
    data = jnp.stack([field, jnp.zeros_like(field)])
    for bit_pos in reversed(range(width_bits)):
        other = partner(data, "lon", bit_pos)
        cosine, sine, upper = section_angles(place, bit_pos, columns)
        differ = other - data
        turned = jnp.stack(
            [differ[0] * cosine + differ[1] * sine, differ[1] * cosine - differ[0] * sine]
        )
        data = jnp.where(upper, turned, data + other)
    out_real, out_imag = local_forward(data[0], data[1])
    return jnp.stack([out_real, out_imag])


def inverse_pairs(spectrum):
    extent = lax.axis_size("lon")
    width_bits = extent.bit_length() - 1
    place = lax.axis_index("lon")
    columns = spectrum.shape[-1]
    back_real, back_imag = local_inverse(spectrum[0], spectrum[1])
    data = jnp.stack([back_real, back_imag])
    for bit_pos in range(width_bits):
        cosine, sine, upper = section_angles(place, bit_pos, columns)
        turned = jnp.stack([data[0] * cosine - data[1] * sine, data[1] * cosine + data[0] * sine])
        outgoing = jnp.where(upper, turned, data)
        other = partner(outgoing, "lon", bit_pos)
        data = jnp.where(upper, other - outgoing, outgoing + other) * 0.5
    return data[0]


def on_device_any_mesh(field, cotangent, conv_weight, spectral_filter):
    lat_rows = field.shape[1]
    columns = field.shape[2]
    total_len = columns * lax.axis_size("lon")
    mixed = apply_taps(with_rims(field), conv_weight, lat_rows, columns)
    hidden_spec = forward_pairs(mixed)
    cot_spec = forward_pairs(cotangent)
    gain_real = spectral_filter[0][:, None, :]
    gain_imag = spectral_filter[1][:, None, :]
    filtered = jnp.stack(
        [
            gain_real * hidden_spec[0] - gain_imag * hidden_spec[1],
            gain_real * hidden_spec[1] + gain_imag * hidden_spec[0],
        ]
    )
    adjoint = jnp.stack(
        [
            gain_real * cot_spec[0] + gain_imag * cot_spec[1],
            gain_real * cot_spec[1] - gain_imag * cot_spec[0],
        ]
    )
    shaped = inverse_pairs(filtered)
    back_field = inverse_pairs(adjoint)
    output = field + shaped
    local_grad = (
        jnp.stack(
            [
                jnp.sum(hidden_spec[0] * cot_spec[0] + hidden_spec[1] * cot_spec[1], axis=1),
                jnp.sum(hidden_spec[0] * cot_spec[1] - hidden_spec[1] * cot_spec[0], axis=1),
            ]
        )
        / total_len
    )
    filter_grad = lax.psum(local_grad, "lat")
    flipped_taps = jnp.transpose(conv_weight[::-1, ::-1], (0, 1, 3, 2))
    input_grad = cotangent + apply_taps(with_rims(back_field), flipped_taps, lat_rows, columns)
    return (output, input_grad, filter_grad)


def reversed_bits(value, width):
    return int(format(value, f"0{width}b")[::-1], 2)


def iotas(rows, columns):
    lane = lax.broadcasted_iota(jnp.int32, (rows, columns), 1)
    row = lax.broadcasted_iota(jnp.int32, (rows, columns), 0)
    return lane, row


def conv_kernel(own_ref, other_ref, cot_ref, filter_ref, taps_ref, out_ref, taps, sems):
    place = lax.axis_index("lat")
    odd = lax.rem(place, 2)
    side = 2 - 2 * odd
    copies = [
        pltpu.make_async_copy(taps_ref.at[1], taps.at[0], sems.at[0]),
        pltpu.make_async_copy(taps_ref.at[side], taps.at[1], sems.at[1]),
    ]
    for copy in copies:
        copy.start()
    channels, columns = own_ref.shape
    owners = channels // 8
    out_ref[:, 0:8, :] = cot_ref[...].reshape(owners, 8, columns)
    plane = filter_ref[place // 2].reshape(owners, 8, columns)
    out_ref[:, 24:28, :] = jnp.where(odd == 0, plane[:, 0:4], plane[:, 4:8])
    own = own_ref[...]
    both = jnp.concatenate([own, other_ref[...]], axis=1)
    for copy in copies:
        copy.wait()
    inner, outer = [], []
    for tap_col in range(3):
        side_part = jnp.dot(taps[1, tap_col], both, precision=three_pass)
        inner.append(
            jnp.dot(taps[0, tap_col], own, precision=three_pass) + side_part[:, columns:]
        )
        outer.append(side_part[:, :columns])
    lane, row = iotas(channels, columns)
    slot = lane - lax.rem(row, 8)
    edges = jnp.zeros((channels, columns), jnp.float32)
    for group, (left, middle, right) in enumerate((inner, outer)):
        from_left = pltpu.roll(left, 1, 1)
        from_right = pltpu.roll(right, columns - 1, 1)
        main = (
            middle
            + jnp.where(lane == 0, 0.0, from_left)
            + jnp.where(lane == columns - 1, 0.0, from_right)
        )
        out_ref[:, 8 + 8 * group : 16 + 8 * group, :] = main.reshape(owners, 8, columns)
        edges = jnp.where(slot == 16 * group, left[:, columns - 1 :], edges)
        edges = jnp.where(slot == 16 * group + 8, right[:, 0:1], edges)
    edge_rows = jnp.sum(edges.reshape(owners, 8, columns), axis=1, keepdims=True)
    out_ref[:, 28:32, :] = jnp.concatenate(
        [edge_rows, jnp.zeros((owners, 3, columns), jnp.float32)], axis=1
    )


def transform_8(x):
    s = [x[d] + x[d + 4] for d in range(4)]
    t = [x[d] - x[d + 4] for d in range(4)]
    plus, minus = ROOT_HALF * (t[1] + t[3]), ROOT_HALF * (t[1] - t[3])
    return [
        (s[0] + s[2] + (s[1] + s[3]), None),
        (t[0] + minus, -t[2] - plus),
        (s[0] - s[2], s[3] - s[1]),
        (t[0] - minus, t[2] - plus),
        (s[0] + s[2] - (s[1] + s[3]), None),
    ]


def spectral_kernel(in_ref, turn_ref, dft_ref, out_ref, work):
    rows, lon = 4, 8
    columns = in_ref.shape[-1]
    lane, sub = iotas(8, columns)
    me = lax.axis_index("lat") * lon + lax.axis_index("lon")
    inward = {1: 2, 2: 1}

    def edge(row, place, group):
        picked = jnp.where(lane == sub + 8 * group, in_ref[row * lon + place, 28:29, :], 0.0)
        if row in inward:
            also = in_ref[inward[row] * lon + place, 28:29, :]
            picked = picked + jnp.where(lane == sub + 8 * group + 16, also, 0.0)
        return jnp.sum(picked, axis=1, keepdims=True)

    grid = []
    for place in range(lon):
        mixed = []
        for row in range(rows):
            tile = in_ref[row * lon + place, 8:16, :]
            if row in inward:
                tile = tile + in_ref[inward[row] * lon + place, 16:24, :]
            tile = tile + jnp.where(lane == 0, edge(row, (place - 1) % lon, 0), 0.0)
            tile = tile + jnp.where(lane == columns - 1, edge(row, (place + 1) % lon, 1), 0.0)
            mixed.append(tile)
        cot = [in_ref[row * lon + place, 0:8, :] for row in range(rows)]
        grid.append(jnp.concatenate(mixed + cot, axis=0))
    pairs = transform_8(grid)
    height = 16 * rows
    for residue in range(lon):
        real, imag = pairs[min(residue, lon - residue)]
        cosine, sine = turn_ref[residue : residue + 1, :], turn_ref[8 + residue : 9 + residue, :]
        if imag is None:
            turned = (real * cosine, -real * sine)
        elif residue < 4:
            turned = (real * cosine + imag * sine, imag * cosine - real * sine)
        else:
            turned = (real * cosine - imag * sine, -imag * cosine - real * sine)
        span = pl.ds(residue * height, height)
        work[span, 0:columns] = turned[0]
        work[span, columns:] = turned[1]
    spectra = jnp.dot(work[...], dft_ref[...], precision=three_pass)
    scale = 1.0 / (lon * columns)
    half = 8 * rows
    gradients = []
    for residue in range(lon):
        place = reversed_bits(residue, 3)
        part = spectra[residue * height : (residue + 1) * height]
        mix_re, mix_im = part[:half, :columns], part[:half, columns:]
        cot_re, cot_im = part[half:, :columns], part[half:, columns:]
        quarters = [in_ref[row * lon + place, 24:28, :] * scale for row in range(rows)]
        gain_re = jnp.concatenate([jnp.concatenate(quarters[0:2], axis=0)] * rows, axis=0)
        gain_im = jnp.concatenate([jnp.concatenate(quarters[2:4], axis=0)] * rows, axis=0)
        top = pl.ds(residue * height, half)
        bottom = pl.ds(residue * height + half, half)
        work[top, 0:columns] = gain_re * mix_re - gain_im * mix_im
        work[top, columns:] = -(gain_re * mix_im + gain_im * mix_re)
        work[bottom, 0:columns] = gain_re * cot_re + gain_im * cot_im
        work[bottom, columns:] = gain_im * cot_re - gain_re * cot_im
        grad_re = (mix_re * cot_re + mix_im * cot_im) * scale
        grad_im = (mix_re * cot_im - mix_im * cot_re) * scale
        gradients.append(
            [
                grad[0:8] + grad[8:16] + (grad[16:24] + grad[24:32])
                for grad in (grad_re, grad_im)
            ]
        )
    back = jnp.dot(work[...], dft_ref[...], precision=three_pass)
    turned = []
    for residue in range(lon):
        part = back[residue * height : (residue + 1) * height]
        real, imag = part[:, :columns], part[:, columns:]
        cosine, sine = turn_ref[residue : residue + 1, :], turn_ref[8 + residue : 9 + residue, :]
        turned.append((real * cosine + imag * sine, real * sine - imag * cosine))
    sums = [turned[r][0] + turned[lon - r][0] for r in (1, 2, 3)]
    gaps = [turned[r][1] - turned[lon - r][1] for r in (1, 2, 3)]
    first, fourth = turned[0][0], turned[4][0]
    even = [
        first + fourth + sums[1],
        first - fourth - gaps[1],
        first + fourth - sums[1],
        first - fourth + gaps[1],
    ]
    swing = [
        sums[0] + sums[2],
        ROOT_HALF * (sums[0] - gaps[0] - sums[2] - gaps[2]),
        gaps[2] - gaps[0],
        ROOT_HALF * (sums[2] - gaps[2] - sums[0] - gaps[0]),
    ]
    series = [even[d] + swing[d] for d in range(4)] + [even[d] - swing[d] for d in range(4)]
    base = 8 * lax.rem(me, 16)
    left_slot = lane == base + sub
    right_slot = lane == base + lax.rem(sub + 4, 8)
    for place in range(lon):
        residue = reversed_bits(place, 3)
        before, after = series[(place - 1) % lon], series[(place + 1) % lon]
        tiles, rims = [], []
        for row in range(rows):
            span = slice(half + 8 * row, half + 8 * row + 8)
            tiles.append(series[place][span])
            rims.append(
                jnp.where(left_slot, before[span, columns - 1 :], 0.0)
                + jnp.where(right_slot, after[span, 0:1], 0.0)
            )
        for row in range(rows):
            owner = row * lon + place
            part, start = row % 2, row // 2
            out_ref[owner, 0:8, :] = series[place][8 * row : 8 * row + 8]
            for step in range(3):
                out_ref[owner, 8 + 4 * step : 12 + 4 * step, :] = tiles[start + step][
                    4 * part : 4 * part + 4
                ]
            out_ref[owner, 20:28, :] = gradients[residue][part]
            lines = [
                jnp.sum(rims[start + step][4 * part : 4 * part + 4], axis=0, keepdims=True)
                for step in range(3)
            ]
            lines.append(jnp.zeros((1, columns), jnp.float32))
            out_ref[owner, 28:32, :] = jnp.concatenate(lines, axis=0)


def adjoint_kernel(
    mine_ref, other_ref, field_ref, cot_ref, taps_ref, out_ref, grad_ref, gain_ref, taps, rows_ref, sem
):
    copy = pltpu.make_async_copy(taps_ref, taps, sem)
    copy.start()
    channels, columns = field_ref.shape
    owners = channels // 8
    place = lax.axis_index("lat")
    part = lax.rem(place, 2)
    index = place - place // 2
    out_ref[...] = field_ref[...] + mine_ref[:, 0:8, :].reshape(channels, columns)
    mine, other = mine_ref[:, 20:28, :], other_ref[:, 20:28, :]
    gain_ref[0] = jnp.where(part == 0, mine, other).reshape(channels, columns)
    gain_ref[1] = jnp.where(part == 0, other, mine).reshape(channels, columns)
    lane, _ = iotas(4, columns)
    lower = lax.rem(lane // 4, 2) == 0
    own_slot = lax.rem(lane // 4, 2) == part
    lefts, rights = [], []
    for first in (0, owners // 2):
        mine = jnp.sum(mine_ref[first : first + owners // 2, 28:32, :], axis=0)
        other = jnp.sum(other_ref[first : first + owners // 2, 28:32, :], axis=0)
        lefts.append(jnp.where(own_slot, mine, other))
        swapped = jnp.where(own_slot, other, mine)
        rights.append(
            jnp.where(lower, pltpu.roll(swapped, columns - 4, 1), pltpu.roll(swapped, 4, 1))
        )
    left = jnp.concatenate(lefts, axis=1)
    right = jnp.concatenate(rights, axis=1)
    rows_ref[0] = jnp.zeros(rows_ref.shape[1:], jnp.float32)
    rows_ref[4] = jnp.zeros(rows_ref.shape[1:], jnp.float32)
    for step in range(3):
        span = slice(8 + 4 * step, 12 + 4 * step)
        mine, other = mine_ref[:, span, :], other_ref[:, span, :]
        tile = jnp.concatenate(
            [jnp.where(part == 0, mine, other), jnp.where(part == 0, other, mine)], axis=1
        )
        rows_ref[1 + step, 8 : 8 + columns, :] = tile.reshape(channels, columns).T
        rows_ref[1 + step, 7:8, :] = left[step : step + 1]
        rows_ref[1 + step, 8 + columns : 9 + columns, :] = right[step : step + 1]
    copy.wait()
    total = jnp.zeros((columns, channels), jnp.float32)
    for tap_row in range(3):
        for tap_col in range(3):
            window = rows_ref[index + 2 - tap_row, 9 - tap_col : 9 - tap_col + columns, :]
            total = total + jnp.dot(window, taps[tap_row, tap_col], precision=three_pass)
    grad_ref[...] = cot_ref[...] + total.T


def transform_tables(columns, lon):
    places = np.arange(columns)
    turn = 2.0 * np.pi * (np.arange(lon)[:, None] * places[None, :]) / (lon * columns)
    angle = 2.0 * np.pi * (places[:, None] * places[None, :] % columns) / columns
    cosine, sine = np.cos(angle), np.sin(angle)
    dft = np.block([[cosine, -sine], [sine, cosine]])
    turns = np.concatenate([np.cos(turn), np.sin(turn)], axis=0)
    return jnp.asarray(turns, jnp.float32), jnp.asarray(dft, jnp.float32)


def on_device(field, cotangent, conv_weight, spectral_filter):
    channels, _, columns = field.shape
    lat, lon = lax.axis_size("lat"), lax.axis_size("lon")
    owners = lat * lon
    swap = [(i, i ^ 1) for i in range(lat)]
    own = field.reshape(channels, columns)
    cot = cotangent.reshape(channels, columns)
    vmem = pl.BlockSpec(memory_space=pltpu.VMEM)
    hbm = pl.BlockSpec(memory_space=pl.ANY)
    params = pltpu.CompilerParams(vmem_limit_bytes=24 * 1024 * 1024)
    message = jax.ShapeDtypeStruct((owners, 32, columns), jnp.float32)
    outgoing = pl.pallas_call(
        conv_kernel,
        out_shape=message,
        in_specs=[vmem, vmem, vmem, vmem, hbm],
        out_specs=vmem,
        scratch_shapes=[
            pltpu.VMEM((2,) + conv_weight.shape[1:], jnp.float32),
            pltpu.SemaphoreType.DMA((2,)),
        ],
        compiler_params=params,
        name="conv",
    )(own, lax.ppermute(own, "lat", swap), cot, spectral_filter, conv_weight)
    owned = lax.all_to_all(outgoing, ("lat", "lon"), 0, 0, tiled=True)
    turns, dft = transform_tables(columns, lon)
    returned = pl.pallas_call(
        spectral_kernel,
        out_shape=message,
        in_specs=[vmem] * 3,
        out_specs=vmem,
        scratch_shapes=[pltpu.VMEM((2 * 8 * lat * lon, 2 * columns), jnp.float32)],
        compiler_params=params,
        name="spectral",
    )(owned, turns, dft)
    mine = lax.all_to_all(returned, ("lat", "lon"), 0, 0, tiled=True)
    other = lax.ppermute(mine, "lat", swap)
    flat = jax.ShapeDtypeStruct((channels, columns), jnp.float32)
    output, input_grad, filter_grad = pl.pallas_call(
        adjoint_kernel,
        out_shape=(flat, flat, jax.ShapeDtypeStruct(spectral_filter.shape, jnp.float32)),
        in_specs=[vmem, vmem, vmem, vmem, hbm],
        out_specs=(vmem, vmem, vmem),
        scratch_shapes=[
            pltpu.VMEM(conv_weight.shape, jnp.float32),
            pltpu.VMEM((5, columns + 16, channels), jnp.float32),
            pltpu.SemaphoreType.DMA,
        ],
        compiler_params=params,
        name="adjoint",
    )(mine, other, own, cot, conv_weight)
    return (output.reshape(field.shape), input_grad.reshape(field.shape), filter_grad)


def solution(mesh):
    placed = (P(None, "lat", "lon"), P(None, "lat", "lon"), P(), P(None, None, "lon"))
    specs = (P(None, "lat", "lon"), P(None, "lat", "lon"), P(None, None, "lon"))

    def layer(field, cotangent, conv_weight, spectral_filter):
        lat, lon = mesh.shape["lat"], mesh.shape["lon"]
        channels, rows, length = field.shape
        owned = rows == lat == 4 and lon == 8 and channels == 8 * lat * lon and length == 128 * lon
        body = on_device if owned else on_device_any_mesh
        mapped = jax.shard_map(body, mesh=mesh, in_specs=placed, out_specs=specs, check_vma=False)
        return mapped(field, cotangent, conv_weight, spectral_filter)

    return layer
```

```python
from functools import partial

import jax
import jax.numpy as jnp
import numpy as np
from jax import lax
from jax.experimental import pallas as pl
from jax.experimental.pallas import tpu as pltpu
from jax.sharding import PartitionSpec as P

precise = lax.Precision.HIGHEST
three_pass = lax.Precision.HIGH
ROOT_HALF = 0.5**0.5


def padded_2(array, sides, width, wrap):
    for axis, dim in sides:
        peers, length = (lax.axis_size(axis), array.shape[dim])
        up = [(i, (i + 1) % peers) for i in range(peers if wrap else peers - 1)]
        down = [(j, i) for i, j in up]
        last = lax.slice_in_dim(array, length - width, length, axis=dim)
        leading = lax.slice_in_dim(array, 0, width, axis=dim)
        before = lax.ppermute(last, axis, up)
        after = lax.ppermute(leading, axis, down)
        array = jnp.concatenate([before, array, after], axis=dim)
    return array


def partner(array, axis, stride):
    return lax.ppermute(array, axis, [(i, i ^ 1 << stride) for i in range(lax.axis_size(axis))])


def angle_table(first, second, modulus):
    product = first[:, None] * second[None, :] % modulus
    return 2.0 * jnp.pi / modulus * product.astype(jnp.float32)


def apply_taps(padded, taps, lat_rows, columns):
    total = jnp.zeros((taps.shape[2], lat_rows, columns), jnp.float32)
    for tap_row in range(3):
        for tap_col in range(3):
            window = padded[:, tap_row : tap_row + lat_rows, tap_col : tap_col + columns]
            total = total + jnp.einsum(
                "oi,iab->oab", taps[tap_row, tap_col], window, precision=precise
            )
    return total


def with_rims(field):
    wider = padded_2(field, (("lon", 2),), 1, True)
    return padded_2(wider, (("lat", 1),), 1, False)


def local_forward(real_part, imag_part):
    columns = real_part.shape[-1]
    places = lax.iota(jnp.int32, columns)
    angles = angle_table(places, places, columns)
    cosine = jnp.cos(angles)
    sine = jnp.sin(angles)
    out_real = jnp.dot(real_part, cosine, precision=precise) + jnp.dot(
        imag_part, sine, precision=precise
    )
    out_imag = jnp.dot(imag_part, cosine, precision=precise) - jnp.dot(
        real_part, sine, precision=precise
    )
    return (out_real, out_imag)


def local_inverse(real_part, imag_part):
    columns = real_part.shape[-1]
    places = lax.iota(jnp.int32, columns)
    angles = angle_table(places, places, columns)
    cosine = jnp.cos(angles)
    sine = jnp.sin(angles)
    out_real = jnp.dot(real_part, cosine, precision=precise) - jnp.dot(
        imag_part, sine, precision=precise
    )
    out_imag = jnp.dot(imag_part, cosine, precision=precise) + jnp.dot(
        real_part, sine, precision=precise
    )
    return (out_real / columns, out_imag / columns)


def section_angles(place, bit_pos, columns):
    offsets = lax.iota(jnp.int32, columns)
    start = place % 2**bit_pos * columns
    span = 2 * columns * 2**bit_pos
    angles = 2.0 * jnp.pi / span * (start + offsets).astype(jnp.float32)
    upper = place // 2**bit_pos % 2 == 1
    return (jnp.cos(angles), jnp.sin(angles), upper)


def forward_pairs(field):
    extent = lax.axis_size("lon")
    width_bits = extent.bit_length() - 1
    place = lax.axis_index("lon")
    columns = field.shape[-1]
    data = jnp.stack([field, jnp.zeros_like(field)])
    for bit_pos in reversed(range(width_bits)):
        other = partner(data, "lon", bit_pos)
        cosine, sine, upper = section_angles(place, bit_pos, columns)
        differ = other - data
        turned = jnp.stack(
            [differ[0] * cosine + differ[1] * sine, differ[1] * cosine - differ[0] * sine]
        )
        data = jnp.where(upper, turned, data + other)
    out_real, out_imag = local_forward(data[0], data[1])
    return jnp.stack([out_real, out_imag])


def inverse_pairs(spectrum):
    extent = lax.axis_size("lon")
    width_bits = extent.bit_length() - 1
    place = lax.axis_index("lon")
    columns = spectrum.shape[-1]
    back_real, back_imag = local_inverse(spectrum[0], spectrum[1])
    data = jnp.stack([back_real, back_imag])
    for bit_pos in range(width_bits):
        cosine, sine, upper = section_angles(place, bit_pos, columns)
        turned = jnp.stack([data[0] * cosine - data[1] * sine, data[1] * cosine + data[0] * sine])
        outgoing = jnp.where(upper, turned, data)
        other = partner(outgoing, "lon", bit_pos)
        data = jnp.where(upper, other - outgoing, outgoing + other) * 0.5
    return data[0]


def on_device_any_mesh(field, cotangent, conv_weight, spectral_filter):
    lat_rows = field.shape[1]
    columns = field.shape[2]
    total_len = columns * lax.axis_size("lon")
    mixed = apply_taps(with_rims(field), conv_weight, lat_rows, columns)
    hidden_spec = forward_pairs(mixed)
    cot_spec = forward_pairs(cotangent)
    gain_real = spectral_filter[0][:, None, :]
    gain_imag = spectral_filter[1][:, None, :]
    filtered = jnp.stack(
        [
            gain_real * hidden_spec[0] - gain_imag * hidden_spec[1],
            gain_real * hidden_spec[1] + gain_imag * hidden_spec[0],
        ]
    )
    adjoint = jnp.stack(
        [
            gain_real * cot_spec[0] + gain_imag * cot_spec[1],
            gain_real * cot_spec[1] - gain_imag * cot_spec[0],
        ]
    )
    shaped = inverse_pairs(filtered)
    back_field = inverse_pairs(adjoint)
    output = field + shaped
    local_grad = (
        jnp.stack(
            [
                jnp.sum(hidden_spec[0] * cot_spec[0] + hidden_spec[1] * cot_spec[1], axis=1),
                jnp.sum(hidden_spec[0] * cot_spec[1] - hidden_spec[1] * cot_spec[0], axis=1),
            ]
        )
        / total_len
    )
    filter_grad = lax.psum(local_grad, "lat")
    flipped_taps = jnp.transpose(conv_weight[::-1, ::-1], (0, 1, 3, 2))
    input_grad = cotangent + apply_taps(with_rims(back_field), flipped_taps, lat_rows, columns)
    return (output, input_grad, filter_grad)


FORTH, BACK = 25, 29


def reversed_bits(value, width):
    return int(format(value, f"0{width}b")[::-1], 2)


def iotas(rows, columns):
    lane = lax.broadcasted_iota(jnp.int32, (rows, columns), 1)
    row = lax.broadcasted_iota(jnp.int32, (rows, columns), 0)
    return lane, row


def fetch_kernel(own_ref, cot_ref, filter_ref, taps_ref, own_out, taps_out, out_ref, cot, gain, sems):
    place = lax.axis_index("lat")
    half = gain.shape[0]
    start = pl.multiple_of(lax.rem(place, 2) * half, half)
    copies = [
        pltpu.make_async_copy(cot_ref, cot, sems.at[0]),
        pltpu.make_async_copy(filter_ref.at[place // 2, pl.ds(start, half)], gain, sems.at[1]),
        pltpu.make_async_copy(own_ref, own_out, sems.at[2]),
        pltpu.make_async_copy(taps_ref, taps_out, sems.at[3]),
    ]
    for copy in copies:
        copy.start()
    copies[0].wait()
    copies[1].wait()
    for owner in range(half // 4):
        first, here = FORTH * owner, slice(4 * owner, 4 * owner + 4)
        out_ref[first : first + 4, :] = cot[here]
        out_ref[first + 4 : first + 8, :] = cot[half + 4 * owner : half + 4 * owner + 4]
        out_ref[first + 20 : first + 24, :] = gain[here]
    copies[2].wait()
    copies[3].wait()


def conv_kernel(own_ref, other_ref, taps_ref, packed_ref, out_ref):
    place = lax.axis_index("lat")
    odd = lax.rem(place, 2)
    channels, columns = own_ref.shape
    half = channels // 2
    side, cross = 2 - 2 * odd, 2 * (place // 2)
    start = pl.multiple_of(odd * half, half)
    own, other = own_ref[...], other_ref[...]
    near = jnp.where(jnp.logical_or(place == 1, place == 2), own, other)
    parts = []
    for tap_col in range(3):
        inner = jnp.dot(taps_ref[1, tap_col], own, precision=three_pass)
        inner = inner + jnp.dot(taps_ref[side, tap_col], other, precision=three_pass)
        outer = jnp.dot(taps_ref[cross, tap_col, pl.ds(start, half)], near, precision=three_pass)
        parts.append(jnp.concatenate([inner, outer], axis=0))
    lane, row = iotas(channels + half, columns)
    left, middle, right = parts
    main = (
        middle
        + jnp.where(lane == 0, 0.0, pltpu.roll(left, 1, 1))
        + jnp.where(lane == columns - 1, 0.0, pltpu.roll(right, columns - 1, 1))
    )
    slot = lane - lax.rem(row, 4) - 4 * (row // half)
    edges = jnp.where(slot == 0, left[:, columns - 1 :], 0.0)
    edges = jnp.where(slot == 12, right[:, 0:1], edges)
    edges = edges[:half] + edges[half:channels] + edges[channels:]
    for owner in range(half // 4):
        first = FORTH * owner
        for part in range(3):
            here = half * part + 4 * owner
            out_ref[first + 8 + 4 * part : first + 12 + 4 * part, :] = main[here : here + 4]
        out_ref[first + 24 : first + 25, :] = jnp.sum(
            edges[4 * owner : 4 * owner + 4], axis=0, keepdims=True
        )


def transform_8(x):
    s = [x[d] + x[d + 4] for d in range(4)]
    t = [x[d] - x[d + 4] for d in range(4)]
    plus, minus = ROOT_HALF * (t[1] + t[3]), ROOT_HALF * (t[1] - t[3])
    return [
        (s[0] + s[2] + (s[1] + s[3]), None),
        (t[0] + minus, -t[2] - plus),
        (s[0] - s[2], s[3] - s[1]),
        (t[0] - minus, t[2] - plus),
        (s[0] + s[2] - (s[1] + s[3]), None),
    ]


def spectral_kernel(in_ref, turn_ref, dft_ref, out_ref, work):
    rows, lon = 4, 8
    columns = in_ref.shape[-1]
    lane, sub = iotas(8, columns)
    me = lax.axis_index("lat") * lon + lax.axis_index("lon")
    inward = {1: (2, 3), 2: (0, 1)}

    def message(row, place, first, count):
        start = FORTH * (row * lon + place) + first
        return in_ref[start : start + count, :]

    def edge(row, place, group):
        line = jnp.where(lane == sub + 12 * group, message(row, place, 24, 1), 0.0)
        for part, giver in enumerate(inward.get(row, ())):
            wanted = jnp.logical_and(lane == lax.rem(sub, 4) + 8 + 12 * group, sub // 4 == part)
            line = line + jnp.where(wanted, message(giver, place, 24, 1), 0.0)
        return jnp.sum(line, axis=1, keepdims=True)

    grid = []
    for place in range(lon):
        mixed = []
        for row in range(rows):
            tile = message(row, place, 8, 8)
            if row in inward:
                pieces = [message(giver, place, 16, 4) for giver in inward[row]]
                tile = tile + jnp.concatenate(pieces, axis=0)
            tile = tile + jnp.where(lane == 0, edge(row, (place - 1) % lon, 0), 0.0)
            tile = tile + jnp.where(lane == columns - 1, edge(row, (place + 1) % lon, 1), 0.0)
            mixed.append(tile)
        cot = [message(row, place, 0, 8) for row in range(rows)]
        grid.append(jnp.concatenate(mixed + cot, axis=0))
    pairs = transform_8(grid)
    height = 16 * rows
    for residue in range(lon):
        real, imag = pairs[min(residue, lon - residue)]
        cosine, sine = turn_ref[residue : residue + 1, :], turn_ref[8 + residue : 9 + residue, :]
        if imag is None:
            turned = (real * cosine, -real * sine)
        elif residue < 4:
            turned = (real * cosine + imag * sine, imag * cosine - real * sine)
        else:
            turned = (real * cosine - imag * sine, -imag * cosine - real * sine)
        span = pl.ds(residue * height, height)
        work[span, 0:columns] = turned[0]
        work[span, columns:] = turned[1]
    spectra = jnp.dot(work[...], dft_ref[...], precision=three_pass)
    scale = 1.0 / (lon * columns)
    half = 8 * rows
    gradients = []
    for residue in range(lon):
        place = reversed_bits(residue, 3)
        part = spectra[residue * height : (residue + 1) * height]
        mix_re, mix_im = part[:half, :columns], part[:half, columns:]
        cot_re, cot_im = part[half:, :columns], part[half:, columns:]
        quarters = [message(row, place, 20, 4) * scale for row in range(rows)]
        gain_re = jnp.concatenate([jnp.concatenate(quarters[0:2], axis=0)] * rows, axis=0)
        gain_im = jnp.concatenate([jnp.concatenate(quarters[2:4], axis=0)] * rows, axis=0)
        top = pl.ds(residue * height, half)
        bottom = pl.ds(residue * height + half, half)
        work[top, 0:columns] = gain_re * mix_re - gain_im * mix_im
        work[top, columns:] = -(gain_re * mix_im + gain_im * mix_re)
        work[bottom, 0:columns] = gain_re * cot_re + gain_im * cot_im
        work[bottom, columns:] = gain_im * cot_re - gain_re * cot_im
        grad_re = (mix_re * cot_re + mix_im * cot_im) * scale
        grad_im = (mix_re * cot_im - mix_im * cot_re) * scale
        gradients.append(
            [
                grad[0:8] + grad[8:16] + (grad[16:24] + grad[24:32])
                for grad in (grad_re, grad_im)
            ]
        )
    back = jnp.dot(work[...], dft_ref[...], precision=three_pass)
    turned = []
    for residue in range(lon):
        part = back[residue * height : (residue + 1) * height]
        real, imag = part[:, :columns], part[:, columns:]
        cosine, sine = turn_ref[residue : residue + 1, :], turn_ref[8 + residue : 9 + residue, :]
        turned.append((real * cosine + imag * sine, real * sine - imag * cosine))
    sums = [turned[r][0] + turned[lon - r][0] for r in (1, 2, 3)]
    gaps = [turned[r][1] - turned[lon - r][1] for r in (1, 2, 3)]
    first, fourth = turned[0][0], turned[4][0]
    even = [
        first + fourth + sums[1],
        first - fourth - gaps[1],
        first + fourth - sums[1],
        first - fourth + gaps[1],
    ]
    swing = [
        sums[0] + sums[2],
        ROOT_HALF * (sums[0] - gaps[0] - sums[2] - gaps[2]),
        gaps[2] - gaps[0],
        ROOT_HALF * (sums[2] - gaps[2] - sums[0] - gaps[0]),
    ]
    series = [even[d] + swing[d] for d in range(4)] + [even[d] - swing[d] for d in range(4)]
    slots = [lane == 4 * lax.rem(me + group, 32) + lax.rem(sub, 4) for group in range(6)]
    for place in range(lon):
        residue = reversed_bits(place, 3)
        before, after = series[(place - 1) % lon], series[(place + 1) % lon]
        for chip in range(2):
            rims = jnp.zeros((8, columns), jnp.float32)
            for step in range(3):
                span = slice(half + 8 * (chip + step), half + 8 * (chip + step) + 8)
                rims = jnp.where(slots[2 * step], before[span, columns - 1 :], rims)
                rims = jnp.where(slots[2 * step + 1], after[span, 0:1], rims)
            for part in range(2):
                row = 2 * chip + part
                start = BACK * (row * lon + place)
                out_ref[start : start + 8, :] = series[place][8 * row : 8 * row + 8]
                for step in range(3):
                    here = half + 8 * (chip + step) + 4 * part
                    out_ref[start + 8 + 4 * step : start + 12 + 4 * step, :] = series[place][
                        here : here + 4
                    ]
                out_ref[start + 20 : start + 28, :] = gradients[residue][part]
                out_ref[start + 28 : start + 29, :] = jnp.sum(
                    rims[4 * part : 4 * part + 4], axis=0, keepdims=True
                )


def partial_adjoint(message_ref, taps_ref, rows_ref, part):
    half, columns = rows_ref.shape[-1], message_ref.shape[-1]
    place = lax.axis_index("lat")
    index = place - place // 2
    owners = half // 4
    lines = message_ref[pl.ds(28, owners, stride=BACK), :]
    lane, owner = iotas(owners, columns)
    rows_ref[0] = jnp.zeros(rows_ref.shape[1:], jnp.float32)
    rows_ref[4] = jnp.zeros(rows_ref.shape[1:], jnp.float32)
    for step in range(3):
        pieces = [
            message_ref[BACK * j + 8 + 4 * step : BACK * j + 12 + 4 * step, :] for j in range(owners)
        ]
        rows_ref[1 + step, 8 : 8 + columns, :] = jnp.concatenate(pieces, axis=0).T
        for rim, target in ((2 * step, 7), (2 * step + 1, 8 + columns)):
            wanted = lane // 4 == lax.rem(owner + rim, owners)
            line = jnp.sum(jnp.where(wanted, lines, 0.0), axis=0, keepdims=True)
            line = jnp.broadcast_to(line, (8, columns))
            if rim:
                line = pltpu.roll(line, columns - 4 * rim, 1)
            rows_ref[1 + step, target : target + 1, :] = line[0:1]
    span = pl.ds(pl.multiple_of(part * half, half), half)
    windows, weights = [], []
    for tap_row in range(3):
        for tap_col in range(3):
            first = 9 - tap_col
            windows.append(rows_ref[index + 2 - tap_row, first : first + columns, :])
            weights.append(taps_ref[tap_row, tap_col, span])
    total = jnp.dot(windows[8], weights[8], precision=three_pass)
    for pair in range(0, 8, 2):
        total = total + jnp.dot(
            jnp.concatenate(windows[pair : pair + 2], axis=1),
            jnp.concatenate(weights[pair : pair + 2], axis=0),
            precision=three_pass,
        )
    return total


def adjoint_kernel(mine_ref, field_ref, taps_ref, out_ref, total_ref, rows_ref):
    half = field_ref.shape[0] // 2
    for owner in range(half // 4):
        for part in range(2):
            here, there = half * part + 4 * owner, BACK * owner + 4 * part
            out_ref[here : here + 4, :] = field_ref[here : here + 4, :] + mine_ref[there : there + 4, :]
    part = lax.rem(lax.axis_index("lat"), 2)
    total_ref[...] = partial_adjoint(mine_ref, taps_ref, rows_ref, part)


def last_kernel(
    mine_ref, other_ref, cot_ref, taps_ref, total_ref, grad_ref, gain_ref, rows_ref, gain, sems
):
    half = cot_ref.shape[0] // 2
    part = lax.rem(lax.axis_index("lat"), 2)
    for owner in range(half // 4):
        for piece in range(2):
            here, there = half * piece + 4 * owner, BACK * owner + 20 + 4 * piece
            gain[0, here : here + 4, :] = mine_ref[there : there + 4, :]
            gain[1, here : here + 4, :] = other_ref[there : there + 4, :]
    copies = [
        pltpu.make_async_copy(gain.at[0], gain_ref.at[part], sems.at[0]),
        pltpu.make_async_copy(gain.at[1], gain_ref.at[1 - part], sems.at[1]),
    ]
    for copy in copies:
        copy.start()
    total = total_ref[...] + partial_adjoint(other_ref, taps_ref, rows_ref, 1 - part)
    grad_ref[...] = cot_ref[...] + total.T
    for copy in copies:
        copy.wait()


def transform_tables(columns, lon):
    places = np.arange(columns)
    turn = 2.0 * np.pi * (np.arange(lon)[:, None] * places[None, :]) / (lon * columns)
    angle = 2.0 * np.pi * (places[:, None] * places[None, :] % columns) / columns
    cosine, sine = np.cos(angle), np.sin(angle)
    dft = np.block([[cosine, -sine], [sine, cosine]])
    turns = np.concatenate([np.cos(turn), np.sin(turn)], axis=0)
    return jnp.asarray(turns, jnp.float32), jnp.asarray(dft, jnp.float32)


def exchanged(flat):
    rows, columns = flat.shape
    moved = lax.all_to_all(flat.reshape(rows, 1, columns), ("lat", "lon"), 0, 0, tiled=True)
    return moved.reshape(rows, columns)


def on_device(field, cotangent, conv_weight, spectral_filter):
    channels, _, columns = field.shape
    lat, lon = lax.axis_size("lat"), lax.axis_size("lon")
    owners = lat * lon
    swap = [(i, i ^ 1) for i in range(lat)]
    own = field.reshape(channels, columns)
    cot = cotangent.reshape(channels, columns)
    vmem = pl.BlockSpec(memory_space=pltpu.VMEM)
    hbm = pl.BlockSpec(memory_space=pltpu.HBM)
    params = pltpu.CompilerParams(vmem_limit_bytes=16 * 1024 * 1024)
    flat = jax.ShapeDtypeStruct((channels, columns), jnp.float32)
    taps_shape = jax.ShapeDtypeStruct(conv_weight.shape, jnp.float32)
    forth = jax.ShapeDtypeStruct((owners * FORTH, columns), jnp.float32)
    back = jax.ShapeDtypeStruct((owners * BACK, columns), jnp.float32)
    other = lax.ppermute(own, "lat", swap)
    own_here, taps, packed = pl.pallas_call(
        fetch_kernel,
        out_shape=(flat, taps_shape, forth),
        in_specs=[hbm] * 4,
        out_specs=(vmem, vmem, vmem),
        scratch_shapes=[
            pltpu.VMEM((channels, columns), jnp.float32),
            pltpu.VMEM((channels // 2, columns), jnp.float32),
            pltpu.SemaphoreType.DMA((4,)),
        ],
        compiler_params=params,
        name="fetch",
    )(*[pltpu.with_memory_space_constraint(x, pltpu.HBM) for x in (own, cot, spectral_filter, conv_weight)])
    outgoing = pl.pallas_call(
        conv_kernel,
        out_shape=forth,
        in_specs=[vmem] * 4,
        out_specs=vmem,
        input_output_aliases={3: 0},
        compiler_params=params,
        name="conv",
    )(own_here, other, taps, packed)
    turns, dft = transform_tables(columns, lon)
    returned = pl.pallas_call(
        spectral_kernel,
        out_shape=back,
        in_specs=[vmem] * 3,
        out_specs=vmem,
        scratch_shapes=[pltpu.VMEM((2 * 8 * lat * lon, 2 * columns), jnp.float32)],
        compiler_params=params,
        name="spectral",
    )(exchanged(outgoing), turns, dft)
    mine = exchanged(returned)
    other = lax.ppermute(mine, "lat", swap)
    rows_scratch = pltpu.VMEM((5, columns + 16, channels // 2), jnp.float32)
    output, total = pl.pallas_call(
        adjoint_kernel,
        out_shape=(flat, jax.ShapeDtypeStruct((columns, channels), jnp.float32)),
        in_specs=[vmem] * 3,
        out_specs=(vmem, vmem),
        scratch_shapes=[rows_scratch],
        compiler_params=params,
        name="adjoint",
    )(mine, own, taps)
    input_grad, filter_grad = pl.pallas_call(
        last_kernel,
        out_shape=(flat, jax.ShapeDtypeStruct(spectral_filter.shape, jnp.float32)),
        in_specs=[vmem] * 5,
        out_specs=(vmem, hbm),
        scratch_shapes=[
            rows_scratch,
            pltpu.VMEM(spectral_filter.shape, jnp.float32),
            pltpu.SemaphoreType.DMA((2,)),
        ],
        compiler_params=params,
        name="last",
    )(mine, other, cot, taps, total)
    return (output.reshape(field.shape), input_grad.reshape(field.shape), filter_grad)


def solution(mesh):
    placed = (P(None, "lat", "lon"), P(None, "lat", "lon"), P(), P(None, None, "lon"))
    specs = (P(None, "lat", "lon"), P(None, "lat", "lon"), P(None, None, "lon"))

    def layer(field, cotangent, conv_weight, spectral_filter):
        lat, lon = mesh.shape["lat"], mesh.shape["lon"]
        channels, rows, length = field.shape
        owned = rows == lat == 4 and lon == 8 and channels == 8 * lat * lon and length == 128 * lon
        body = on_device if owned else on_device_any_mesh
        mapped = jax.shard_map(body, mesh=mesh, in_specs=placed, out_specs=specs, check_vma=False)
        return mapped(field, cotangent, conv_weight, spectral_filter)

    return layer
```

```python
from functools import partial

import jax
import jax.numpy as jnp
import numpy as np
from jax import lax
from jax.experimental import pallas as pl
from jax.experimental.pallas import tpu as pltpu
from jax.sharding import PartitionSpec as P

precise = lax.Precision.HIGHEST
three_pass = lax.Precision.HIGH
ROOT_HALF = 0.5**0.5


def padded_2(array, sides, width, wrap):
    for axis, dim in sides:
        peers, length = (lax.axis_size(axis), array.shape[dim])
        up = [(i, (i + 1) % peers) for i in range(peers if wrap else peers - 1)]
        down = [(j, i) for i, j in up]
        last = lax.slice_in_dim(array, length - width, length, axis=dim)
        leading = lax.slice_in_dim(array, 0, width, axis=dim)
        before = lax.ppermute(last, axis, up)
        after = lax.ppermute(leading, axis, down)
        array = jnp.concatenate([before, array, after], axis=dim)
    return array


def partner(array, axis, stride):
    return lax.ppermute(array, axis, [(i, i ^ 1 << stride) for i in range(lax.axis_size(axis))])


def angle_table(first, second, modulus):
    product = first[:, None] * second[None, :] % modulus
    return 2.0 * jnp.pi / modulus * product.astype(jnp.float32)


def apply_taps(padded, taps, lat_rows, columns):
    total = jnp.zeros((taps.shape[2], lat_rows, columns), jnp.float32)
    for tap_row in range(3):
        for tap_col in range(3):
            window = padded[:, tap_row : tap_row + lat_rows, tap_col : tap_col + columns]
            total = total + jnp.einsum(
                "oi,iab->oab", taps[tap_row, tap_col], window, precision=precise
            )
    return total


def with_rims(field):
    wider = padded_2(field, (("lon", 2),), 1, True)
    return padded_2(wider, (("lat", 1),), 1, False)


def local_forward(real_part, imag_part):
    columns = real_part.shape[-1]
    places = lax.iota(jnp.int32, columns)
    angles = angle_table(places, places, columns)
    cosine = jnp.cos(angles)
    sine = jnp.sin(angles)
    out_real = jnp.dot(real_part, cosine, precision=precise) + jnp.dot(
        imag_part, sine, precision=precise
    )
    out_imag = jnp.dot(imag_part, cosine, precision=precise) - jnp.dot(
        real_part, sine, precision=precise
    )
    return (out_real, out_imag)


def local_inverse(real_part, imag_part):
    columns = real_part.shape[-1]
    places = lax.iota(jnp.int32, columns)
    angles = angle_table(places, places, columns)
    cosine = jnp.cos(angles)
    sine = jnp.sin(angles)
    out_real = jnp.dot(real_part, cosine, precision=precise) - jnp.dot(
        imag_part, sine, precision=precise
    )
    out_imag = jnp.dot(imag_part, cosine, precision=precise) + jnp.dot(
        real_part, sine, precision=precise
    )
    return (out_real / columns, out_imag / columns)


def section_angles(place, bit_pos, columns):
    offsets = lax.iota(jnp.int32, columns)
    start = place % 2**bit_pos * columns
    span = 2 * columns * 2**bit_pos
    angles = 2.0 * jnp.pi / span * (start + offsets).astype(jnp.float32)
    upper = place // 2**bit_pos % 2 == 1
    return (jnp.cos(angles), jnp.sin(angles), upper)


def forward_pairs(field):
    extent = lax.axis_size("lon")
    width_bits = extent.bit_length() - 1
    place = lax.axis_index("lon")
    columns = field.shape[-1]
    data = jnp.stack([field, jnp.zeros_like(field)])
    for bit_pos in reversed(range(width_bits)):
        other = partner(data, "lon", bit_pos)
        cosine, sine, upper = section_angles(place, bit_pos, columns)
        differ = other - data
        turned = jnp.stack(
            [differ[0] * cosine + differ[1] * sine, differ[1] * cosine - differ[0] * sine]
        )
        data = jnp.where(upper, turned, data + other)
    out_real, out_imag = local_forward(data[0], data[1])
    return jnp.stack([out_real, out_imag])


def inverse_pairs(spectrum):
    extent = lax.axis_size("lon")
    width_bits = extent.bit_length() - 1
    place = lax.axis_index("lon")
    columns = spectrum.shape[-1]
    back_real, back_imag = local_inverse(spectrum[0], spectrum[1])
    data = jnp.stack([back_real, back_imag])
    for bit_pos in range(width_bits):
        cosine, sine, upper = section_angles(place, bit_pos, columns)
        turned = jnp.stack([data[0] * cosine - data[1] * sine, data[1] * cosine + data[0] * sine])
        outgoing = jnp.where(upper, turned, data)
        other = partner(outgoing, "lon", bit_pos)
        data = jnp.where(upper, other - outgoing, outgoing + other) * 0.5
    return data[0]


def on_device_any_mesh(field, cotangent, conv_weight, spectral_filter):
    lat_rows = field.shape[1]
    columns = field.shape[2]
    total_len = columns * lax.axis_size("lon")
    mixed = apply_taps(with_rims(field), conv_weight, lat_rows, columns)
    hidden_spec = forward_pairs(mixed)
    cot_spec = forward_pairs(cotangent)
    gain_real = spectral_filter[0][:, None, :]
    gain_imag = spectral_filter[1][:, None, :]
    filtered = jnp.stack(
        [
            gain_real * hidden_spec[0] - gain_imag * hidden_spec[1],
            gain_real * hidden_spec[1] + gain_imag * hidden_spec[0],
        ]
    )
    adjoint = jnp.stack(
        [
            gain_real * cot_spec[0] + gain_imag * cot_spec[1],
            gain_real * cot_spec[1] - gain_imag * cot_spec[0],
        ]
    )
    shaped = inverse_pairs(filtered)
    back_field = inverse_pairs(adjoint)
    output = field + shaped
    local_grad = (
        jnp.stack(
            [
                jnp.sum(hidden_spec[0] * cot_spec[0] + hidden_spec[1] * cot_spec[1], axis=1),
                jnp.sum(hidden_spec[0] * cot_spec[1] - hidden_spec[1] * cot_spec[0], axis=1),
            ]
        )
        / total_len
    )
    filter_grad = lax.psum(local_grad, "lat")
    flipped_taps = jnp.transpose(conv_weight[::-1, ::-1], (0, 1, 3, 2))
    input_grad = cotangent + apply_taps(with_rims(back_field), flipped_taps, lat_rows, columns)
    return (output, input_grad, filter_grad)


FORTH, BACK = 25, 29


def reversed_bits(value, width):
    return int(format(value, f"0{width}b")[::-1], 2)


def iotas(rows, columns):
    lane = lax.broadcasted_iota(jnp.int32, (rows, columns), 1)
    row = lax.broadcasted_iota(jnp.int32, (rows, columns), 0)
    return lane, row


def fetch_kernel(
    own_ref, cot_ref, filter_ref, taps_ref, own_out, middle, side, cross, out_ref, cot, gain, sems
):
    place = lax.axis_index("lat")
    odd, half = lax.rem(place, 2), gain.shape[0]
    span = pl.ds(pl.multiple_of(odd * half, half), half)
    cross_row = 2 * (place // 2)
    copies = [
        pltpu.make_async_copy(cot_ref, cot, sems.at[0]),
        pltpu.make_async_copy(filter_ref.at[place // 2, span], gain, sems.at[1]),
        pltpu.make_async_copy(own_ref, own_out, sems.at[2]),
        pltpu.make_async_copy(taps_ref.at[1], middle, sems.at[3]),
        pltpu.make_async_copy(taps_ref.at[2 - 2 * odd], side, sems.at[4]),
    ]
    for tap_col in range(3):
        piece = taps_ref.at[cross_row, tap_col, span]
        copies.append(pltpu.make_async_copy(piece, cross.at[tap_col], sems.at[5 + tap_col]))
    for copy in copies:
        copy.start()
    copies[0].wait()
    copies[1].wait()
    for owner in range(half // 4):
        first, here = FORTH * owner, slice(4 * owner, 4 * owner + 4)
        out_ref[first : first + 4, :] = cot[here]
        out_ref[first + 4 : first + 8, :] = cot[half + 4 * owner : half + 4 * owner + 4]
        out_ref[first + 20 : first + 24, :] = gain[here]
    for copy in copies[2:]:
        copy.wait()


def high_low(x):
    high = x.astype(jnp.bfloat16)
    return high, (x - high.astype(jnp.float32)).astype(jnp.bfloat16)


def both_parts(x):
    return jnp.concatenate(high_low(x), axis=1)


def product(weights, parts):
    columns = parts.shape[1] // 2
    high, low = high_low(weights)
    wide = jnp.dot(high, parts, preferred_element_type=jnp.float32)
    rest = jnp.dot(low, parts[:, :columns], preferred_element_type=jnp.float32)
    return wide[:, :columns] + (wide[:, columns:] + rest)


def tall_product(x, high, low):
    rows = x.shape[0]
    x_high, x_low = high_low(x)
    both = jnp.concatenate([x_high, x_low], axis=0)
    both = jnp.dot(both, high, preferred_element_type=jnp.float32)
    rest = jnp.dot(x_high, low, preferred_element_type=jnp.float32)
    return both[:rows] + (both[rows:] + rest)


def conv_kernel(own_ref, other_ref, middle_ref, side_ref, cross_ref, packed_ref, out_ref):
    place = lax.axis_index("lat")
    channels, columns = own_ref.shape
    half = channels // 2
    own, other = own_ref[...], other_ref[...]
    near = jnp.where(jnp.logical_or(place == 1, place == 2), own, other)
    own, other, near = both_parts(own), both_parts(other), both_parts(near)
    parts = []
    for tap_col in range(3):
        inner = product(middle_ref[tap_col], own) + product(side_ref[tap_col], other)
        outer = product(cross_ref[tap_col], near)
        parts.append(jnp.concatenate([inner, outer], axis=0))
    lane, row = iotas(channels + half, columns)
    left, middle, right = parts
    main = (
        middle
        + jnp.where(lane == 0, 0.0, pltpu.roll(left, 1, 1))
        + jnp.where(lane == columns - 1, 0.0, pltpu.roll(right, columns - 1, 1))
    )
    slot = lane - lax.rem(row, 4) - 4 * (row // half)
    edges = jnp.where(slot == 0, left[:, columns - 1 :], 0.0)
    edges = jnp.where(slot == 12, right[:, 0:1], edges)
    edges = edges[:half] + edges[half:channels] + edges[channels:]
    for owner in range(half // 4):
        first = FORTH * owner
        for part in range(3):
            here = half * part + 4 * owner
            out_ref[first + 8 + 4 * part : first + 12 + 4 * part, :] = main[here : here + 4]
        out_ref[first + 24 : first + 25, :] = jnp.sum(
            edges[4 * owner : 4 * owner + 4], axis=0, keepdims=True
        )


def transform_8(x):
    s = [x[d] + x[d + 4] for d in range(4)]
    t = [x[d] - x[d + 4] for d in range(4)]
    plus, minus = ROOT_HALF * (t[1] + t[3]), ROOT_HALF * (t[1] - t[3])
    return [
        (s[0] + s[2] + (s[1] + s[3]), None),
        (t[0] + minus, -t[2] - plus),
        (s[0] - s[2], s[3] - s[1]),
        (t[0] - minus, t[2] - plus),
        (s[0] + s[2] - (s[1] + s[3]), None),
    ]


def spectral_kernel(in_ref, turn_ref, dft_ref, out_ref, work):
    rows, lon = 4, 8
    columns = in_ref.shape[-1]
    lane, sub = iotas(8, columns)
    me = lax.axis_index("lat") * lon + lax.axis_index("lon")
    inward = {1: (2, 3), 2: (0, 1)}

    def message(row, place, first, count):
        start = FORTH * (row * lon + place) + first
        return in_ref[start : start + count, :]

    def edge(row, place, group):
        line = jnp.where(lane == sub + 12 * group, message(row, place, 24, 1), 0.0)
        for part, giver in enumerate(inward.get(row, ())):
            wanted = jnp.logical_and(lane == lax.rem(sub, 4) + 8 + 12 * group, sub // 4 == part)
            line = line + jnp.where(wanted, message(giver, place, 24, 1), 0.0)
        return jnp.sum(line, axis=1, keepdims=True)

    grid = []
    for place in range(lon):
        mixed = []
        for row in range(rows):
            tile = message(row, place, 8, 8)
            if row in inward:
                pieces = [message(giver, place, 16, 4) for giver in inward[row]]
                tile = tile + jnp.concatenate(pieces, axis=0)
            tile = tile + jnp.where(lane == 0, edge(row, (place - 1) % lon, 0), 0.0)
            tile = tile + jnp.where(lane == columns - 1, edge(row, (place + 1) % lon, 1), 0.0)
            mixed.append(tile)
        cot = [message(row, place, 0, 8) for row in range(rows)]
        grid.append(jnp.concatenate(mixed + cot, axis=0))
    pairs = transform_8(grid)
    height = 16 * rows
    for residue in range(lon):
        real, imag = pairs[min(residue, lon - residue)]
        cosine, sine = turn_ref[residue : residue + 1, :], turn_ref[8 + residue : 9 + residue, :]
        if imag is None:
            turned = (real * cosine, -real * sine)
        elif residue < 4:
            turned = (real * cosine + imag * sine, imag * cosine - real * sine)
        else:
            turned = (real * cosine - imag * sine, -imag * cosine - real * sine)
        span = pl.ds(residue * height, height)
        work[span, 0:columns] = turned[0]
        work[span, columns:] = turned[1]
    chunk = lon * height // 4
    pieces = [pl.ds(first, chunk) for first in range(0, lon * height, chunk)]
    table = high_low(dft_ref[...])
    spectra = jnp.concatenate(
        [tall_product(work[piece], *table) for piece in pieces], axis=0
    )
    scale = 1.0 / (lon * columns)
    half = 8 * rows
    gradients = []
    for residue in range(lon):
        place = reversed_bits(residue, 3)
        part = spectra[residue * height : (residue + 1) * height]
        mix_re, mix_im = part[:half, :columns], part[:half, columns:]
        cot_re, cot_im = part[half:, :columns], part[half:, columns:]
        quarters = [message(row, place, 20, 4) * scale for row in range(rows)]
        gain_re = jnp.concatenate([jnp.concatenate(quarters[0:2], axis=0)] * rows, axis=0)
        gain_im = jnp.concatenate([jnp.concatenate(quarters[2:4], axis=0)] * rows, axis=0)
        top = pl.ds(residue * height, half)
        bottom = pl.ds(residue * height + half, half)
        work[top, 0:columns] = gain_re * mix_re - gain_im * mix_im
        work[top, columns:] = -(gain_re * mix_im + gain_im * mix_re)
        work[bottom, 0:columns] = gain_re * cot_re + gain_im * cot_im
        work[bottom, columns:] = gain_im * cot_re - gain_re * cot_im
        grad_re = (mix_re * cot_re + mix_im * cot_im) * scale
        grad_im = (mix_re * cot_im - mix_im * cot_re) * scale
        gradients.append(
            [
                grad[0:8] + grad[8:16] + (grad[16:24] + grad[24:32])
                for grad in (grad_re, grad_im)
            ]
        )
    back = jnp.concatenate(
        [tall_product(work[piece], *table) for piece in pieces], axis=0
    )
    turned = []
    for residue in range(lon):
        part = back[residue * height : (residue + 1) * height]
        real, imag = part[:, :columns], part[:, columns:]
        cosine, sine = turn_ref[residue : residue + 1, :], turn_ref[8 + residue : 9 + residue, :]
        turned.append((real * cosine + imag * sine, real * sine - imag * cosine))
    sums = [turned[r][0] + turned[lon - r][0] for r in (1, 2, 3)]
    gaps = [turned[r][1] - turned[lon - r][1] for r in (1, 2, 3)]
    first, fourth = turned[0][0], turned[4][0]
    even = [
        first + fourth + sums[1],
        first - fourth - gaps[1],
        first + fourth - sums[1],
        first - fourth + gaps[1],
    ]
    swing = [
        sums[0] + sums[2],
        ROOT_HALF * (sums[0] - gaps[0] - sums[2] - gaps[2]),
        gaps[2] - gaps[0],
        ROOT_HALF * (sums[2] - gaps[2] - sums[0] - gaps[0]),
    ]
    series = [even[d] + swing[d] for d in range(4)] + [even[d] - swing[d] for d in range(4)]
    slots = [lane == 4 * lax.rem(me + group, 32) + lax.rem(sub, 4) for group in range(6)]
    for place in range(lon):
        residue = reversed_bits(place, 3)
        before, after = series[(place - 1) % lon], series[(place + 1) % lon]
        for chip in range(2):
            rims = jnp.zeros((8, columns), jnp.float32)
            for step in range(3):
                span = slice(half + 8 * (chip + step), half + 8 * (chip + step) + 8)
                rims = jnp.where(slots[2 * step], before[span, columns - 1 :], rims)
                rims = jnp.where(slots[2 * step + 1], after[span, 0:1], rims)
            for part in range(2):
                row = 2 * chip + part
                start = BACK * (row * lon + place)
                out_ref[start : start + 8, :] = series[place][8 * row : 8 * row + 8]
                for step in range(3):
                    here = half + 8 * (chip + step) + 4 * part
                    out_ref[start + 8 + 4 * step : start + 12 + 4 * step, :] = series[place][
                        here : here + 4
                    ]
                out_ref[start + 20 : start + 28, :] = gradients[residue][part]
                out_ref[start + 28 : start + 29, :] = jnp.sum(
                    rims[4 * part : 4 * part + 4], axis=0, keepdims=True
                )


def partial_adjoint(message_ref, taps_ref, rows_ref, part):
    half, columns = rows_ref.shape[-1], message_ref.shape[-1]
    place = lax.axis_index("lat")
    index = place - place // 2
    owners = half // 4
    lines = message_ref[pl.ds(28, owners, stride=BACK), :]
    lane, owner = iotas(owners, columns)
    rows_ref[0] = jnp.zeros(rows_ref.shape[1:], jnp.float32)
    rows_ref[4] = jnp.zeros(rows_ref.shape[1:], jnp.float32)
    for step in range(3):
        pieces = [
            message_ref[BACK * j + 8 + 4 * step : BACK * j + 12 + 4 * step, :] for j in range(owners)
        ]
        rows_ref[1 + step, 8 : 8 + columns, :] = jnp.concatenate(pieces, axis=0).T
        for rim, target in ((2 * step, 7), (2 * step + 1, 8 + columns)):
            wanted = lane // 4 == lax.rem(owner + rim, owners)
            line = jnp.sum(jnp.where(wanted, lines, 0.0), axis=0, keepdims=True)
            line = jnp.broadcast_to(line, (8, columns))
            if rim:
                line = pltpu.roll(line, columns - 4 * rim, 1)
            rows_ref[1 + step, target : target + 1, :] = line[0:1]
    span = pl.ds(pl.multiple_of(part * half, half), half)
    windows, weights = [], []
    for tap_row in range(3):
        for tap_col in range(3):
            first = 9 - tap_col
            windows.append(rows_ref[index + 2 - tap_row, first : first + columns, :])
            weights.append(taps_ref[tap_row, tap_col, span])
    total = 0.0
    for pair in range(0, 9, 2):
        window = jnp.concatenate(windows[pair : pair + 2], axis=1)
        weight = jnp.concatenate(weights[pair : pair + 2], axis=0)
        total = total + tall_product(window, *high_low(weight))
    return total


def adjoint_kernel(mine_ref, field_ref, taps_ref, out_ref, total_ref, rows_ref):
    half = field_ref.shape[0] // 2
    for owner in range(half // 4):
        for part in range(2):
            here, there = half * part + 4 * owner, BACK * owner + 4 * part
            out_ref[here : here + 4, :] = field_ref[here : here + 4, :] + mine_ref[there : there + 4, :]
    part = lax.rem(lax.axis_index("lat"), 2)
    total_ref[...] = partial_adjoint(mine_ref, taps_ref, rows_ref, part)


def last_kernel(mine_ref, other_ref, cot_ref, taps_ref, total_ref, grad_ref, gain_ref, rows_ref):
    half = cot_ref.shape[0] // 2
    part = lax.rem(lax.axis_index("lat"), 2)
    for owner in range(half // 4):
        for piece in range(2):
            here, there = half * piece + 4 * owner, BACK * owner + 20 + 4 * piece
            gain_ref[part, here : here + 4, :] = mine_ref[there : there + 4, :]
            gain_ref[1 - part, here : here + 4, :] = other_ref[there : there + 4, :]
    total = total_ref[...] + partial_adjoint(other_ref, taps_ref, rows_ref, 1 - part)
    grad_ref[...] = cot_ref[...] + total.T


def transform_tables(columns, lon):
    places = np.arange(columns)
    turn = 2.0 * np.pi * (np.arange(lon)[:, None] * places[None, :]) / (lon * columns)
    angle = 2.0 * np.pi * (places[:, None] * places[None, :] % columns) / columns
    cosine, sine = np.cos(angle), np.sin(angle)
    dft = np.block([[cosine, -sine], [sine, cosine]])
    turns = np.concatenate([np.cos(turn), np.sin(turn)], axis=0)
    return jnp.asarray(turns, jnp.float32), jnp.asarray(dft, jnp.float32)


def exchanged(flat):
    rows, columns = flat.shape
    moved = lax.all_to_all(flat.reshape(rows, 1, columns), ("lat", "lon"), 0, 0, tiled=True)
    return moved.reshape(rows, columns)


def on_device(field, cotangent, conv_weight, spectral_filter):
    channels, _, columns = field.shape
    lat, lon = lax.axis_size("lat"), lax.axis_size("lon")
    owners = lat * lon
    swap = [(i, i ^ 1) for i in range(lat)]
    own = field.reshape(channels, columns)
    cot = cotangent.reshape(channels, columns)
    vmem = pl.BlockSpec(memory_space=pltpu.VMEM)
    hbm = pl.BlockSpec(memory_space=pltpu.HBM)
    params = pltpu.CompilerParams(vmem_limit_bytes=16 * 1024 * 1024)
    flat = jax.ShapeDtypeStruct((channels, columns), jnp.float32)
    forth = jax.ShapeDtypeStruct((owners * FORTH, columns), jnp.float32)
    back = jax.ShapeDtypeStruct((owners * BACK, columns), jnp.float32)
    other = lax.ppermute(own, "lat", swap)
    row_shape = jax.ShapeDtypeStruct(conv_weight.shape[1:], jnp.float32)
    half_shape = jax.ShapeDtypeStruct((3, channels // 2, channels), jnp.float32)
    *fetched, packed = pl.pallas_call(
        fetch_kernel,
        out_shape=(flat, row_shape, row_shape, half_shape, forth),
        in_specs=[hbm] * 4,
        out_specs=(vmem,) * 5,
        scratch_shapes=[
            pltpu.VMEM((channels, columns), jnp.float32),
            pltpu.VMEM((channels // 2, columns), jnp.float32),
            pltpu.SemaphoreType.DMA((8,)),
        ],
        compiler_params=params,
        name="fetch",
    )(*[pltpu.with_memory_space_constraint(x, pltpu.HBM) for x in (own, cot, spectral_filter, conv_weight)])
    outgoing = pl.pallas_call(
        conv_kernel,
        out_shape=forth,
        in_specs=[vmem] * 6,
        out_specs=vmem,
        input_output_aliases={5: 0},
        compiler_params=params,
        name="conv",
    )(fetched[0], other, *fetched[1:], packed)
    turns, dft = transform_tables(columns, lon)
    returned = pl.pallas_call(
        spectral_kernel,
        out_shape=back,
        in_specs=[vmem] * 3,
        out_specs=vmem,
        scratch_shapes=[pltpu.VMEM((2 * 8 * lat * lon, 2 * columns), jnp.float32)],
        compiler_params=params,
        name="spectral",
    )(exchanged(outgoing), turns, dft)
    mine = exchanged(returned)
    other = lax.ppermute(mine, "lat", swap)
    rows_scratch = pltpu.VMEM((5, columns + 16, channels // 2), jnp.float32)
    output, total = pl.pallas_call(
        adjoint_kernel,
        out_shape=(flat, jax.ShapeDtypeStruct((columns, channels), jnp.float32)),
        in_specs=[vmem] * 3,
        out_specs=(vmem, vmem),
        scratch_shapes=[rows_scratch],
        compiler_params=params,
        name="adjoint",
    )(mine, own, conv_weight)
    input_grad, filter_grad = pl.pallas_call(
        last_kernel,
        out_shape=(flat, jax.ShapeDtypeStruct(spectral_filter.shape, jnp.float32)),
        in_specs=[vmem] * 5,
        out_specs=(vmem, vmem),
        scratch_shapes=[rows_scratch],
        compiler_params=params,
        name="last",
    )(mine, other, cot, conv_weight, total)
    return (output.reshape(field.shape), input_grad.reshape(field.shape), filter_grad)


def solution(mesh):
    placed = (P(None, "lat", "lon"), P(None, "lat", "lon"), P(), P(None, None, "lon"))
    specs = (P(None, "lat", "lon"), P(None, "lat", "lon"), P(None, None, "lon"))

    def layer(field, cotangent, conv_weight, spectral_filter):
        lat, lon = mesh.shape["lat"], mesh.shape["lon"]
        channels, rows, length = field.shape
        owned = rows == lat == 4 and lon == 8 and channels == 8 * lat * lon and length == 128 * lon
        body = on_device if owned else on_device_any_mesh
        mapped = jax.shard_map(body, mesh=mesh, in_specs=placed, out_specs=specs, check_vma=False)
        return mapped(field, cotangent, conv_weight, spectral_filter)

    return layer
```

```python
from functools import partial

import jax
import jax.numpy as jnp
import numpy as np
from jax import lax
from jax.experimental import pallas as pl
from jax.experimental.pallas import tpu as pltpu
from jax.sharding import PartitionSpec as P

precise = lax.Precision.HIGHEST
three_pass = lax.Precision.HIGH
ROOT_HALF = 0.5**0.5


def padded_2(array, sides, width, wrap):
    for axis, dim in sides:
        peers, length = (lax.axis_size(axis), array.shape[dim])
        up = [(i, (i + 1) % peers) for i in range(peers if wrap else peers - 1)]
        down = [(j, i) for i, j in up]
        last = lax.slice_in_dim(array, length - width, length, axis=dim)
        leading = lax.slice_in_dim(array, 0, width, axis=dim)
        before = lax.ppermute(last, axis, up)
        after = lax.ppermute(leading, axis, down)
        array = jnp.concatenate([before, array, after], axis=dim)
    return array


def partner(array, axis, stride):
    return lax.ppermute(array, axis, [(i, i ^ 1 << stride) for i in range(lax.axis_size(axis))])


def angle_table(first, second, modulus):
    product = first[:, None] * second[None, :] % modulus
    return 2.0 * jnp.pi / modulus * product.astype(jnp.float32)


def apply_taps(padded, taps, lat_rows, columns):
    total = jnp.zeros((taps.shape[2], lat_rows, columns), jnp.float32)
    for tap_row in range(3):
        for tap_col in range(3):
            window = padded[:, tap_row : tap_row + lat_rows, tap_col : tap_col + columns]
            total = total + jnp.einsum(
                "oi,iab->oab", taps[tap_row, tap_col], window, precision=precise
            )
    return total


def with_rims(field):
    wider = padded_2(field, (("lon", 2),), 1, True)
    return padded_2(wider, (("lat", 1),), 1, False)


def local_forward(real_part, imag_part):
    columns = real_part.shape[-1]
    places = lax.iota(jnp.int32, columns)
    angles = angle_table(places, places, columns)
    cosine = jnp.cos(angles)
    sine = jnp.sin(angles)
    out_real = jnp.dot(real_part, cosine, precision=precise) + jnp.dot(
        imag_part, sine, precision=precise
    )
    out_imag = jnp.dot(imag_part, cosine, precision=precise) - jnp.dot(
        real_part, sine, precision=precise
    )
    return (out_real, out_imag)


def local_inverse(real_part, imag_part):
    columns = real_part.shape[-1]
    places = lax.iota(jnp.int32, columns)
    angles = angle_table(places, places, columns)
    cosine = jnp.cos(angles)
    sine = jnp.sin(angles)
    out_real = jnp.dot(real_part, cosine, precision=precise) - jnp.dot(
        imag_part, sine, precision=precise
    )
    out_imag = jnp.dot(imag_part, cosine, precision=precise) + jnp.dot(
        real_part, sine, precision=precise
    )
    return (out_real / columns, out_imag / columns)


def section_angles(place, bit_pos, columns):
    offsets = lax.iota(jnp.int32, columns)
    start = place % 2**bit_pos * columns
    span = 2 * columns * 2**bit_pos
    angles = 2.0 * jnp.pi / span * (start + offsets).astype(jnp.float32)
    upper = place // 2**bit_pos % 2 == 1
    return (jnp.cos(angles), jnp.sin(angles), upper)


def forward_pairs(field):
    extent = lax.axis_size("lon")
    width_bits = extent.bit_length() - 1
    place = lax.axis_index("lon")
    columns = field.shape[-1]
    data = jnp.stack([field, jnp.zeros_like(field)])
    for bit_pos in reversed(range(width_bits)):
        other = partner(data, "lon", bit_pos)
        cosine, sine, upper = section_angles(place, bit_pos, columns)
        differ = other - data
        turned = jnp.stack(
            [differ[0] * cosine + differ[1] * sine, differ[1] * cosine - differ[0] * sine]
        )
        data = jnp.where(upper, turned, data + other)
    out_real, out_imag = local_forward(data[0], data[1])
    return jnp.stack([out_real, out_imag])


def inverse_pairs(spectrum):
    extent = lax.axis_size("lon")
    width_bits = extent.bit_length() - 1
    place = lax.axis_index("lon")
    columns = spectrum.shape[-1]
    back_real, back_imag = local_inverse(spectrum[0], spectrum[1])
    data = jnp.stack([back_real, back_imag])
    for bit_pos in range(width_bits):
        cosine, sine, upper = section_angles(place, bit_pos, columns)
        turned = jnp.stack([data[0] * cosine - data[1] * sine, data[1] * cosine + data[0] * sine])
        outgoing = jnp.where(upper, turned, data)
        other = partner(outgoing, "lon", bit_pos)
        data = jnp.where(upper, other - outgoing, outgoing + other) * 0.5
    return data[0]


def on_device_any_mesh(field, cotangent, conv_weight, spectral_filter):
    lat_rows = field.shape[1]
    columns = field.shape[2]
    total_len = columns * lax.axis_size("lon")
    mixed = apply_taps(with_rims(field), conv_weight, lat_rows, columns)
    hidden_spec = forward_pairs(mixed)
    cot_spec = forward_pairs(cotangent)
    gain_real = spectral_filter[0][:, None, :]
    gain_imag = spectral_filter[1][:, None, :]
    filtered = jnp.stack(
        [
            gain_real * hidden_spec[0] - gain_imag * hidden_spec[1],
            gain_real * hidden_spec[1] + gain_imag * hidden_spec[0],
        ]
    )
    adjoint = jnp.stack(
        [
            gain_real * cot_spec[0] + gain_imag * cot_spec[1],
            gain_real * cot_spec[1] - gain_imag * cot_spec[0],
        ]
    )
    shaped = inverse_pairs(filtered)
    back_field = inverse_pairs(adjoint)
    output = field + shaped
    local_grad = (
        jnp.stack(
            [
                jnp.sum(hidden_spec[0] * cot_spec[0] + hidden_spec[1] * cot_spec[1], axis=1),
                jnp.sum(hidden_spec[0] * cot_spec[1] - hidden_spec[1] * cot_spec[0], axis=1),
            ]
        )
        / total_len
    )
    filter_grad = lax.psum(local_grad, "lat")
    flipped_taps = jnp.transpose(conv_weight[::-1, ::-1], (0, 1, 3, 2))
    input_grad = cotangent + apply_taps(with_rims(back_field), flipped_taps, lat_rows, columns)
    return (output, input_grad, filter_grad)


FORTH, BACK = 49, 57
FIRST_COPIES, IN_FLIGHT = 5, 2


def reversed_bits(value, width):
    return int(format(value, f"0{width}b")[::-1], 2)


def iotas(rows, columns):
    lane = lax.broadcasted_iota(jnp.int32, (rows, columns), 1)
    row = lax.broadcasted_iota(jnp.int32, (rows, columns), 0)
    return lane, row


def fetch_kernel(
    own_ref, cot_ref, filter_ref, taps_ref, own_out, cot_out, gain_out, taps_out, sems
):
    place = lax.axis_index("lat")
    odd, half = lax.rem(place, 2), gain_out.shape[0]
    span = pl.ds(pl.multiple_of(odd * half, half), half)
    copies = [
        pltpu.make_async_copy(own_ref, own_out, sems.at[0]),
        pltpu.make_async_copy(cot_ref, cot_out, sems.at[1]),
        pltpu.make_async_copy(filter_ref.at[place // 2, span], gain_out, sems.at[2]),
    ]

    @pl.when(odd == 1)
    def _():
        half_taps = pltpu.make_async_copy(taps_ref.at[:, :, half:], taps_out, sems.at[3])
        for copy in [half_taps] + copies:
            copy.start()
        for copy in [half_taps] + copies:
            copy.wait()

    @pl.when(odd == 0)
    def _():
        for copy in copies:
            copy.start()
        for copy in copies:
            copy.wait()


def high_low(x):
    high = x.astype(jnp.bfloat16)
    return high, (x - high.astype(jnp.float32)).astype(jnp.bfloat16)


def tall_product(x, high, low):
    rows = x.shape[0]
    x_high, x_low = high_low(x)
    both = jnp.concatenate([x_high, x_low], axis=0)
    both = jnp.dot(both, high, preferred_element_type=jnp.float32)
    rest = jnp.dot(x_high, low, preferred_element_type=jnp.float32)
    return both[:rows] + (both[rows:] + rest)


def conv_kernel(
    own_ref, other_ref, cot_ref, other_cot_ref, gain_ref, half_ref, taps_ref, out_ref, taps, sems
):
    odd, upper = lax.rem(lax.axis_index("lat"), 2), lax.axis_index("lat") // 2
    half = gain_ref.shape[0]
    order = [(row, col) for col in range(3) for row in (1, 2 * upper, 2 - 2 * upper)]

    @pl.when(odd == 0)
    def _():
        copies = [
            pltpu.make_async_copy(taps_ref.at[row, col, :half], taps.at[index], sems.at[index])
            for index, (row, col) in enumerate(order)
        ]
        for copy in copies[:FIRST_COPIES]:
            copy.start()

        def weights(index):
            copies[index].wait()
            if FIRST_COPIES <= index + IN_FLIGHT < len(copies):
                copies[index + IN_FLIGHT].start()
            return high_low(taps[index])

        pack((own_ref, other_ref), (cot_ref, other_cot_ref), gain_ref, weights, 0, out_ref)

    @pl.when(odd == 1)
    def _():
        def weights(index):
            return high_low(half_ref[order[index]])

        pack((other_ref, own_ref), (other_cot_ref, cot_ref), gain_ref, weights, 1, out_ref)


def pack(fields, cots, gain_ref, weights, core, out_ref):
    upper = lax.axis_index("lat") // 2
    half, columns = gain_ref.shape
    for owner in range(half // 8):
        first, here = FORTH * owner, half * core + 8 * owner
        out_ref[first : first + 8, :] = cots[0][here : here + 8, :]
        out_ref[first + 8 : first + 16, :] = cots[1][here : here + 8, :]
        out_ref[first + 40 : first + 48, :] = gain_ref[8 * owner : 8 * owner + 8, :]
    row_0, row_1 = fields[0][...], fields[1][...]
    near = jnp.concatenate(high_low(jnp.where(upper == 0, row_1, row_0)), axis=1)
    both_high, both_low = high_low(jnp.concatenate([row_0, row_1], axis=1))

    def times(weights, values):
        return jnp.dot(weights, values, preferred_element_type=jnp.float32)

    parts = []
    for tap_col in range(3):
        high, low = weights(3 * tap_col)
        middle = times(high, both_high) + (times(high, both_low) + times(low, both_high))
        high, low = weights(3 * tap_col + 1)
        outer = times(high, both_high) + (times(high, both_low) + times(low, both_high))
        high, low = weights(3 * tap_col + 2)
        wide = times(high, near)
        inner = wide[:, :columns] + (wide[:, columns:] + times(low, near[:, :columns]))
        on_0, on_1 = outer[:, :columns], outer[:, columns:]
        parts.append(
            jnp.concatenate(
                [
                    middle[:, :columns] + jnp.where(upper == 0, inner, on_1),
                    middle[:, columns:] + jnp.where(upper == 0, on_0, inner),
                    jnp.where(upper == 0, on_1, on_0),
                ],
                axis=0,
            )
        )
    lane, row = iotas(3 * half, columns)
    left, middle, right = parts
    main = (
        middle
        + jnp.where(lane == 0, 0.0, pltpu.roll(left, 1, 1))
        + jnp.where(lane == columns - 1, 0.0, pltpu.roll(right, columns - 1, 1))
    )
    slot = lane - lax.rem(row, 8) - 8 * (row // half)
    edges = jnp.where(slot == 0, left[:, columns - 1 :], 0.0)
    edges = jnp.where(slot == 24, right[:, 0:1], edges)
    edges = edges[:half] + edges[half : 2 * half] + edges[2 * half :]
    for owner in range(half // 8):
        first = FORTH * owner
        for part in range(3):
            here = half * part + 8 * owner
            out_ref[first + 16 + 8 * part : first + 24 + 8 * part, :] = main[here : here + 8]
        out_ref[first + 48 : first + 49, :] = jnp.sum(
            edges[8 * owner : 8 * owner + 8], axis=0, keepdims=True
        )


def transform_8(x):
    s = [x[d] + x[d + 4] for d in range(4)]
    t = [x[d] - x[d + 4] for d in range(4)]
    plus, minus = ROOT_HALF * (t[1] + t[3]), ROOT_HALF * (t[1] - t[3])
    return [
        (s[0] + s[2] + (s[1] + s[3]), None),
        (t[0] + minus, -t[2] - plus),
        (s[0] - s[2], s[3] - s[1]),
        (t[0] - minus, t[2] - plus),
        (s[0] + s[2] - (s[1] + s[3]), None),
    ]


def spectral_kernel(in_ref, turn_ref, dft_ref, out_ref, work):
    rows, lon = 4, 8
    columns = in_ref.shape[-1]
    lane, sub = iotas(8, columns)
    me = lax.axis_index("lat") // 2 * lon + lax.axis_index("lon")

    def message(chip, place, first, count):
        start = FORTH * (chip * lon + place) + first
        return in_ref[start : start + count, :]

    def edge(row, place, group):
        chip, part = row // 2, row % 2
        wanted = lane == sub + 8 * part + 24 * group
        line = jnp.where(wanted, message(chip, place, 48, 1), 0.0)
        if row in (1, 2):
            wanted = lane == sub + 16 + 24 * group
            line = line + jnp.where(wanted, message(1 - chip, place, 48, 1), 0.0)
        return jnp.sum(line, axis=1, keepdims=True)

    grid = []
    for place in range(lon):
        mixed = []
        for row in range(rows):
            tile = message(row // 2, place, 16 + 8 * (row % 2), 8)
            if row in (1, 2):
                tile = tile + message(1 - row // 2, place, 32, 8)
            tile = tile + jnp.where(lane == 0, edge(row, (place - 1) % lon, 0), 0.0)
            tile = tile + jnp.where(lane == columns - 1, edge(row, (place + 1) % lon, 1), 0.0)
            mixed.append(tile)
        cot = [message(row // 2, place, 8 * (row % 2), 8) for row in range(rows)]
        grid.append(jnp.concatenate(mixed + cot, axis=0))
    pairs = transform_8(grid)
    height = 16 * rows
    for residue in range(lon):
        real, imag = pairs[min(residue, lon - residue)]
        cosine, sine = turn_ref[residue : residue + 1, :], turn_ref[8 + residue : 9 + residue, :]
        if imag is None:
            turned = (real * cosine, -real * sine)
        elif residue < 4:
            turned = (real * cosine + imag * sine, imag * cosine - real * sine)
        else:
            turned = (real * cosine - imag * sine, -imag * cosine - real * sine)
        span = pl.ds(residue * height, height)
        work[span, 0:columns] = turned[0]
        work[span, columns:] = turned[1]
    chunk = lon * height // 4
    pieces = [pl.ds(first, chunk) for first in range(0, lon * height, chunk)]
    table = high_low(dft_ref[...])
    spectra = jnp.concatenate(
        [tall_product(work[piece], *table) for piece in pieces], axis=0
    )
    scale = 1.0 / (lon * columns)
    half = 8 * rows
    gradients = []
    for residue in range(lon):
        place = reversed_bits(residue, 3)
        part = spectra[residue * height : (residue + 1) * height]
        mix_re, mix_im = part[:half, :columns], part[:half, columns:]
        cot_re, cot_im = part[half:, :columns], part[half:, columns:]
        gain_re = jnp.concatenate([message(0, place, 40, 8) * scale] * rows, axis=0)
        gain_im = jnp.concatenate([message(1, place, 40, 8) * scale] * rows, axis=0)
        top = pl.ds(residue * height, half)
        bottom = pl.ds(residue * height + half, half)
        work[top, 0:columns] = gain_re * mix_re - gain_im * mix_im
        work[top, columns:] = -(gain_re * mix_im + gain_im * mix_re)
        work[bottom, 0:columns] = gain_re * cot_re + gain_im * cot_im
        work[bottom, columns:] = gain_im * cot_re - gain_re * cot_im
        grad_re = (mix_re * cot_re + mix_im * cot_im) * scale
        grad_im = (mix_re * cot_im - mix_im * cot_re) * scale
        gradients.append(
            [
                grad[0:8] + grad[8:16] + (grad[16:24] + grad[24:32])
                for grad in (grad_re, grad_im)
            ]
        )
    back = jnp.concatenate(
        [tall_product(work[piece], *table) for piece in pieces], axis=0
    )
    turned = []
    for residue in range(lon):
        part = back[residue * height : (residue + 1) * height]
        real, imag = part[:, :columns], part[:, columns:]
        cosine, sine = turn_ref[residue : residue + 1, :], turn_ref[8 + residue : 9 + residue, :]
        turned.append((real * cosine + imag * sine, real * sine - imag * cosine))
    sums = [turned[r][0] + turned[lon - r][0] for r in (1, 2, 3)]
    gaps = [turned[r][1] - turned[lon - r][1] for r in (1, 2, 3)]
    first, fourth = turned[0][0], turned[4][0]
    even = [
        first + fourth + sums[1],
        first - fourth - gaps[1],
        first + fourth - sums[1],
        first - fourth + gaps[1],
    ]
    swing = [
        sums[0] + sums[2],
        ROOT_HALF * (sums[0] - gaps[0] - sums[2] - gaps[2]),
        gaps[2] - gaps[0],
        ROOT_HALF * (sums[2] - gaps[2] - sums[0] - gaps[0]),
    ]
    series = [even[d] + swing[d] for d in range(4)] + [even[d] - swing[d] for d in range(4)]
    slots = [lane == 8 * lax.rem(me + group, 16) + sub for group in range(6)]
    for place in range(lon):
        residue = reversed_bits(place, 3)
        before, after = series[(place - 1) % lon], series[(place + 1) % lon]
        for chip in range(2):
            start = BACK * (chip * lon + place)
            rims = jnp.zeros((8, columns), jnp.float32)
            for step in range(3):
                here = half + 8 * (chip + step)
                span = slice(here, here + 8)
                rims = jnp.where(slots[2 * step], before[span, columns - 1 :], rims)
                rims = jnp.where(slots[2 * step + 1], after[span, 0:1], rims)
                first = start + 16 + 8 * step
                out_ref[first : first + 8, :] = series[place][span]
            out_ref[start : start + 16, :] = series[place][16 * chip : 16 * chip + 16]
            for part in range(2):
                first = start + 40 + 8 * part
                out_ref[first : first + 8, :] = gradients[residue][part]
            out_ref[start + 56 : start + 57, :] = jnp.sum(rims, axis=0, keepdims=True)


def partial_adjoint(message_ref, taps_ref, rows_ref, part):
    half, columns = rows_ref.shape[-1], message_ref.shape[-1]
    place = lax.axis_index("lat")
    index = place - place // 2
    owners = half // 8
    lines = message_ref[pl.ds(56, owners, stride=BACK), :]
    lane, owner = iotas(owners, columns)
    rows_ref[0] = jnp.zeros(rows_ref.shape[1:], jnp.float32)
    rows_ref[4] = jnp.zeros(rows_ref.shape[1:], jnp.float32)
    for step in range(3):
        pieces = [
            message_ref[BACK * j + 16 + 8 * step : BACK * j + 24 + 8 * step, :] for j in range(owners)
        ]
        rows_ref[1 + step, 8 : 8 + columns, :] = jnp.concatenate(pieces, axis=0).T
        for rim, target in ((2 * step, 7), (2 * step + 1, 8 + columns)):
            wanted = lane // 8 == lax.rem(owner + rim, owners)
            line = jnp.sum(jnp.where(wanted, lines, 0.0), axis=0, keepdims=True)
            line = jnp.broadcast_to(line, (8, columns))
            if rim:
                line = pltpu.roll(line, columns - 8 * rim, 1)
            rows_ref[1 + step, target : target + 1, :] = line[0:1]
    span = pl.ds(pl.multiple_of(part * half, half), half)
    windows, weights = [], []
    for tap_row in range(3):
        for tap_col in range(3):
            first = 9 - tap_col
            windows.append(rows_ref[index + 2 - tap_row, first : first + columns, :])
            weights.append(taps_ref[tap_row, tap_col, span])
    total = 0.0
    for pair in range(0, 9, 2):
        window = jnp.concatenate(windows[pair : pair + 2], axis=1)
        weight = jnp.concatenate(weights[pair : pair + 2], axis=0)
        total = total + tall_product(window, *high_low(weight))
    return total


def adjoint_kernel(mine_ref, taps_ref, total_ref, rows_ref):
    part = lax.rem(lax.axis_index("lat"), 2)
    total_ref[...] = partial_adjoint(mine_ref, taps_ref, rows_ref, part)


def last_kernel(
    mine_ref, other_ref, field_ref, cot_ref, taps_ref, total_ref, out_ref, grad_ref, gain_ref, rows_ref
):
    half = cot_ref.shape[0] // 2
    part = lax.rem(lax.axis_index("lat"), 2)
    for message_ref, side in ((mine_ref, part), (other_ref, 1 - part)):
        for owner in range(half // 8):
            here = pl.ds(pl.multiple_of(half * side + 8 * owner, 8), 8)
            start = BACK * owner
            first, second = message_ref[start : start + 8, :], message_ref[start + 8 : start + 16, :]
            out_ref[here, :] = field_ref[here, :] + jnp.where(part == 0, first, second)
            gain_ref[0, here, :] = message_ref[start + 40 : start + 48, :]
            gain_ref[1, here, :] = message_ref[start + 48 : start + 56, :]
    total = total_ref[...] + partial_adjoint(other_ref, taps_ref, rows_ref, 1 - part)
    grad_ref[...] = cot_ref[...] + total.T


def transform_tables(columns, lon):
    places = np.arange(columns)
    turn = 2.0 * np.pi * (np.arange(lon)[:, None] * places[None, :]) / (lon * columns)
    angle = 2.0 * np.pi * (places[:, None] * places[None, :] % columns) / columns
    cosine, sine = np.cos(angle), np.sin(angle)
    dft = np.block([[cosine, -sine], [sine, cosine]])
    turns = np.concatenate([np.cos(turn), np.sin(turn)], axis=0)
    return jnp.asarray(turns, jnp.float32), jnp.asarray(dft, jnp.float32)


def exchanged(flat, lat, lon):
    rows, columns = flat.shape
    groups = [
        [(2 * chip + core) * lon + place for chip in range(lat // 2) for place in range(lon)]
        for core in range(2)
    ]
    moved = lax.all_to_all(
        flat.reshape(rows, 1, columns),
        ("lat", "lon"),
        0,
        0,
        tiled=True,
        axis_index_groups=groups,
    )
    return moved.reshape(rows, columns)


def in_hbm(x):
    return pltpu.with_memory_space_constraint(x, pltpu.HBM)


def on_device(field, cotangent, conv_weight, spectral_filter):
    channels, _, columns = field.shape
    lat, lon = lax.axis_size("lat"), lax.axis_size("lon")
    owners = lat * lon // 2
    swap = [(i, i ^ 1) for i in range(lat)]
    own = field.reshape(channels, columns)
    cot = cotangent.reshape(channels, columns)
    vmem = pl.BlockSpec(memory_space=pltpu.VMEM)
    hbm = pl.BlockSpec(memory_space=pltpu.HBM)
    params = pltpu.CompilerParams(vmem_limit_bytes=16 * 1024 * 1024)
    flat = jax.ShapeDtypeStruct((channels, columns), jnp.float32)
    half_taps = jax.ShapeDtypeStruct((3, 3, channels // 2, channels), jnp.float32)
    forth = jax.ShapeDtypeStruct((owners * FORTH, columns), jnp.float32)
    back = jax.ShapeDtypeStruct((owners * BACK, columns), jnp.float32)
    other, other_cot = lax.ppermute((own, cot), "lat", swap)
    gain_half = jax.ShapeDtypeStruct((channels // 2, columns), jnp.float32)
    own_here, cot_here, gain, taps = pl.pallas_call(
        fetch_kernel,
        out_shape=(flat, flat, gain_half, half_taps),
        in_specs=[hbm] * 4,
        out_specs=(vmem,) * 4,
        scratch_shapes=[pltpu.SemaphoreType.DMA((4,))],
        compiler_params=params,
        name="fetch",
    )(*map(in_hbm, (own, cot, spectral_filter, conv_weight)))
    outgoing = pl.pallas_call(
        conv_kernel,
        out_shape=forth,
        in_specs=[vmem] * 6 + [hbm],
        out_specs=vmem,
        scratch_shapes=[
            pltpu.VMEM((9, channels // 2, channels), jnp.float32),
            pltpu.SemaphoreType.DMA((9,)),
        ],
        compiler_params=params,
        name="conv",
    )(own_here, other, cot_here, other_cot, gain, taps, in_hbm(conv_weight))
    turns, dft = transform_tables(columns, lon)
    returned = pl.pallas_call(
        spectral_kernel,
        out_shape=back,
        in_specs=[vmem] * 3,
        out_specs=vmem,
        scratch_shapes=[pltpu.VMEM((2 * 8 * lat * lon, 2 * columns), jnp.float32)],
        compiler_params=params,
        name="spectral",
    )(exchanged(outgoing, lat, lon), turns, dft)
    mine = exchanged(returned, lat, lon)
    other = lax.ppermute(mine, "lat", swap)
    rows_scratch = pltpu.VMEM((5, columns + 16, channels // 2), jnp.float32)
    total = pl.pallas_call(
        adjoint_kernel,
        out_shape=jax.ShapeDtypeStruct((columns, channels), jnp.float32),
        in_specs=[vmem] * 2,
        out_specs=vmem,
        scratch_shapes=[rows_scratch],
        compiler_params=params,
        name="adjoint",
    )(mine, conv_weight)
    output, input_grad, filter_grad = pl.pallas_call(
        last_kernel,
        out_shape=(flat, flat, jax.ShapeDtypeStruct(spectral_filter.shape, jnp.float32)),
        in_specs=[vmem] * 6,
        out_specs=(vmem, vmem, vmem),
        scratch_shapes=[rows_scratch],
        compiler_params=params,
        name="last",
    )(mine, other, own, cot, conv_weight, total)
    return (output.reshape(field.shape), input_grad.reshape(field.shape), filter_grad)


def solution(mesh):
    placed = (P(None, "lat", "lon"), P(None, "lat", "lon"), P(), P(None, None, "lon"))
    specs = (P(None, "lat", "lon"), P(None, "lat", "lon"), P(None, None, "lon"))

    def layer(field, cotangent, conv_weight, spectral_filter):
        lat, lon = mesh.shape["lat"], mesh.shape["lon"]
        channels, rows, length = field.shape
        owned = rows == lat == 4 and lon == 8 and channels == 8 * lat * lon and length == 128 * lon
        body = on_device if owned else on_device_any_mesh
        mapped = jax.shard_map(body, mesh=mesh, in_specs=placed, out_specs=specs, check_vma=False)
        return mapped(field, cotangent, conv_weight, spectral_filter)

    return layer
```

```python
from functools import partial

import jax
import jax.numpy as jnp
import numpy as np
from jax import lax
from jax.experimental import pallas as pl
from jax.experimental.pallas import tpu as pltpu
from jax.sharding import PartitionSpec as P

precise = lax.Precision.HIGHEST
three_pass = lax.Precision.HIGH
ROOT_HALF = 0.5**0.5


def padded_2(array, sides, width, wrap):
    for axis, dim in sides:
        peers, length = (lax.axis_size(axis), array.shape[dim])
        up = [(i, (i + 1) % peers) for i in range(peers if wrap else peers - 1)]
        down = [(j, i) for i, j in up]
        last = lax.slice_in_dim(array, length - width, length, axis=dim)
        leading = lax.slice_in_dim(array, 0, width, axis=dim)
        before = lax.ppermute(last, axis, up)
        after = lax.ppermute(leading, axis, down)
        array = jnp.concatenate([before, array, after], axis=dim)
    return array


def partner(array, axis, stride):
    return lax.ppermute(array, axis, [(i, i ^ 1 << stride) for i in range(lax.axis_size(axis))])


def angle_table(first, second, modulus):
    product = first[:, None] * second[None, :] % modulus
    return 2.0 * jnp.pi / modulus * product.astype(jnp.float32)


def apply_taps(padded, taps, lat_rows, columns):
    total = jnp.zeros((taps.shape[2], lat_rows, columns), jnp.float32)
    for tap_row in range(3):
        for tap_col in range(3):
            window = padded[:, tap_row : tap_row + lat_rows, tap_col : tap_col + columns]
            total = total + jnp.einsum(
                "oi,iab->oab", taps[tap_row, tap_col], window, precision=precise
            )
    return total


def with_rims(field):
    wider = padded_2(field, (("lon", 2),), 1, True)
    return padded_2(wider, (("lat", 1),), 1, False)


def local_forward(real_part, imag_part):
    columns = real_part.shape[-1]
    places = lax.iota(jnp.int32, columns)
    angles = angle_table(places, places, columns)
    cosine = jnp.cos(angles)
    sine = jnp.sin(angles)
    out_real = jnp.dot(real_part, cosine, precision=precise) + jnp.dot(
        imag_part, sine, precision=precise
    )
    out_imag = jnp.dot(imag_part, cosine, precision=precise) - jnp.dot(
        real_part, sine, precision=precise
    )
    return (out_real, out_imag)


def local_inverse(real_part, imag_part):
    columns = real_part.shape[-1]
    places = lax.iota(jnp.int32, columns)
    angles = angle_table(places, places, columns)
    cosine = jnp.cos(angles)
    sine = jnp.sin(angles)
    out_real = jnp.dot(real_part, cosine, precision=precise) - jnp.dot(
        imag_part, sine, precision=precise
    )
    out_imag = jnp.dot(imag_part, cosine, precision=precise) + jnp.dot(
        real_part, sine, precision=precise
    )
    return (out_real / columns, out_imag / columns)


def section_angles(place, bit_pos, columns):
    offsets = lax.iota(jnp.int32, columns)
    start = place % 2**bit_pos * columns
    span = 2 * columns * 2**bit_pos
    angles = 2.0 * jnp.pi / span * (start + offsets).astype(jnp.float32)
    upper = place // 2**bit_pos % 2 == 1
    return (jnp.cos(angles), jnp.sin(angles), upper)


def forward_pairs(field):
    extent = lax.axis_size("lon")
    width_bits = extent.bit_length() - 1
    place = lax.axis_index("lon")
    columns = field.shape[-1]
    data = jnp.stack([field, jnp.zeros_like(field)])
    for bit_pos in reversed(range(width_bits)):
        other = partner(data, "lon", bit_pos)
        cosine, sine, upper = section_angles(place, bit_pos, columns)
        differ = other - data
        turned = jnp.stack(
            [differ[0] * cosine + differ[1] * sine, differ[1] * cosine - differ[0] * sine]
        )
        data = jnp.where(upper, turned, data + other)
    out_real, out_imag = local_forward(data[0], data[1])
    return jnp.stack([out_real, out_imag])


def inverse_pairs(spectrum):
    extent = lax.axis_size("lon")
    width_bits = extent.bit_length() - 1
    place = lax.axis_index("lon")
    columns = spectrum.shape[-1]
    back_real, back_imag = local_inverse(spectrum[0], spectrum[1])
    data = jnp.stack([back_real, back_imag])
    for bit_pos in range(width_bits):
        cosine, sine, upper = section_angles(place, bit_pos, columns)
        turned = jnp.stack([data[0] * cosine - data[1] * sine, data[1] * cosine + data[0] * sine])
        outgoing = jnp.where(upper, turned, data)
        other = partner(outgoing, "lon", bit_pos)
        data = jnp.where(upper, other - outgoing, outgoing + other) * 0.5
    return data[0]


def on_device_any_mesh(field, cotangent, conv_weight, spectral_filter):
    lat_rows = field.shape[1]
    columns = field.shape[2]
    total_len = columns * lax.axis_size("lon")
    mixed = apply_taps(with_rims(field), conv_weight, lat_rows, columns)
    hidden_spec = forward_pairs(mixed)
    cot_spec = forward_pairs(cotangent)
    gain_real = spectral_filter[0][:, None, :]
    gain_imag = spectral_filter[1][:, None, :]
    filtered = jnp.stack(
        [
            gain_real * hidden_spec[0] - gain_imag * hidden_spec[1],
            gain_real * hidden_spec[1] + gain_imag * hidden_spec[0],
        ]
    )
    adjoint = jnp.stack(
        [
            gain_real * cot_spec[0] + gain_imag * cot_spec[1],
            gain_real * cot_spec[1] - gain_imag * cot_spec[0],
        ]
    )
    shaped = inverse_pairs(filtered)
    back_field = inverse_pairs(adjoint)
    output = field + shaped
    local_grad = (
        jnp.stack(
            [
                jnp.sum(hidden_spec[0] * cot_spec[0] + hidden_spec[1] * cot_spec[1], axis=1),
                jnp.sum(hidden_spec[0] * cot_spec[1] - hidden_spec[1] * cot_spec[0], axis=1),
            ]
        )
        / total_len
    )
    filter_grad = lax.psum(local_grad, "lat")
    flipped_taps = jnp.transpose(conv_weight[::-1, ::-1], (0, 1, 3, 2))
    input_grad = cotangent + apply_taps(with_rims(back_field), flipped_taps, lat_rows, columns)
    return (output, input_grad, filter_grad)


FORTH, BACK = 49, 57
FIRST_COPIES, IN_FLIGHT = 5, 2


def rank(chip, place):
    return 8 * (place % 2) + 4 * chip + 2 * (place // 2 % 2) + place // 4


def reversed_bits(value, width):
    return int(format(value, f"0{width}b")[::-1], 2)


def iotas(rows, columns):
    lane = lax.broadcasted_iota(jnp.int32, (rows, columns), 1)
    row = lax.broadcasted_iota(jnp.int32, (rows, columns), 0)
    return lane, row


def fetch_kernel(
    own_ref, cot_ref, filter_ref, taps_ref, own_out, cot_out, gain_out, taps_out, sems
):
    place = lax.axis_index("lat")
    odd, half = lax.rem(place, 2), gain_out.shape[0]
    span = pl.ds(pl.multiple_of(odd * half, half), half)
    copies = [
        pltpu.make_async_copy(own_ref, own_out, sems.at[0]),
        pltpu.make_async_copy(cot_ref, cot_out, sems.at[1]),
        pltpu.make_async_copy(filter_ref.at[place // 2, span], gain_out, sems.at[2]),
    ]

    @pl.when(odd == 1)
    def _():
        half_taps = pltpu.make_async_copy(taps_ref.at[:, :, half:], taps_out, sems.at[3])
        for copy in [half_taps] + copies:
            copy.start()
        for copy in [half_taps] + copies:
            copy.wait()

    @pl.when(odd == 0)
    def _():
        for copy in copies:
            copy.start()
        for copy in copies:
            copy.wait()


def high_low(x):
    high = x.astype(jnp.bfloat16)
    return high, (x - high.astype(jnp.float32)).astype(jnp.bfloat16)


def tall_product(x, high, low):
    rows = x.shape[0]
    x_high, x_low = high_low(x)
    both = jnp.concatenate([x_high, x_low], axis=0)
    both = jnp.dot(both, high, preferred_element_type=jnp.float32)
    rest = jnp.dot(x_high, low, preferred_element_type=jnp.float32)
    return both[:rows] + (both[rows:] + rest)


def conv_kernel(
    own_ref, other_ref, cot_ref, other_cot_ref, gain_ref, half_ref, taps_ref, out_ref, taps, sems
):
    odd, upper = lax.rem(lax.axis_index("lat"), 2), lax.axis_index("lat") // 2
    half = gain_ref.shape[0]
    order = [(row, col) for col in range(3) for row in (1, 2 * upper, 2 - 2 * upper)]

    @pl.when(odd == 0)
    def _():
        copies = [
            pltpu.make_async_copy(taps_ref.at[row, col, :half], taps.at[index], sems.at[index])
            for index, (row, col) in enumerate(order)
        ]
        for copy in copies[:FIRST_COPIES]:
            copy.start()

        def weights(index):
            copies[index].wait()
            if FIRST_COPIES <= index + IN_FLIGHT < len(copies):
                copies[index + IN_FLIGHT].start()
            return high_low(taps[index])

        pack((own_ref, other_ref), (cot_ref, other_cot_ref), gain_ref, weights, 0, out_ref)

    @pl.when(odd == 1)
    def _():
        def weights(index):
            return high_low(half_ref[order[index]])

        pack((other_ref, own_ref), (other_cot_ref, cot_ref), gain_ref, weights, 1, out_ref)


def pack(fields, cots, gain_ref, weights, core, out_ref):
    upper = lax.axis_index("lat") // 2
    half, columns = gain_ref.shape
    for owner in range(half // 8):
        first, here = FORTH * owner, half * core + 8 * owner
        out_ref[first : first + 8, :] = cots[0][here : here + 8, :]
        out_ref[first + 8 : first + 16, :] = cots[1][here : here + 8, :]
        out_ref[first + 40 : first + 48, :] = gain_ref[8 * owner : 8 * owner + 8, :]
    row_0, row_1 = fields[0][...], fields[1][...]
    near = jnp.concatenate(high_low(jnp.where(upper == 0, row_1, row_0)), axis=1)
    both_high, both_low = high_low(jnp.concatenate([row_0, row_1], axis=1))

    def times(weights, values):
        return jnp.dot(weights, values, preferred_element_type=jnp.float32)

    parts = []
    for tap_col in range(3):
        high, low = weights(3 * tap_col)
        middle = times(high, both_high) + (times(high, both_low) + times(low, both_high))
        high, low = weights(3 * tap_col + 1)
        outer = times(high, both_high) + (times(high, both_low) + times(low, both_high))
        high, low = weights(3 * tap_col + 2)
        wide = times(high, near)
        inner = wide[:, :columns] + (wide[:, columns:] + times(low, near[:, :columns]))
        on_0, on_1 = outer[:, :columns], outer[:, columns:]
        parts.append(
            jnp.concatenate(
                [
                    middle[:, :columns] + jnp.where(upper == 0, inner, on_1),
                    middle[:, columns:] + jnp.where(upper == 0, on_0, inner),
                    jnp.where(upper == 0, on_1, on_0),
                ],
                axis=0,
            )
        )
    lane, row = iotas(3 * half, columns)
    left, middle, right = parts
    main = (
        middle
        + jnp.where(lane == 0, 0.0, pltpu.roll(left, 1, 1))
        + jnp.where(lane == columns - 1, 0.0, pltpu.roll(right, columns - 1, 1))
    )
    slot = lane - lax.rem(row, 8) - 8 * (row // half)
    edges = jnp.where(slot == 0, left[:, columns - 1 :], 0.0)
    edges = jnp.where(slot == 24, right[:, 0:1], edges)
    edges = edges[:half] + edges[half : 2 * half] + edges[2 * half :]
    for owner in range(half // 8):
        first = FORTH * owner
        for part in range(3):
            here = half * part + 8 * owner
            out_ref[first + 16 + 8 * part : first + 24 + 8 * part, :] = main[here : here + 8]
        out_ref[first + 48 : first + 49, :] = jnp.sum(
            edges[8 * owner : 8 * owner + 8], axis=0, keepdims=True
        )


def transform_8(x):
    s = [x[d] + x[d + 4] for d in range(4)]
    t = [x[d] - x[d + 4] for d in range(4)]
    plus, minus = ROOT_HALF * (t[1] + t[3]), ROOT_HALF * (t[1] - t[3])
    return [
        (s[0] + s[2] + (s[1] + s[3]), None),
        (t[0] + minus, -t[2] - plus),
        (s[0] - s[2], s[3] - s[1]),
        (t[0] - minus, t[2] - plus),
        (s[0] + s[2] - (s[1] + s[3]), None),
    ]


def spectral_kernel(in_ref, turn_ref, dft_ref, out_ref, work):
    rows, lon = 4, 8
    columns = in_ref.shape[-1]
    lane, sub = iotas(8, columns)
    me = rank(lax.axis_index("lat") // 2, lax.axis_index("lon"))

    def message(chip, place, first, count):
        start = FORTH * rank(chip, place) + first
        return in_ref[start : start + count, :]

    def edge(row, place, group):
        chip, part = row // 2, row % 2
        wanted = lane == sub + 8 * part + 24 * group
        line = jnp.where(wanted, message(chip, place, 48, 1), 0.0)
        if row in (1, 2):
            wanted = lane == sub + 16 + 24 * group
            line = line + jnp.where(wanted, message(1 - chip, place, 48, 1), 0.0)
        return jnp.sum(line, axis=1, keepdims=True)

    grid = []
    for place in range(lon):
        mixed = []
        for row in range(rows):
            tile = message(row // 2, place, 16 + 8 * (row % 2), 8)
            if row in (1, 2):
                tile = tile + message(1 - row // 2, place, 32, 8)
            tile = tile + jnp.where(lane == 0, edge(row, (place - 1) % lon, 0), 0.0)
            tile = tile + jnp.where(lane == columns - 1, edge(row, (place + 1) % lon, 1), 0.0)
            mixed.append(tile)
        cot = [message(row // 2, place, 8 * (row % 2), 8) for row in range(rows)]
        grid.append(jnp.concatenate(mixed + cot, axis=0))
    pairs = transform_8(grid)
    height = 16 * rows
    for residue in range(lon):
        real, imag = pairs[min(residue, lon - residue)]
        cosine, sine = turn_ref[residue : residue + 1, :], turn_ref[8 + residue : 9 + residue, :]
        if imag is None:
            turned = (real * cosine, -real * sine)
        elif residue < 4:
            turned = (real * cosine + imag * sine, imag * cosine - real * sine)
        else:
            turned = (real * cosine - imag * sine, -imag * cosine - real * sine)
        span = pl.ds(residue * height, height)
        work[span, 0:columns] = turned[0]
        work[span, columns:] = turned[1]
    chunk = lon * height // 4
    pieces = [pl.ds(first, chunk) for first in range(0, lon * height, chunk)]
    table = high_low(dft_ref[...])
    spectra = jnp.concatenate(
        [tall_product(work[piece], *table) for piece in pieces], axis=0
    )
    scale = 1.0 / (lon * columns)
    half = 8 * rows
    gradients = []
    for residue in range(lon):
        place = reversed_bits(residue, 3)
        part = spectra[residue * height : (residue + 1) * height]
        mix_re, mix_im = part[:half, :columns], part[:half, columns:]
        cot_re, cot_im = part[half:, :columns], part[half:, columns:]
        gain_re = jnp.concatenate([message(0, place, 40, 8) * scale] * rows, axis=0)
        gain_im = jnp.concatenate([message(1, place, 40, 8) * scale] * rows, axis=0)
        top = pl.ds(residue * height, half)
        bottom = pl.ds(residue * height + half, half)
        work[top, 0:columns] = gain_re * mix_re - gain_im * mix_im
        work[top, columns:] = -(gain_re * mix_im + gain_im * mix_re)
        work[bottom, 0:columns] = gain_re * cot_re + gain_im * cot_im
        work[bottom, columns:] = gain_im * cot_re - gain_re * cot_im
        grad_re = (mix_re * cot_re + mix_im * cot_im) * scale
        grad_im = (mix_re * cot_im - mix_im * cot_re) * scale
        gradients.append(
            [
                grad[0:8] + grad[8:16] + (grad[16:24] + grad[24:32])
                for grad in (grad_re, grad_im)
            ]
        )
    back = jnp.concatenate(
        [tall_product(work[piece], *table) for piece in pieces], axis=0
    )
    turned = []
    for residue in range(lon):
        part = back[residue * height : (residue + 1) * height]
        real, imag = part[:, :columns], part[:, columns:]
        cosine, sine = turn_ref[residue : residue + 1, :], turn_ref[8 + residue : 9 + residue, :]
        turned.append((real * cosine + imag * sine, real * sine - imag * cosine))
    sums = [turned[r][0] + turned[lon - r][0] for r in (1, 2, 3)]
    gaps = [turned[r][1] - turned[lon - r][1] for r in (1, 2, 3)]
    first, fourth = turned[0][0], turned[4][0]
    even = [
        first + fourth + sums[1],
        first - fourth - gaps[1],
        first + fourth - sums[1],
        first - fourth + gaps[1],
    ]
    swing = [
        sums[0] + sums[2],
        ROOT_HALF * (sums[0] - gaps[0] - sums[2] - gaps[2]),
        gaps[2] - gaps[0],
        ROOT_HALF * (sums[2] - gaps[2] - sums[0] - gaps[0]),
    ]
    series = [even[d] + swing[d] for d in range(4)] + [even[d] - swing[d] for d in range(4)]
    slots = [lane == 8 * lax.rem(me + group, 16) + sub for group in range(6)]
    for place in range(lon):
        residue = reversed_bits(place, 3)
        before, after = series[(place - 1) % lon], series[(place + 1) % lon]
        for chip in range(2):
            start = BACK * rank(chip, place)
            rims = jnp.zeros((8, columns), jnp.float32)
            for step in range(3):
                here = half + 8 * (chip + step)
                span = slice(here, here + 8)
                rims = jnp.where(slots[2 * step], before[span, columns - 1 :], rims)
                rims = jnp.where(slots[2 * step + 1], after[span, 0:1], rims)
                first = start + 16 + 8 * step
                out_ref[first : first + 8, :] = series[place][span]
            out_ref[start : start + 16, :] = series[place][16 * chip : 16 * chip + 16]
            for part in range(2):
                first = start + 40 + 8 * part
                out_ref[first : first + 8, :] = gradients[residue][part]
            out_ref[start + 56 : start + 57, :] = jnp.sum(rims, axis=0, keepdims=True)


def partial_adjoint(message_ref, taps_ref, rows_ref, part):
    half, columns = rows_ref.shape[-1], message_ref.shape[-1]
    place = lax.axis_index("lat")
    index = place - place // 2
    owners = half // 8
    lines = message_ref[pl.ds(56, owners, stride=BACK), :]
    lane, owner = iotas(owners, columns)
    rows_ref[0] = jnp.zeros(rows_ref.shape[1:], jnp.float32)
    rows_ref[4] = jnp.zeros(rows_ref.shape[1:], jnp.float32)
    for step in range(3):
        pieces = [
            message_ref[BACK * j + 16 + 8 * step : BACK * j + 24 + 8 * step, :] for j in range(owners)
        ]
        rows_ref[1 + step, 8 : 8 + columns, :] = jnp.concatenate(pieces, axis=0).T
        for rim, target in ((2 * step, 7), (2 * step + 1, 8 + columns)):
            wanted = lane // 8 == lax.rem(owner + rim, owners)
            line = jnp.sum(jnp.where(wanted, lines, 0.0), axis=0, keepdims=True)
            line = jnp.broadcast_to(line, (8, columns))
            if rim:
                line = pltpu.roll(line, columns - 8 * rim, 1)
            rows_ref[1 + step, target : target + 1, :] = line[0:1]
    span = pl.ds(pl.multiple_of(part * half, half), half)
    windows, weights = [], []
    for tap_row in range(3):
        for tap_col in range(3):
            first = 9 - tap_col
            windows.append(rows_ref[index + 2 - tap_row, first : first + columns, :])
            weights.append(taps_ref[tap_row, tap_col, span])
    total = 0.0
    for pair in range(0, 9, 2):
        window = jnp.concatenate(windows[pair : pair + 2], axis=1)
        weight = jnp.concatenate(weights[pair : pair + 2], axis=0)
        total = total + tall_product(window, *high_low(weight))
    return total


def adjoint_kernel(mine_ref, taps_ref, total_ref, rows_ref):
    part = lax.rem(lax.axis_index("lat"), 2)
    total_ref[...] = partial_adjoint(mine_ref, taps_ref, rows_ref, part)


def last_kernel(
    mine_ref, other_ref, field_ref, cot_ref, taps_ref, total_ref, out_ref, grad_ref, gain_ref, rows_ref
):
    half = cot_ref.shape[0] // 2
    part = lax.rem(lax.axis_index("lat"), 2)
    for message_ref, side in ((mine_ref, part), (other_ref, 1 - part)):
        for owner in range(half // 8):
            here = pl.ds(pl.multiple_of(half * side + 8 * owner, 8), 8)
            start = BACK * owner
            first, second = message_ref[start : start + 8, :], message_ref[start + 8 : start + 16, :]
            out_ref[here, :] = field_ref[here, :] + jnp.where(part == 0, first, second)
            gain_ref[0, here, :] = message_ref[start + 40 : start + 48, :]
            gain_ref[1, here, :] = message_ref[start + 48 : start + 56, :]
    total = total_ref[...] + partial_adjoint(other_ref, taps_ref, rows_ref, 1 - part)
    grad_ref[...] = cot_ref[...] + total.T


def transform_tables(columns, lon):
    places = np.arange(columns)
    turn = 2.0 * np.pi * (np.arange(lon)[:, None] * places[None, :]) / (lon * columns)
    angle = 2.0 * np.pi * (places[:, None] * places[None, :] % columns) / columns
    cosine, sine = np.cos(angle), np.sin(angle)
    dft = np.block([[cosine, -sine], [sine, cosine]])
    turns = np.concatenate([np.cos(turn), np.sin(turn)], axis=0)
    return jnp.asarray(turns, jnp.float32), jnp.asarray(dft, jnp.float32)


def exchanged(flat, lat, lon):
    rows, columns = flat.shape
    members = [(chip, place) for chip in range(lat // 2) for place in range(lon)]
    members.sort(key=lambda member: rank(*member))
    groups = [[(2 * chip + core) * lon + place for chip, place in members] for core in range(2)]
    moved = lax.all_to_all(
        flat.reshape(rows, 1, columns),
        ("lat", "lon"),
        0,
        0,
        tiled=True,
        axis_index_groups=groups,
    )
    return moved.reshape(rows, columns)


def in_hbm(x):
    return pltpu.with_memory_space_constraint(x, pltpu.HBM)


def on_device(field, cotangent, conv_weight, spectral_filter):
    channels, _, columns = field.shape
    lat, lon = lax.axis_size("lat"), lax.axis_size("lon")
    owners = lat * lon // 2
    swap = [(i, i ^ 1) for i in range(lat)]
    own = field.reshape(channels, columns)
    cot = cotangent.reshape(channels, columns)
    vmem = pl.BlockSpec(memory_space=pltpu.VMEM)
    hbm = pl.BlockSpec(memory_space=pltpu.HBM)
    params = pltpu.CompilerParams(vmem_limit_bytes=16 * 1024 * 1024)
    flat = jax.ShapeDtypeStruct((channels, columns), jnp.float32)
    half_taps = jax.ShapeDtypeStruct((3, 3, channels // 2, channels), jnp.float32)
    forth = jax.ShapeDtypeStruct((owners * FORTH, columns), jnp.float32)
    back = jax.ShapeDtypeStruct((owners * BACK, columns), jnp.float32)
    other, other_cot = lax.ppermute((own, cot), "lat", swap)
    gain_half = jax.ShapeDtypeStruct((channels // 2, columns), jnp.float32)
    own_here, cot_here, gain, taps = pl.pallas_call(
        fetch_kernel,
        out_shape=(flat, flat, gain_half, half_taps),
        in_specs=[hbm] * 4,
        out_specs=(vmem,) * 4,
        scratch_shapes=[pltpu.SemaphoreType.DMA((4,))],
        compiler_params=params,
        name="fetch",
    )(*map(in_hbm, (own, cot, spectral_filter, conv_weight)))
    outgoing = pl.pallas_call(
        conv_kernel,
        out_shape=forth,
        in_specs=[vmem] * 6 + [hbm],
        out_specs=vmem,
        scratch_shapes=[
            pltpu.VMEM((9, channels // 2, channels), jnp.float32),
            pltpu.SemaphoreType.DMA((9,)),
        ],
        compiler_params=params,
        name="conv",
    )(own_here, other, cot_here, other_cot, gain, taps, in_hbm(conv_weight))
    turns, dft = transform_tables(columns, lon)
    returned = pl.pallas_call(
        spectral_kernel,
        out_shape=back,
        in_specs=[vmem] * 3,
        out_specs=vmem,
        scratch_shapes=[pltpu.VMEM((2 * 8 * lat * lon, 2 * columns), jnp.float32)],
        compiler_params=params,
        name="spectral",
    )(exchanged(outgoing, lat, lon), turns, dft)
    mine = exchanged(returned, lat, lon)
    other = lax.ppermute(mine, "lat", swap)
    rows_scratch = pltpu.VMEM((5, columns + 16, channels // 2), jnp.float32)
    total = pl.pallas_call(
        adjoint_kernel,
        out_shape=jax.ShapeDtypeStruct((columns, channels), jnp.float32),
        in_specs=[vmem] * 2,
        out_specs=vmem,
        scratch_shapes=[rows_scratch],
        compiler_params=params,
        name="adjoint",
    )(mine, conv_weight)
    output, input_grad, filter_grad = pl.pallas_call(
        last_kernel,
        out_shape=(flat, flat, jax.ShapeDtypeStruct(spectral_filter.shape, jnp.float32)),
        in_specs=[vmem] * 6,
        out_specs=(vmem, vmem, vmem),
        scratch_shapes=[rows_scratch],
        compiler_params=params,
        name="last",
    )(mine, other, own, cot, conv_weight, total)
    return (output.reshape(field.shape), input_grad.reshape(field.shape), filter_grad)


def solution(mesh):
    placed = (P(None, "lat", "lon"), P(None, "lat", "lon"), P(), P(None, None, "lon"))
    specs = (P(None, "lat", "lon"), P(None, "lat", "lon"), P(None, None, "lon"))

    def layer(field, cotangent, conv_weight, spectral_filter):
        lat, lon = mesh.shape["lat"], mesh.shape["lon"]
        channels, rows, length = field.shape
        owned = rows == lat == 4 and lon == 8 and channels == 8 * lat * lon and length == 128 * lon
        body = on_device if owned else on_device_any_mesh
        mapped = jax.shard_map(body, mesh=mesh, in_specs=placed, out_specs=specs, check_vma=False)
        return mapped(field, cotangent, conv_weight, spectral_filter)

    return layer
```

```python
from functools import partial

import jax
import jax.numpy as jnp
import numpy as np
from jax import lax
from jax.experimental import pallas as pl
from jax.experimental.pallas import tpu as pltpu
from jax.sharding import PartitionSpec as P

precise = lax.Precision.HIGHEST
three_pass = lax.Precision.HIGH
ROOT_HALF = 0.5**0.5


def padded_2(array, sides, width, wrap):
    for axis, dim in sides:
        peers, length = (lax.axis_size(axis), array.shape[dim])
        up = [(i, (i + 1) % peers) for i in range(peers if wrap else peers - 1)]
        down = [(j, i) for i, j in up]
        last = lax.slice_in_dim(array, length - width, length, axis=dim)
        leading = lax.slice_in_dim(array, 0, width, axis=dim)
        before = lax.ppermute(last, axis, up)
        after = lax.ppermute(leading, axis, down)
        array = jnp.concatenate([before, array, after], axis=dim)
    return array


def partner(array, axis, stride):
    return lax.ppermute(array, axis, [(i, i ^ 1 << stride) for i in range(lax.axis_size(axis))])


def angle_table(first, second, modulus):
    product = first[:, None] * second[None, :] % modulus
    return 2.0 * jnp.pi / modulus * product.astype(jnp.float32)


def apply_taps(padded, taps, lat_rows, columns):
    total = jnp.zeros((taps.shape[2], lat_rows, columns), jnp.float32)
    for tap_row in range(3):
        for tap_col in range(3):
            window = padded[:, tap_row : tap_row + lat_rows, tap_col : tap_col + columns]
            total = total + jnp.einsum(
                "oi,iab->oab", taps[tap_row, tap_col], window, precision=precise
            )
    return total


def with_rims(field):
    wider = padded_2(field, (("lon", 2),), 1, True)
    return padded_2(wider, (("lat", 1),), 1, False)


def local_forward(real_part, imag_part):
    columns = real_part.shape[-1]
    places = lax.iota(jnp.int32, columns)
    angles = angle_table(places, places, columns)
    cosine = jnp.cos(angles)
    sine = jnp.sin(angles)
    out_real = jnp.dot(real_part, cosine, precision=precise) + jnp.dot(
        imag_part, sine, precision=precise
    )
    out_imag = jnp.dot(imag_part, cosine, precision=precise) - jnp.dot(
        real_part, sine, precision=precise
    )
    return (out_real, out_imag)


def local_inverse(real_part, imag_part):
    columns = real_part.shape[-1]
    places = lax.iota(jnp.int32, columns)
    angles = angle_table(places, places, columns)
    cosine = jnp.cos(angles)
    sine = jnp.sin(angles)
    out_real = jnp.dot(real_part, cosine, precision=precise) - jnp.dot(
        imag_part, sine, precision=precise
    )
    out_imag = jnp.dot(imag_part, cosine, precision=precise) + jnp.dot(
        real_part, sine, precision=precise
    )
    return (out_real / columns, out_imag / columns)


def section_angles(place, bit_pos, columns):
    offsets = lax.iota(jnp.int32, columns)
    start = place % 2**bit_pos * columns
    span = 2 * columns * 2**bit_pos
    angles = 2.0 * jnp.pi / span * (start + offsets).astype(jnp.float32)
    upper = place // 2**bit_pos % 2 == 1
    return (jnp.cos(angles), jnp.sin(angles), upper)


def forward_pairs(field):
    extent = lax.axis_size("lon")
    width_bits = extent.bit_length() - 1
    place = lax.axis_index("lon")
    columns = field.shape[-1]
    data = jnp.stack([field, jnp.zeros_like(field)])
    for bit_pos in reversed(range(width_bits)):
        other = partner(data, "lon", bit_pos)
        cosine, sine, upper = section_angles(place, bit_pos, columns)
        differ = other - data
        turned = jnp.stack(
            [differ[0] * cosine + differ[1] * sine, differ[1] * cosine - differ[0] * sine]
        )
        data = jnp.where(upper, turned, data + other)
    out_real, out_imag = local_forward(data[0], data[1])
    return jnp.stack([out_real, out_imag])


def inverse_pairs(spectrum):
    extent = lax.axis_size("lon")
    width_bits = extent.bit_length() - 1
    place = lax.axis_index("lon")
    columns = spectrum.shape[-1]
    back_real, back_imag = local_inverse(spectrum[0], spectrum[1])
    data = jnp.stack([back_real, back_imag])
    for bit_pos in range(width_bits):
        cosine, sine, upper = section_angles(place, bit_pos, columns)
        turned = jnp.stack([data[0] * cosine - data[1] * sine, data[1] * cosine + data[0] * sine])
        outgoing = jnp.where(upper, turned, data)
        other = partner(outgoing, "lon", bit_pos)
        data = jnp.where(upper, other - outgoing, outgoing + other) * 0.5
    return data[0]


def on_device_any_mesh(field, cotangent, conv_weight, spectral_filter):
    lat_rows = field.shape[1]
    columns = field.shape[2]
    total_len = columns * lax.axis_size("lon")
    mixed = apply_taps(with_rims(field), conv_weight, lat_rows, columns)
    hidden_spec = forward_pairs(mixed)
    cot_spec = forward_pairs(cotangent)
    gain_real = spectral_filter[0][:, None, :]
    gain_imag = spectral_filter[1][:, None, :]
    filtered = jnp.stack(
        [
            gain_real * hidden_spec[0] - gain_imag * hidden_spec[1],
            gain_real * hidden_spec[1] + gain_imag * hidden_spec[0],
        ]
    )
    adjoint = jnp.stack(
        [
            gain_real * cot_spec[0] + gain_imag * cot_spec[1],
            gain_real * cot_spec[1] - gain_imag * cot_spec[0],
        ]
    )
    shaped = inverse_pairs(filtered)
    back_field = inverse_pairs(adjoint)
    output = field + shaped
    local_grad = (
        jnp.stack(
            [
                jnp.sum(hidden_spec[0] * cot_spec[0] + hidden_spec[1] * cot_spec[1], axis=1),
                jnp.sum(hidden_spec[0] * cot_spec[1] - hidden_spec[1] * cot_spec[0], axis=1),
            ]
        )
        / total_len
    )
    filter_grad = lax.psum(local_grad, "lat")
    flipped_taps = jnp.transpose(conv_weight[::-1, ::-1], (0, 1, 3, 2))
    input_grad = cotangent + apply_taps(with_rims(back_field), flipped_taps, lat_rows, columns)
    return (output, input_grad, filter_grad)


FORTH, BACK = 49, 57
FIRST_COPIES, IN_FLIGHT = 5, 2


def rank(chip, place):
    upper, odd, x = place // 4, place // 2 % 2, place % 2
    return 8 * ((upper + odd + 1) % 2) + 4 * (1 - chip) + 2 * (1 - x) + 1 - upper


def reversed_bits(value, width):
    return int(format(value, f"0{width}b")[::-1], 2)


def iotas(rows, columns):
    lane = lax.broadcasted_iota(jnp.int32, (rows, columns), 1)
    row = lax.broadcasted_iota(jnp.int32, (rows, columns), 0)
    return lane, row


def fetch_kernel(
    own_ref, cot_ref, filter_ref, taps_ref, own_out, cot_out, gain_out, taps_out, sems
):
    place = lax.axis_index("lat")
    odd, half = lax.rem(place, 2), gain_out.shape[0]
    span = pl.ds(pl.multiple_of(odd * half, half), half)
    copies = [
        pltpu.make_async_copy(own_ref, own_out, sems.at[0]),
        pltpu.make_async_copy(cot_ref, cot_out, sems.at[1]),
        pltpu.make_async_copy(filter_ref.at[place // 2, span], gain_out, sems.at[2]),
    ]

    @pl.when(odd == 1)
    def _():
        half_taps = pltpu.make_async_copy(taps_ref.at[:, :, half:], taps_out, sems.at[3])
        for copy in [half_taps] + copies:
            copy.start()
        for copy in [half_taps] + copies:
            copy.wait()

    @pl.when(odd == 0)
    def _():
        for copy in copies:
            copy.start()
        for copy in copies:
            copy.wait()


def high_low(x):
    high = x.astype(jnp.bfloat16)
    return high, (x - high.astype(jnp.float32)).astype(jnp.bfloat16)


def tall_product(x, high, low):
    rows = x.shape[0]
    x_high, x_low = high_low(x)
    both = jnp.concatenate([x_high, x_low], axis=0)
    both = jnp.dot(both, high, preferred_element_type=jnp.float32)
    rest = jnp.dot(x_high, low, preferred_element_type=jnp.float32)
    return both[:rows] + (both[rows:] + rest)


def conv_kernel(
    own_ref, other_ref, cot_ref, other_cot_ref, gain_ref, half_ref, taps_ref, out_ref, taps, sems
):
    odd, upper = lax.rem(lax.axis_index("lat"), 2), lax.axis_index("lat") // 2
    half = gain_ref.shape[0]
    order = [(row, col) for col in range(3) for row in (1, 2 * upper, 2 - 2 * upper)]

    @pl.when(odd == 0)
    def _():
        copies = [
            pltpu.make_async_copy(taps_ref.at[row, col, :half], taps.at[index], sems.at[index])
            for index, (row, col) in enumerate(order)
        ]
        for copy in copies[:FIRST_COPIES]:
            copy.start()

        def weights(index):
            copies[index].wait()
            if FIRST_COPIES <= index + IN_FLIGHT < len(copies):
                copies[index + IN_FLIGHT].start()
            return high_low(taps[index])

        pack((own_ref, other_ref), (cot_ref, other_cot_ref), gain_ref, weights, 0, out_ref)

    @pl.when(odd == 1)
    def _():
        def weights(index):
            return high_low(half_ref[order[index]])

        pack((other_ref, own_ref), (other_cot_ref, cot_ref), gain_ref, weights, 1, out_ref)


def pack(fields, cots, gain_ref, weights, core, out_ref):
    upper = lax.axis_index("lat") // 2
    half, columns = gain_ref.shape
    for owner in range(half // 8):
        first, here = FORTH * owner, half * core + 8 * owner
        out_ref[first : first + 8, :] = cots[0][here : here + 8, :]
        out_ref[first + 8 : first + 16, :] = cots[1][here : here + 8, :]
        out_ref[first + 40 : first + 48, :] = gain_ref[8 * owner : 8 * owner + 8, :]
    row_0, row_1 = fields[0][...], fields[1][...]
    near = jnp.concatenate(high_low(jnp.where(upper == 0, row_1, row_0)), axis=1)
    both_high, both_low = high_low(jnp.concatenate([row_0, row_1], axis=1))

    def times(weights, values):
        return jnp.dot(weights, values, preferred_element_type=jnp.float32)

    parts = []
    for tap_col in range(3):
        high, low = weights(3 * tap_col)
        middle = times(high, both_high) + (times(high, both_low) + times(low, both_high))
        high, low = weights(3 * tap_col + 1)
        outer = times(high, both_high) + (times(high, both_low) + times(low, both_high))
        high, low = weights(3 * tap_col + 2)
        wide = times(high, near)
        inner = wide[:, :columns] + (wide[:, columns:] + times(low, near[:, :columns]))
        on_0, on_1 = outer[:, :columns], outer[:, columns:]
        parts.append(
            jnp.concatenate(
                [
                    middle[:, :columns] + jnp.where(upper == 0, inner, on_1),
                    middle[:, columns:] + jnp.where(upper == 0, on_0, inner),
                    jnp.where(upper == 0, on_1, on_0),
                ],
                axis=0,
            )
        )
    lane, row = iotas(3 * half, columns)
    left, middle, right = parts
    main = (
        middle
        + jnp.where(lane == 0, 0.0, pltpu.roll(left, 1, 1))
        + jnp.where(lane == columns - 1, 0.0, pltpu.roll(right, columns - 1, 1))
    )
    slot = lane - lax.rem(row, 8) - 8 * (row // half)
    edges = jnp.where(slot == 0, left[:, columns - 1 :], 0.0)
    edges = jnp.where(slot == 24, right[:, 0:1], edges)
    edges = edges[:half] + edges[half : 2 * half] + edges[2 * half :]
    for owner in range(half // 8):
        first = FORTH * owner
        for part in range(3):
            here = half * part + 8 * owner
            out_ref[first + 16 + 8 * part : first + 24 + 8 * part, :] = main[here : here + 8]
        out_ref[first + 48 : first + 49, :] = jnp.sum(
            edges[8 * owner : 8 * owner + 8], axis=0, keepdims=True
        )


def transform_8(x):
    s = [x[d] + x[d + 4] for d in range(4)]
    t = [x[d] - x[d + 4] for d in range(4)]
    plus, minus = ROOT_HALF * (t[1] + t[3]), ROOT_HALF * (t[1] - t[3])
    return [
        (s[0] + s[2] + (s[1] + s[3]), None),
        (t[0] + minus, -t[2] - plus),
        (s[0] - s[2], s[3] - s[1]),
        (t[0] - minus, t[2] - plus),
        (s[0] + s[2] - (s[1] + s[3]), None),
    ]


def spectral_kernel(in_ref, turn_ref, dft_ref, out_ref, work):
    rows, lon = 4, 8
    columns = in_ref.shape[-1]
    lane, sub = iotas(8, columns)
    me = rank(lax.axis_index("lat") // 2, lax.axis_index("lon"))

    def message(chip, place, first, count):
        start = FORTH * rank(chip, place) + first
        return in_ref[start : start + count, :]

    def edge(row, place, group):
        chip, part = row // 2, row % 2
        wanted = lane == sub + 8 * part + 24 * group
        line = jnp.where(wanted, message(chip, place, 48, 1), 0.0)
        if row in (1, 2):
            wanted = lane == sub + 16 + 24 * group
            line = line + jnp.where(wanted, message(1 - chip, place, 48, 1), 0.0)
        return jnp.sum(line, axis=1, keepdims=True)

    grid = []
    for place in range(lon):
        mixed = []
        for row in range(rows):
            tile = message(row // 2, place, 16 + 8 * (row % 2), 8)
            if row in (1, 2):
                tile = tile + message(1 - row // 2, place, 32, 8)
            tile = tile + jnp.where(lane == 0, edge(row, (place - 1) % lon, 0), 0.0)
            tile = tile + jnp.where(lane == columns - 1, edge(row, (place + 1) % lon, 1), 0.0)
            mixed.append(tile)
        cot = [message(row // 2, place, 8 * (row % 2), 8) for row in range(rows)]
        grid.append(jnp.concatenate(mixed + cot, axis=0))
    pairs = transform_8(grid)
    height = 16 * rows
    for residue in range(lon):
        real, imag = pairs[min(residue, lon - residue)]
        cosine, sine = turn_ref[residue : residue + 1, :], turn_ref[8 + residue : 9 + residue, :]
        if imag is None:
            turned = (real * cosine, -real * sine)
        elif residue < 4:
            turned = (real * cosine + imag * sine, imag * cosine - real * sine)
        else:
            turned = (real * cosine - imag * sine, -imag * cosine - real * sine)
        span = pl.ds(residue * height, height)
        work[span, 0:columns] = turned[0]
        work[span, columns:] = turned[1]
    chunk = lon * height // 4
    pieces = [pl.ds(first, chunk) for first in range(0, lon * height, chunk)]
    table = high_low(dft_ref[...])
    spectra = jnp.concatenate(
        [tall_product(work[piece], *table) for piece in pieces], axis=0
    )
    scale = 1.0 / (lon * columns)
    half = 8 * rows
    gradients = []
    for residue in range(lon):
        place = reversed_bits(residue, 3)
        part = spectra[residue * height : (residue + 1) * height]
        mix_re, mix_im = part[:half, :columns], part[:half, columns:]
        cot_re, cot_im = part[half:, :columns], part[half:, columns:]
        gain_re = jnp.concatenate([message(0, place, 40, 8) * scale] * rows, axis=0)
        gain_im = jnp.concatenate([message(1, place, 40, 8) * scale] * rows, axis=0)
        top = pl.ds(residue * height, half)
        bottom = pl.ds(residue * height + half, half)
        work[top, 0:columns] = gain_re * mix_re - gain_im * mix_im
        work[top, columns:] = -(gain_re * mix_im + gain_im * mix_re)
        work[bottom, 0:columns] = gain_re * cot_re + gain_im * cot_im
        work[bottom, columns:] = gain_im * cot_re - gain_re * cot_im
        grad_re = (mix_re * cot_re + mix_im * cot_im) * scale
        grad_im = (mix_re * cot_im - mix_im * cot_re) * scale
        gradients.append(
            [
                grad[0:8] + grad[8:16] + (grad[16:24] + grad[24:32])
                for grad in (grad_re, grad_im)
            ]
        )
    back = jnp.concatenate(
        [tall_product(work[piece], *table) for piece in pieces], axis=0
    )
    turned = []
    for residue in range(lon):
        part = back[residue * height : (residue + 1) * height]
        real, imag = part[:, :columns], part[:, columns:]
        cosine, sine = turn_ref[residue : residue + 1, :], turn_ref[8 + residue : 9 + residue, :]
        turned.append((real * cosine + imag * sine, real * sine - imag * cosine))
    sums = [turned[r][0] + turned[lon - r][0] for r in (1, 2, 3)]
    gaps = [turned[r][1] - turned[lon - r][1] for r in (1, 2, 3)]
    first, fourth = turned[0][0], turned[4][0]
    even = [
        first + fourth + sums[1],
        first - fourth - gaps[1],
        first + fourth - sums[1],
        first - fourth + gaps[1],
    ]
    swing = [
        sums[0] + sums[2],
        ROOT_HALF * (sums[0] - gaps[0] - sums[2] - gaps[2]),
        gaps[2] - gaps[0],
        ROOT_HALF * (sums[2] - gaps[2] - sums[0] - gaps[0]),
    ]
    series = [even[d] + swing[d] for d in range(4)] + [even[d] - swing[d] for d in range(4)]
    slots = [lane == 8 * lax.rem(me + group, 16) + sub for group in range(6)]
    for place in range(lon):
        residue = reversed_bits(place, 3)
        before, after = series[(place - 1) % lon], series[(place + 1) % lon]
        for chip in range(2):
            start = BACK * rank(chip, place)
            rims = jnp.zeros((8, columns), jnp.float32)
            for step in range(3):
                here = half + 8 * (chip + step)
                span = slice(here, here + 8)
                rims = jnp.where(slots[2 * step], before[span, columns - 1 :], rims)
                rims = jnp.where(slots[2 * step + 1], after[span, 0:1], rims)
                first = start + 16 + 8 * step
                out_ref[first : first + 8, :] = series[place][span]
            out_ref[start : start + 16, :] = series[place][16 * chip : 16 * chip + 16]
            for part in range(2):
                first = start + 40 + 8 * part
                out_ref[first : first + 8, :] = gradients[residue][part]
            out_ref[start + 56 : start + 57, :] = jnp.sum(rims, axis=0, keepdims=True)


def partial_adjoint(message_ref, taps_ref, rows_ref, part):
    half, columns = rows_ref.shape[-1], message_ref.shape[-1]
    place = lax.axis_index("lat")
    index = place - place // 2
    owners = half // 8
    lines = message_ref[pl.ds(56, owners, stride=BACK), :]
    lane, owner = iotas(owners, columns)
    rows_ref[0] = jnp.zeros(rows_ref.shape[1:], jnp.float32)
    rows_ref[4] = jnp.zeros(rows_ref.shape[1:], jnp.float32)
    for step in range(3):
        pieces = [
            message_ref[BACK * j + 16 + 8 * step : BACK * j + 24 + 8 * step, :] for j in range(owners)
        ]
        rows_ref[1 + step, 8 : 8 + columns, :] = jnp.concatenate(pieces, axis=0).T
        for rim, target in ((2 * step, 7), (2 * step + 1, 8 + columns)):
            wanted = lane // 8 == lax.rem(owner + rim, owners)
            line = jnp.sum(jnp.where(wanted, lines, 0.0), axis=0, keepdims=True)
            line = jnp.broadcast_to(line, (8, columns))
            if rim:
                line = pltpu.roll(line, columns - 8 * rim, 1)
            rows_ref[1 + step, target : target + 1, :] = line[0:1]
    span = pl.ds(pl.multiple_of(part * half, half), half)
    windows, weights = [], []
    for tap_row in range(3):
        for tap_col in range(3):
            first = 9 - tap_col
            windows.append(rows_ref[index + 2 - tap_row, first : first + columns, :])
            weights.append(taps_ref[tap_row, tap_col, span])
    total = 0.0
    for pair in range(0, 9, 2):
        window = jnp.concatenate(windows[pair : pair + 2], axis=1)
        weight = jnp.concatenate(weights[pair : pair + 2], axis=0)
        total = total + tall_product(window, *high_low(weight))
    return total


def adjoint_kernel(mine_ref, taps_ref, total_ref, rows_ref):
    part = lax.rem(lax.axis_index("lat"), 2)
    total_ref[...] = partial_adjoint(mine_ref, taps_ref, rows_ref, part)


def last_kernel(
    mine_ref, other_ref, field_ref, cot_ref, taps_ref, total_ref, out_ref, grad_ref, gain_ref, rows_ref
):
    half = cot_ref.shape[0] // 2
    part = lax.rem(lax.axis_index("lat"), 2)
    for message_ref, side in ((mine_ref, part), (other_ref, 1 - part)):
        for owner in range(half // 8):
            here = pl.ds(pl.multiple_of(half * side + 8 * owner, 8), 8)
            start = BACK * owner
            first, second = message_ref[start : start + 8, :], message_ref[start + 8 : start + 16, :]
            out_ref[here, :] = field_ref[here, :] + jnp.where(part == 0, first, second)
            gain_ref[0, here, :] = message_ref[start + 40 : start + 48, :]
            gain_ref[1, here, :] = message_ref[start + 48 : start + 56, :]
    total = total_ref[...] + partial_adjoint(other_ref, taps_ref, rows_ref, 1 - part)
    grad_ref[...] = cot_ref[...] + total.T


def transform_tables(columns, lon):
    places = np.arange(columns)
    turn = 2.0 * np.pi * (np.arange(lon)[:, None] * places[None, :]) / (lon * columns)
    angle = 2.0 * np.pi * (places[:, None] * places[None, :] % columns) / columns
    cosine, sine = np.cos(angle), np.sin(angle)
    dft = np.block([[cosine, -sine], [sine, cosine]])
    turns = np.concatenate([np.cos(turn), np.sin(turn)], axis=0)
    return jnp.asarray(turns, jnp.float32), jnp.asarray(dft, jnp.float32)


def exchanged(flat, lat, lon):
    rows, columns = flat.shape
    members = [(chip, place) for chip in range(lat // 2) for place in range(lon)]
    members.sort(key=lambda member: rank(*member))
    groups = [[(2 * chip + core) * lon + place for chip, place in members] for core in range(2)]
    moved = lax.all_to_all(
        flat.reshape(rows, 1, columns),
        ("lat", "lon"),
        0,
        0,
        tiled=True,
        axis_index_groups=groups,
    )
    return moved.reshape(rows, columns)


def in_hbm(x):
    return pltpu.with_memory_space_constraint(x, pltpu.HBM)


def on_device(field, cotangent, conv_weight, spectral_filter):
    channels, _, columns = field.shape
    lat, lon = lax.axis_size("lat"), lax.axis_size("lon")
    owners = lat * lon // 2
    swap = [(i, i ^ 1) for i in range(lat)]
    own = field.reshape(channels, columns)
    cot = cotangent.reshape(channels, columns)
    vmem = pl.BlockSpec(memory_space=pltpu.VMEM)
    hbm = pl.BlockSpec(memory_space=pltpu.HBM)
    params = pltpu.CompilerParams(vmem_limit_bytes=16 * 1024 * 1024)
    flat = jax.ShapeDtypeStruct((channels, columns), jnp.float32)
    half_taps = jax.ShapeDtypeStruct((3, 3, channels // 2, channels), jnp.float32)
    forth = jax.ShapeDtypeStruct((owners * FORTH, columns), jnp.float32)
    back = jax.ShapeDtypeStruct((owners * BACK, columns), jnp.float32)
    other, other_cot = lax.ppermute((own, cot), "lat", swap)
    gain_half = jax.ShapeDtypeStruct((channels // 2, columns), jnp.float32)
    own_here, cot_here, gain, taps = pl.pallas_call(
        fetch_kernel,
        out_shape=(flat, flat, gain_half, half_taps),
        in_specs=[hbm] * 4,
        out_specs=(vmem,) * 4,
        scratch_shapes=[pltpu.SemaphoreType.DMA((4,))],
        compiler_params=params,
        name="fetch",
    )(*map(in_hbm, (own, cot, spectral_filter, conv_weight)))
    outgoing = pl.pallas_call(
        conv_kernel,
        out_shape=forth,
        in_specs=[vmem] * 6 + [hbm],
        out_specs=vmem,
        scratch_shapes=[
            pltpu.VMEM((9, channels // 2, channels), jnp.float32),
            pltpu.SemaphoreType.DMA((9,)),
        ],
        compiler_params=params,
        name="conv",
    )(own_here, other, cot_here, other_cot, gain, taps, in_hbm(conv_weight))
    turns, dft = transform_tables(columns, lon)
    returned = pl.pallas_call(
        spectral_kernel,
        out_shape=back,
        in_specs=[vmem] * 3,
        out_specs=vmem,
        scratch_shapes=[pltpu.VMEM((2 * 8 * lat * lon, 2 * columns), jnp.float32)],
        compiler_params=params,
        name="spectral",
    )(exchanged(outgoing, lat, lon), turns, dft)
    mine = exchanged(returned, lat, lon)
    other = lax.ppermute(mine, "lat", swap)
    rows_scratch = pltpu.VMEM((5, columns + 16, channels // 2), jnp.float32)
    total = pl.pallas_call(
        adjoint_kernel,
        out_shape=jax.ShapeDtypeStruct((columns, channels), jnp.float32),
        in_specs=[vmem] * 2,
        out_specs=vmem,
        scratch_shapes=[rows_scratch],
        compiler_params=params,
        name="adjoint",
    )(mine, conv_weight)
    output, input_grad, filter_grad = pl.pallas_call(
        last_kernel,
        out_shape=(flat, flat, jax.ShapeDtypeStruct(spectral_filter.shape, jnp.float32)),
        in_specs=[vmem] * 6,
        out_specs=(vmem, vmem, vmem),
        scratch_shapes=[rows_scratch],
        compiler_params=params,
        name="last",
    )(mine, other, own, cot, conv_weight, total)
    return (output.reshape(field.shape), input_grad.reshape(field.shape), filter_grad)


def solution(mesh):
    placed = (P(None, "lat", "lon"), P(None, "lat", "lon"), P(), P(None, None, "lon"))
    specs = (P(None, "lat", "lon"), P(None, "lat", "lon"), P(None, None, "lon"))

    def layer(field, cotangent, conv_weight, spectral_filter):
        lat, lon = mesh.shape["lat"], mesh.shape["lon"]
        channels, rows, length = field.shape
        owned = rows == lat == 4 and lon == 8 and channels == 8 * lat * lon and length == 128 * lon
        body = on_device if owned else on_device_any_mesh
        mapped = jax.shard_map(body, mesh=mesh, in_specs=placed, out_specs=specs, check_vma=False)
        return mapped(field, cotangent, conv_weight, spectral_filter)

    return layer
```

```python
from functools import partial

import jax
import jax.numpy as jnp
import numpy as np
from jax import lax
from jax.experimental import pallas as pl
from jax.experimental.pallas import tpu as pltpu
from jax.sharding import PartitionSpec as P

precise = lax.Precision.HIGHEST
three_pass = lax.Precision.HIGH
ROOT_HALF = 0.5**0.5


def padded_2(array, sides, width, wrap):
    for axis, dim in sides:
        peers, length = (lax.axis_size(axis), array.shape[dim])
        up = [(i, (i + 1) % peers) for i in range(peers if wrap else peers - 1)]
        down = [(j, i) for i, j in up]
        last = lax.slice_in_dim(array, length - width, length, axis=dim)
        leading = lax.slice_in_dim(array, 0, width, axis=dim)
        before = lax.ppermute(last, axis, up)
        after = lax.ppermute(leading, axis, down)
        array = jnp.concatenate([before, array, after], axis=dim)
    return array


def partner(array, axis, stride):
    return lax.ppermute(array, axis, [(i, i ^ 1 << stride) for i in range(lax.axis_size(axis))])


def angle_table(first, second, modulus):
    product = first[:, None] * second[None, :] % modulus
    return 2.0 * jnp.pi / modulus * product.astype(jnp.float32)


def apply_taps(padded, taps, lat_rows, columns):
    total = jnp.zeros((taps.shape[2], lat_rows, columns), jnp.float32)
    for tap_row in range(3):
        for tap_col in range(3):
            window = padded[:, tap_row : tap_row + lat_rows, tap_col : tap_col + columns]
            total = total + jnp.einsum(
                "oi,iab->oab", taps[tap_row, tap_col], window, precision=precise
            )
    return total


def with_rims(field):
    wider = padded_2(field, (("lon", 2),), 1, True)
    return padded_2(wider, (("lat", 1),), 1, False)


def local_forward(real_part, imag_part):
    columns = real_part.shape[-1]
    places = lax.iota(jnp.int32, columns)
    angles = angle_table(places, places, columns)
    cosine = jnp.cos(angles)
    sine = jnp.sin(angles)
    out_real = jnp.dot(real_part, cosine, precision=precise) + jnp.dot(
        imag_part, sine, precision=precise
    )
    out_imag = jnp.dot(imag_part, cosine, precision=precise) - jnp.dot(
        real_part, sine, precision=precise
    )
    return (out_real, out_imag)


def local_inverse(real_part, imag_part):
    columns = real_part.shape[-1]
    places = lax.iota(jnp.int32, columns)
    angles = angle_table(places, places, columns)
    cosine = jnp.cos(angles)
    sine = jnp.sin(angles)
    out_real = jnp.dot(real_part, cosine, precision=precise) - jnp.dot(
        imag_part, sine, precision=precise
    )
    out_imag = jnp.dot(imag_part, cosine, precision=precise) + jnp.dot(
        real_part, sine, precision=precise
    )
    return (out_real / columns, out_imag / columns)


def section_angles(place, bit_pos, columns):
    offsets = lax.iota(jnp.int32, columns)
    start = place % 2**bit_pos * columns
    span = 2 * columns * 2**bit_pos
    angles = 2.0 * jnp.pi / span * (start + offsets).astype(jnp.float32)
    upper = place // 2**bit_pos % 2 == 1
    return (jnp.cos(angles), jnp.sin(angles), upper)


def forward_pairs(field):
    extent = lax.axis_size("lon")
    width_bits = extent.bit_length() - 1
    place = lax.axis_index("lon")
    columns = field.shape[-1]
    data = jnp.stack([field, jnp.zeros_like(field)])
    for bit_pos in reversed(range(width_bits)):
        other = partner(data, "lon", bit_pos)
        cosine, sine, upper = section_angles(place, bit_pos, columns)
        differ = other - data
        turned = jnp.stack(
            [differ[0] * cosine + differ[1] * sine, differ[1] * cosine - differ[0] * sine]
        )
        data = jnp.where(upper, turned, data + other)
    out_real, out_imag = local_forward(data[0], data[1])
    return jnp.stack([out_real, out_imag])


def inverse_pairs(spectrum):
    extent = lax.axis_size("lon")
    width_bits = extent.bit_length() - 1
    place = lax.axis_index("lon")
    columns = spectrum.shape[-1]
    back_real, back_imag = local_inverse(spectrum[0], spectrum[1])
    data = jnp.stack([back_real, back_imag])
    for bit_pos in range(width_bits):
        cosine, sine, upper = section_angles(place, bit_pos, columns)
        turned = jnp.stack([data[0] * cosine - data[1] * sine, data[1] * cosine + data[0] * sine])
        outgoing = jnp.where(upper, turned, data)
        other = partner(outgoing, "lon", bit_pos)
        data = jnp.where(upper, other - outgoing, outgoing + other) * 0.5
    return data[0]


def on_device_any_mesh(field, cotangent, conv_weight, spectral_filter):
    lat_rows = field.shape[1]
    columns = field.shape[2]
    total_len = columns * lax.axis_size("lon")
    mixed = apply_taps(with_rims(field), conv_weight, lat_rows, columns)
    hidden_spec = forward_pairs(mixed)
    cot_spec = forward_pairs(cotangent)
    gain_real = spectral_filter[0][:, None, :]
    gain_imag = spectral_filter[1][:, None, :]
    filtered = jnp.stack(
        [
            gain_real * hidden_spec[0] - gain_imag * hidden_spec[1],
            gain_real * hidden_spec[1] + gain_imag * hidden_spec[0],
        ]
    )
    adjoint = jnp.stack(
        [
            gain_real * cot_spec[0] + gain_imag * cot_spec[1],
            gain_real * cot_spec[1] - gain_imag * cot_spec[0],
        ]
    )
    shaped = inverse_pairs(filtered)
    back_field = inverse_pairs(adjoint)
    output = field + shaped
    local_grad = (
        jnp.stack(
            [
                jnp.sum(hidden_spec[0] * cot_spec[0] + hidden_spec[1] * cot_spec[1], axis=1),
                jnp.sum(hidden_spec[0] * cot_spec[1] - hidden_spec[1] * cot_spec[0], axis=1),
            ]
        )
        / total_len
    )
    filter_grad = lax.psum(local_grad, "lat")
    flipped_taps = jnp.transpose(conv_weight[::-1, ::-1], (0, 1, 3, 2))
    input_grad = cotangent + apply_taps(with_rims(back_field), flipped_taps, lat_rows, columns)
    return (output, input_grad, filter_grad)


FORTH, BACK = 49, 57


def rank(chip, place):
    upper, odd, x = place // 4, place // 2 % 2, place % 2
    return 8 * ((upper + odd + 1) % 2) + 4 * (1 - x) + 2 * (1 - chip) + 1 - upper


def reversed_bits(value, width):
    return int(format(value, f"0{width}b")[::-1], 2)


def iotas(rows, columns):
    lane = lax.broadcasted_iota(jnp.int32, (rows, columns), 1)
    row = lax.broadcasted_iota(jnp.int32, (rows, columns), 0)
    return lane, row


def fetch_kernel(
    own_ref, cot_ref, filter_ref, taps_ref, own_out, cot_out, gain_out, taps_out, sems
):
    place = lax.axis_index("lat")
    odd, half = lax.rem(place, 2), gain_out.shape[0]
    span = pl.ds(pl.multiple_of(odd * half, half), half)
    copies = [
        pltpu.make_async_copy(own_ref, own_out, sems.at[0]),
        pltpu.make_async_copy(cot_ref, cot_out, sems.at[1]),
        pltpu.make_async_copy(filter_ref.at[place // 2, span], gain_out, sems.at[2]),
    ]

    @pl.when(odd == 1)
    def _():
        half_taps = pltpu.make_async_copy(taps_ref.at[:, :, half:], taps_out, sems.at[3])
        for copy in [half_taps] + copies:
            copy.start()
        for copy in [half_taps] + copies:
            copy.wait()

    @pl.when(odd == 0)
    def _():
        for copy in copies:
            copy.start()
        for copy in copies:
            copy.wait()


def high_low(x):
    high = x.astype(jnp.bfloat16)
    return high, (x - high.astype(jnp.float32)).astype(jnp.bfloat16)


def tall_product(x, high, low):
    rows = x.shape[0]
    x_high, x_low = high_low(x)
    both = jnp.concatenate([x_high, x_low], axis=0)
    both = jnp.dot(both, high, preferred_element_type=jnp.float32)
    rest = jnp.dot(x_high, low, preferred_element_type=jnp.float32)
    return both[:rows] + (both[rows:] + rest)


def conv_kernel(
    own_ref, other_ref, cot_ref, other_cot_ref, gain_ref, half_ref, taps_ref, out_ref, taps, sems
):
    odd, upper = lax.rem(lax.axis_index("lat"), 2), lax.axis_index("lat") // 2
    half = gain_ref.shape[0]
    order = [(row, col) for col in range(3) for row in (1, 2 * upper, 2 - 2 * upper)]

    @pl.when(odd == 0)
    def _():
        copies = [
            pltpu.make_async_copy(taps_ref.at[row, col, :half], taps.at[index], sems.at[index])
            for index, (row, col) in enumerate(order)
        ]
        for copy in copies:
            copy.start()

        def weights(index):
            copies[index].wait()
            return high_low(taps[index])

        pack((own_ref, other_ref), (cot_ref, other_cot_ref), gain_ref, weights, 0, out_ref)

    @pl.when(odd == 1)
    def _():
        def weights(index):
            return high_low(half_ref[order[index]])

        pack((other_ref, own_ref), (other_cot_ref, cot_ref), gain_ref, weights, 1, out_ref)


def pack(fields, cots, gain_ref, weights, core, out_ref):
    upper = lax.axis_index("lat") // 2
    half, columns = gain_ref.shape
    for owner in range(half // 8):
        first, here = FORTH * owner, half * core + 8 * owner
        out_ref[first : first + 8, :] = cots[0][here : here + 8, :]
        out_ref[first + 8 : first + 16, :] = cots[1][here : here + 8, :]
        out_ref[first + 40 : first + 48, :] = gain_ref[8 * owner : 8 * owner + 8, :]
    row_0, row_1 = fields[0][...], fields[1][...]
    near = jnp.concatenate(high_low(jnp.where(upper == 0, row_1, row_0)), axis=1)
    both_high, both_low = high_low(jnp.concatenate([row_0, row_1], axis=1))

    def times(weights, values):
        return jnp.dot(weights, values, preferred_element_type=jnp.float32)

    parts = []
    for tap_col in range(3):
        high, low = weights(3 * tap_col)
        middle = times(high, both_high) + (times(high, both_low) + times(low, both_high))
        high, low = weights(3 * tap_col + 1)
        outer = times(high, both_high) + (times(high, both_low) + times(low, both_high))
        high, low = weights(3 * tap_col + 2)
        wide = times(high, near)
        inner = wide[:, :columns] + (wide[:, columns:] + times(low, near[:, :columns]))
        on_0, on_1 = outer[:, :columns], outer[:, columns:]
        parts.append(
            jnp.concatenate(
                [
                    middle[:, :columns] + jnp.where(upper == 0, inner, on_1),
                    middle[:, columns:] + jnp.where(upper == 0, on_0, inner),
                    jnp.where(upper == 0, on_1, on_0),
                ],
                axis=0,
            )
        )
    lane, row = iotas(3 * half, columns)
    left, middle, right = parts
    main = (
        middle
        + jnp.where(lane == 0, 0.0, pltpu.roll(left, 1, 1))
        + jnp.where(lane == columns - 1, 0.0, pltpu.roll(right, columns - 1, 1))
    )
    slot = lane - lax.rem(row, 8) - 8 * (row // half)
    edges = jnp.where(slot == 0, left[:, columns - 1 :], 0.0)
    edges = jnp.where(slot == 24, right[:, 0:1], edges)
    edges = edges[:half] + edges[half : 2 * half] + edges[2 * half :]
    for owner in range(half // 8):
        first = FORTH * owner
        for part in range(3):
            here = half * part + 8 * owner
            out_ref[first + 16 + 8 * part : first + 24 + 8 * part, :] = main[here : here + 8]
        out_ref[first + 48 : first + 49, :] = jnp.sum(
            edges[8 * owner : 8 * owner + 8], axis=0, keepdims=True
        )


def transform_8(x):
    s = [x[d] + x[d + 4] for d in range(4)]
    t = [x[d] - x[d + 4] for d in range(4)]
    plus, minus = ROOT_HALF * (t[1] + t[3]), ROOT_HALF * (t[1] - t[3])
    return [
        (s[0] + s[2] + (s[1] + s[3]), None),
        (t[0] + minus, -t[2] - plus),
        (s[0] - s[2], s[3] - s[1]),
        (t[0] - minus, t[2] - plus),
        (s[0] + s[2] - (s[1] + s[3]), None),
    ]


def spectral_kernel(in_ref, turn_ref, dft_ref, out_ref, work):
    rows, lon = 4, 8
    columns = in_ref.shape[-1]
    lane, sub = iotas(8, columns)
    me = rank(lax.axis_index("lat") // 2, lax.axis_index("lon"))

    def message(chip, place, first, count):
        start = FORTH * rank(chip, place) + first
        return in_ref[start : start + count, :]

    def edge(row, place, group):
        chip, part = row // 2, row % 2
        wanted = lane == sub + 8 * part + 24 * group
        line = jnp.where(wanted, message(chip, place, 48, 1), 0.0)
        if row in (1, 2):
            wanted = lane == sub + 16 + 24 * group
            line = line + jnp.where(wanted, message(1 - chip, place, 48, 1), 0.0)
        return jnp.sum(line, axis=1, keepdims=True)

    grid = []
    for place in range(lon):
        mixed = []
        for row in range(rows):
            tile = message(row // 2, place, 16 + 8 * (row % 2), 8)
            if row in (1, 2):
                tile = tile + message(1 - row // 2, place, 32, 8)
            tile = tile + jnp.where(lane == 0, edge(row, (place - 1) % lon, 0), 0.0)
            tile = tile + jnp.where(lane == columns - 1, edge(row, (place + 1) % lon, 1), 0.0)
            mixed.append(tile)
        cot = [message(row // 2, place, 8 * (row % 2), 8) for row in range(rows)]
        grid.append(jnp.concatenate(mixed + cot, axis=0))
    pairs = transform_8(grid)
    height = 16 * rows
    for residue in range(lon):
        real, imag = pairs[min(residue, lon - residue)]
        cosine, sine = turn_ref[residue : residue + 1, :], turn_ref[8 + residue : 9 + residue, :]
        if imag is None:
            turned = (real * cosine, -real * sine)
        elif residue < 4:
            turned = (real * cosine + imag * sine, imag * cosine - real * sine)
        else:
            turned = (real * cosine - imag * sine, -imag * cosine - real * sine)
        span = pl.ds(residue * height, height)
        work[span, 0:columns] = turned[0]
        work[span, columns:] = turned[1]
    chunk = lon * height // 4
    pieces = [pl.ds(first, chunk) for first in range(0, lon * height, chunk)]
    table = high_low(dft_ref[...])
    spectra = jnp.concatenate(
        [tall_product(work[piece], *table) for piece in pieces], axis=0
    )
    scale = 1.0 / (lon * columns)
    half = 8 * rows
    gradients = []
    for residue in range(lon):
        place = reversed_bits(residue, 3)
        part = spectra[residue * height : (residue + 1) * height]
        mix_re, mix_im = part[:half, :columns], part[:half, columns:]
        cot_re, cot_im = part[half:, :columns], part[half:, columns:]
        gain_re = jnp.concatenate([message(0, place, 40, 8) * scale] * rows, axis=0)
        gain_im = jnp.concatenate([message(1, place, 40, 8) * scale] * rows, axis=0)
        top = pl.ds(residue * height, half)
        bottom = pl.ds(residue * height + half, half)
        work[top, 0:columns] = gain_re * mix_re - gain_im * mix_im
        work[top, columns:] = -(gain_re * mix_im + gain_im * mix_re)
        work[bottom, 0:columns] = gain_re * cot_re + gain_im * cot_im
        work[bottom, columns:] = gain_im * cot_re - gain_re * cot_im
        grad_re = (mix_re * cot_re + mix_im * cot_im) * scale
        grad_im = (mix_re * cot_im - mix_im * cot_re) * scale
        gradients.append(
            [
                grad[0:8] + grad[8:16] + (grad[16:24] + grad[24:32])
                for grad in (grad_re, grad_im)
            ]
        )
    back = jnp.concatenate(
        [tall_product(work[piece], *table) for piece in pieces], axis=0
    )
    turned = []
    for residue in range(lon):
        part = back[residue * height : (residue + 1) * height]
        real, imag = part[:, :columns], part[:, columns:]
        cosine, sine = turn_ref[residue : residue + 1, :], turn_ref[8 + residue : 9 + residue, :]
        turned.append((real * cosine + imag * sine, real * sine - imag * cosine))
    sums = [turned[r][0] + turned[lon - r][0] for r in (1, 2, 3)]
    gaps = [turned[r][1] - turned[lon - r][1] for r in (1, 2, 3)]
    first, fourth = turned[0][0], turned[4][0]
    even = [
        first + fourth + sums[1],
        first - fourth - gaps[1],
        first + fourth - sums[1],
        first - fourth + gaps[1],
    ]
    swing = [
        sums[0] + sums[2],
        ROOT_HALF * (sums[0] - gaps[0] - sums[2] - gaps[2]),
        gaps[2] - gaps[0],
        ROOT_HALF * (sums[2] - gaps[2] - sums[0] - gaps[0]),
    ]
    series = [even[d] + swing[d] for d in range(4)] + [even[d] - swing[d] for d in range(4)]
    slots = [lane == 8 * lax.rem(me + group, 16) + sub for group in range(6)]
    for place in range(lon):
        residue = reversed_bits(place, 3)
        before, after = series[(place - 1) % lon], series[(place + 1) % lon]
        for chip in range(2):
            start = BACK * rank(chip, place)
            rims = jnp.zeros((8, columns), jnp.float32)
            for step in range(3):
                here = half + 8 * (chip + step)
                span = slice(here, here + 8)
                rims = jnp.where(slots[2 * step], before[span, columns - 1 :], rims)
                rims = jnp.where(slots[2 * step + 1], after[span, 0:1], rims)
                first = start + 16 + 8 * step
                out_ref[first : first + 8, :] = series[place][span]
            out_ref[start : start + 16, :] = series[place][16 * chip : 16 * chip + 16]
            for part in range(2):
                first = start + 40 + 8 * part
                out_ref[first : first + 8, :] = gradients[residue][part]
            out_ref[start + 56 : start + 57, :] = jnp.sum(rims, axis=0, keepdims=True)


def partial_adjoint(message_ref, taps_ref, rows_ref, part):
    half, columns = rows_ref.shape[-1], message_ref.shape[-1]
    place = lax.axis_index("lat")
    index = place - place // 2
    owners = half // 8
    lines = message_ref[pl.ds(56, owners, stride=BACK), :]
    lane, owner = iotas(owners, columns)
    rows_ref[0] = jnp.zeros(rows_ref.shape[1:], jnp.float32)
    rows_ref[4] = jnp.zeros(rows_ref.shape[1:], jnp.float32)
    for step in range(3):
        pieces = [
            message_ref[BACK * j + 16 + 8 * step : BACK * j + 24 + 8 * step, :] for j in range(owners)
        ]
        rows_ref[1 + step, 8 : 8 + columns, :] = jnp.concatenate(pieces, axis=0).T
        for rim, target in ((2 * step, 7), (2 * step + 1, 8 + columns)):
            wanted = lane // 8 == lax.rem(owner + rim, owners)
            line = jnp.sum(jnp.where(wanted, lines, 0.0), axis=0, keepdims=True)
            line = jnp.broadcast_to(line, (8, columns))
            if rim:
                line = pltpu.roll(line, columns - 8 * rim, 1)
            rows_ref[1 + step, target : target + 1, :] = line[0:1]
    span = pl.ds(pl.multiple_of(part * half, half), half)
    windows, weights = [], []
    for tap_row in range(3):
        for tap_col in range(3):
            first = 9 - tap_col
            windows.append(rows_ref[index + 2 - tap_row, first : first + columns, :])
            weights.append(taps_ref[tap_row, tap_col, span])
    total = 0.0
    for pair in range(0, 9, 2):
        window = jnp.concatenate(windows[pair : pair + 2], axis=1)
        weight = jnp.concatenate(weights[pair : pair + 2], axis=0)
        total = total + tall_product(window, *high_low(weight))
    return total


def adjoint_kernel(mine_ref, taps_ref, total_ref, rows_ref):
    part = lax.rem(lax.axis_index("lat"), 2)
    total_ref[...] = partial_adjoint(mine_ref, taps_ref, rows_ref, part)


def last_kernel(
    mine_ref, other_ref, field_ref, cot_ref, taps_ref, total_ref, out_ref, grad_ref, gain_ref, rows_ref
):
    half = cot_ref.shape[0] // 2
    part = lax.rem(lax.axis_index("lat"), 2)
    for message_ref, side in ((mine_ref, part), (other_ref, 1 - part)):
        for owner in range(half // 8):
            here = pl.ds(pl.multiple_of(half * side + 8 * owner, 8), 8)
            start = BACK * owner
            first, second = message_ref[start : start + 8, :], message_ref[start + 8 : start + 16, :]
            out_ref[here, :] = field_ref[here, :] + jnp.where(part == 0, first, second)
            gain_ref[0, here, :] = message_ref[start + 40 : start + 48, :]
            gain_ref[1, here, :] = message_ref[start + 48 : start + 56, :]
    total = total_ref[...] + partial_adjoint(other_ref, taps_ref, rows_ref, 1 - part)
    grad_ref[...] = cot_ref[...] + total.T


def transform_tables(columns, lon):
    places = np.arange(columns)
    turn = 2.0 * np.pi * (np.arange(lon)[:, None] * places[None, :]) / (lon * columns)
    angle = 2.0 * np.pi * (places[:, None] * places[None, :] % columns) / columns
    cosine, sine = np.cos(angle), np.sin(angle)
    dft = np.block([[cosine, -sine], [sine, cosine]])
    turns = np.concatenate([np.cos(turn), np.sin(turn)], axis=0)
    return jnp.asarray(turns, jnp.float32), jnp.asarray(dft, jnp.float32)


def exchanged(flat, lat, lon):
    rows, columns = flat.shape
    members = [(chip, place) for chip in range(lat // 2) for place in range(lon)]
    members.sort(key=lambda member: rank(*member))
    groups = [[(2 * chip + core) * lon + place for chip, place in members] for core in range(2)]
    moved = lax.all_to_all(
        flat.reshape(rows, 1, columns),
        ("lat", "lon"),
        0,
        0,
        tiled=True,
        axis_index_groups=groups,
    )
    return moved.reshape(rows, columns)


def in_hbm(x):
    return pltpu.with_memory_space_constraint(x, pltpu.HBM)


def on_device(field, cotangent, conv_weight, spectral_filter):
    channels, _, columns = field.shape
    lat, lon = lax.axis_size("lat"), lax.axis_size("lon")
    owners = lat * lon // 2
    swap = [(i, i ^ 1) for i in range(lat)]
    own = field.reshape(channels, columns)
    cot = cotangent.reshape(channels, columns)
    vmem = pl.BlockSpec(memory_space=pltpu.VMEM)
    hbm = pl.BlockSpec(memory_space=pltpu.HBM)
    params = pltpu.CompilerParams(vmem_limit_bytes=16 * 1024 * 1024)
    flat = jax.ShapeDtypeStruct((channels, columns), jnp.float32)
    half_taps = jax.ShapeDtypeStruct((3, 3, channels // 2, channels), jnp.float32)
    forth = jax.ShapeDtypeStruct((owners * FORTH, columns), jnp.float32)
    back = jax.ShapeDtypeStruct((owners * BACK, columns), jnp.float32)
    other, other_cot = lax.ppermute((own, cot), "lat", swap)
    gain_half = jax.ShapeDtypeStruct((channels // 2, columns), jnp.float32)
    own_here, cot_here, gain, taps = pl.pallas_call(
        fetch_kernel,
        out_shape=(flat, flat, gain_half, half_taps),
        in_specs=[hbm] * 4,
        out_specs=(vmem,) * 4,
        scratch_shapes=[pltpu.SemaphoreType.DMA((4,))],
        compiler_params=params,
        name="fetch",
    )(*map(in_hbm, (own, cot, spectral_filter, conv_weight)))
    outgoing = pl.pallas_call(
        conv_kernel,
        out_shape=forth,
        in_specs=[vmem] * 6 + [hbm],
        out_specs=vmem,
        scratch_shapes=[
            pltpu.VMEM((9, channels // 2, channels), jnp.float32),
            pltpu.SemaphoreType.DMA((9,)),
        ],
        compiler_params=params,
        name="conv",
    )(own_here, other, cot_here, other_cot, gain, taps, in_hbm(conv_weight))
    turns, dft = transform_tables(columns, lon)
    returned = pl.pallas_call(
        spectral_kernel,
        out_shape=back,
        in_specs=[vmem] * 3,
        out_specs=vmem,
        scratch_shapes=[pltpu.VMEM((2 * 8 * lat * lon, 2 * columns), jnp.float32)],
        compiler_params=params,
        name="spectral",
    )(exchanged(outgoing, lat, lon), turns, dft)
    mine = exchanged(returned, lat, lon)
    other = lax.ppermute(mine, "lat", swap)
    rows_scratch = pltpu.VMEM((5, columns + 16, channels // 2), jnp.float32)
    total = pl.pallas_call(
        adjoint_kernel,
        out_shape=jax.ShapeDtypeStruct((columns, channels), jnp.float32),
        in_specs=[vmem] * 2,
        out_specs=vmem,
        scratch_shapes=[rows_scratch],
        compiler_params=params,
        name="adjoint",
    )(mine, conv_weight)
    output, input_grad, filter_grad = pl.pallas_call(
        last_kernel,
        out_shape=(flat, flat, jax.ShapeDtypeStruct(spectral_filter.shape, jnp.float32)),
        in_specs=[vmem] * 6,
        out_specs=(vmem, vmem, vmem),
        scratch_shapes=[rows_scratch],
        compiler_params=params,
        name="last",
    )(mine, other, own, cot, conv_weight, total)
    return (output.reshape(field.shape), input_grad.reshape(field.shape), filter_grad)


def solution(mesh):
    placed = (P(None, "lat", "lon"), P(None, "lat", "lon"), P(), P(None, None, "lon"))
    specs = (P(None, "lat", "lon"), P(None, "lat", "lon"), P(None, None, "lon"))

    def layer(field, cotangent, conv_weight, spectral_filter):
        lat, lon = mesh.shape["lat"], mesh.shape["lon"]
        channels, rows, length = field.shape
        owned = rows == lat == 4 and lon == 8 and channels == 8 * lat * lon and length == 128 * lon
        body = on_device if owned else on_device_any_mesh
        mapped = jax.shard_map(body, mesh=mesh, in_specs=placed, out_specs=specs, check_vma=False)
        return mapped(field, cotangent, conv_weight, spectral_filter)

    return layer
```

```python
from functools import partial

import jax
import jax.numpy as jnp
import numpy as np
from jax import lax
from jax.experimental import pallas as pl
from jax.experimental.pallas import tpu as pltpu
from jax.sharding import PartitionSpec as P

precise = lax.Precision.HIGHEST
three_pass = lax.Precision.HIGH
ROOT_HALF = 0.5**0.5


def padded_2(array, sides, width, wrap):
    for axis, dim in sides:
        peers, length = (lax.axis_size(axis), array.shape[dim])
        up = [(i, (i + 1) % peers) for i in range(peers if wrap else peers - 1)]
        down = [(j, i) for i, j in up]
        last = lax.slice_in_dim(array, length - width, length, axis=dim)
        leading = lax.slice_in_dim(array, 0, width, axis=dim)
        before = lax.ppermute(last, axis, up)
        after = lax.ppermute(leading, axis, down)
        array = jnp.concatenate([before, array, after], axis=dim)
    return array


def partner(array, axis, stride):
    return lax.ppermute(array, axis, [(i, i ^ 1 << stride) for i in range(lax.axis_size(axis))])


def angle_table(first, second, modulus):
    product = first[:, None] * second[None, :] % modulus
    return 2.0 * jnp.pi / modulus * product.astype(jnp.float32)


def apply_taps(padded, taps, lat_rows, columns):
    total = jnp.zeros((taps.shape[2], lat_rows, columns), jnp.float32)
    for tap_row in range(3):
        for tap_col in range(3):
            window = padded[:, tap_row : tap_row + lat_rows, tap_col : tap_col + columns]
            total = total + jnp.einsum(
                "oi,iab->oab", taps[tap_row, tap_col], window, precision=precise
            )
    return total


def with_rims(field):
    wider = padded_2(field, (("lon", 2),), 1, True)
    return padded_2(wider, (("lat", 1),), 1, False)


def local_forward(real_part, imag_part):
    columns = real_part.shape[-1]
    places = lax.iota(jnp.int32, columns)
    angles = angle_table(places, places, columns)
    cosine = jnp.cos(angles)
    sine = jnp.sin(angles)
    out_real = jnp.dot(real_part, cosine, precision=precise) + jnp.dot(
        imag_part, sine, precision=precise
    )
    out_imag = jnp.dot(imag_part, cosine, precision=precise) - jnp.dot(
        real_part, sine, precision=precise
    )
    return (out_real, out_imag)


def local_inverse(real_part, imag_part):
    columns = real_part.shape[-1]
    places = lax.iota(jnp.int32, columns)
    angles = angle_table(places, places, columns)
    cosine = jnp.cos(angles)
    sine = jnp.sin(angles)
    out_real = jnp.dot(real_part, cosine, precision=precise) - jnp.dot(
        imag_part, sine, precision=precise
    )
    out_imag = jnp.dot(imag_part, cosine, precision=precise) + jnp.dot(
        real_part, sine, precision=precise
    )
    return (out_real / columns, out_imag / columns)


def section_angles(place, bit_pos, columns):
    offsets = lax.iota(jnp.int32, columns)
    start = place % 2**bit_pos * columns
    span = 2 * columns * 2**bit_pos
    angles = 2.0 * jnp.pi / span * (start + offsets).astype(jnp.float32)
    upper = place // 2**bit_pos % 2 == 1
    return (jnp.cos(angles), jnp.sin(angles), upper)


def forward_pairs(field):
    extent = lax.axis_size("lon")
    width_bits = extent.bit_length() - 1
    place = lax.axis_index("lon")
    columns = field.shape[-1]
    data = jnp.stack([field, jnp.zeros_like(field)])
    for bit_pos in reversed(range(width_bits)):
        other = partner(data, "lon", bit_pos)
        cosine, sine, upper = section_angles(place, bit_pos, columns)
        differ = other - data
        turned = jnp.stack(
            [differ[0] * cosine + differ[1] * sine, differ[1] * cosine - differ[0] * sine]
        )
        data = jnp.where(upper, turned, data + other)
    out_real, out_imag = local_forward(data[0], data[1])
    return jnp.stack([out_real, out_imag])


def inverse_pairs(spectrum):
    extent = lax.axis_size("lon")
    width_bits = extent.bit_length() - 1
    place = lax.axis_index("lon")
    columns = spectrum.shape[-1]
    back_real, back_imag = local_inverse(spectrum[0], spectrum[1])
    data = jnp.stack([back_real, back_imag])
    for bit_pos in range(width_bits):
        cosine, sine, upper = section_angles(place, bit_pos, columns)
        turned = jnp.stack([data[0] * cosine - data[1] * sine, data[1] * cosine + data[0] * sine])
        outgoing = jnp.where(upper, turned, data)
        other = partner(outgoing, "lon", bit_pos)
        data = jnp.where(upper, other - outgoing, outgoing + other) * 0.5
    return data[0]


def on_device_any_mesh(field, cotangent, conv_weight, spectral_filter):
    lat_rows = field.shape[1]
    columns = field.shape[2]
    total_len = columns * lax.axis_size("lon")
    mixed = apply_taps(with_rims(field), conv_weight, lat_rows, columns)
    hidden_spec = forward_pairs(mixed)
    cot_spec = forward_pairs(cotangent)
    gain_real = spectral_filter[0][:, None, :]
    gain_imag = spectral_filter[1][:, None, :]
    filtered = jnp.stack(
        [
            gain_real * hidden_spec[0] - gain_imag * hidden_spec[1],
            gain_real * hidden_spec[1] + gain_imag * hidden_spec[0],
        ]
    )
    adjoint = jnp.stack(
        [
            gain_real * cot_spec[0] + gain_imag * cot_spec[1],
            gain_real * cot_spec[1] - gain_imag * cot_spec[0],
        ]
    )
    shaped = inverse_pairs(filtered)
    back_field = inverse_pairs(adjoint)
    output = field + shaped
    local_grad = (
        jnp.stack(
            [
                jnp.sum(hidden_spec[0] * cot_spec[0] + hidden_spec[1] * cot_spec[1], axis=1),
                jnp.sum(hidden_spec[0] * cot_spec[1] - hidden_spec[1] * cot_spec[0], axis=1),
            ]
        )
        / total_len
    )
    filter_grad = lax.psum(local_grad, "lat")
    flipped_taps = jnp.transpose(conv_weight[::-1, ::-1], (0, 1, 3, 2))
    input_grad = cotangent + apply_taps(with_rims(back_field), flipped_taps, lat_rows, columns)
    return (output, input_grad, filter_grad)


FORTH, BACK = 49, 57


def rank(chip, place):
    upper, odd, x = place // 4, place // 2 % 2, place % 2
    return 8 * ((upper + odd + 1) % 2) + 4 * (1 - x) + 2 * (1 - chip) + 1 - upper


def reversed_bits(value, width):
    return int(format(value, f"0{width}b")[::-1], 2)


def iotas(rows, columns):
    lane = lax.broadcasted_iota(jnp.int32, (rows, columns), 1)
    row = lax.broadcasted_iota(jnp.int32, (rows, columns), 0)
    return lane, row


def fetch_kernel(
    own_ref, cot_ref, filter_ref, taps_ref, own_out, cot_out, gain_out, taps_out, sems
):
    place = lax.axis_index("lat")
    odd, half = lax.rem(place, 2), gain_out.shape[0]
    span = pl.ds(pl.multiple_of(odd * half, half), half)
    copies = [
        pltpu.make_async_copy(own_ref, own_out, sems.at[0]),
        pltpu.make_async_copy(cot_ref, cot_out, sems.at[1]),
        pltpu.make_async_copy(filter_ref.at[place // 2, span], gain_out, sems.at[2]),
    ]

    @pl.when(odd == 1)
    def _():
        half_taps = pltpu.make_async_copy(taps_ref.at[:, :, half:], taps_out, sems.at[3])
        for copy in [half_taps] + copies:
            copy.start()
        for copy in [half_taps] + copies:
            copy.wait()

    @pl.when(odd == 0)
    def _():
        for copy in copies:
            copy.start()
        for copy in copies:
            copy.wait()


def high_low(x):
    high = x.astype(jnp.bfloat16)
    return high, (x - high.astype(jnp.float32)).astype(jnp.bfloat16)


def tall_product(x, high, low):
    rows = x.shape[0]
    x_high, x_low = high_low(x)
    both = jnp.concatenate([x_high, x_low], axis=0)
    both = jnp.dot(both, high, preferred_element_type=jnp.float32)
    rest = jnp.dot(x_high, low, preferred_element_type=jnp.float32)
    return both[:rows] + (both[rows:] + rest)


def conv_kernel(
    own_ref, other_ref, cot_ref, other_cot_ref, gain_ref, half_ref, taps_ref, out_ref, taps, sems
):
    odd, upper = lax.rem(lax.axis_index("lat"), 2), lax.axis_index("lat") // 2
    half = gain_ref.shape[0]
    order = [(row, col) for col in range(3) for row in (1, 2 * upper, 2 - 2 * upper)]

    @pl.when(odd == 0)
    def _():
        copies = [
            pltpu.make_async_copy(taps_ref.at[row, col, :half], taps.at[index], sems.at[index])
            for index, (row, col) in enumerate(order)
        ]
        for copy in copies:
            copy.start()

        def weights(index):
            copies[index].wait()
            return high_low(taps[index])

        pack((own_ref, other_ref), (cot_ref, other_cot_ref), gain_ref, weights, 0, out_ref)

    @pl.when(odd == 1)
    def _():
        def weights(index):
            return high_low(half_ref[order[index]])

        pack((other_ref, own_ref), (other_cot_ref, cot_ref), gain_ref, weights, 1, out_ref)


def pack(fields, cots, gain_ref, weights, core, out_ref):
    upper = lax.axis_index("lat") // 2
    half, columns = gain_ref.shape
    row_0, row_1 = fields[0][...], fields[1][...]
    near = jnp.concatenate(high_low(jnp.where(upper == 0, row_1, row_0)), axis=1)
    both_high, both_low = high_low(jnp.concatenate([row_0, row_1], axis=1))

    def times(weights, values):
        return jnp.dot(weights, values, preferred_element_type=jnp.float32)

    parts = []
    for tap_col in range(3):
        high, low = weights(3 * tap_col)
        middle = times(high, both_high) + (times(high, both_low) + times(low, both_high))
        high, low = weights(3 * tap_col + 1)
        outer = times(high, both_high) + (times(high, both_low) + times(low, both_high))
        high, low = weights(3 * tap_col + 2)
        wide = times(high, near)
        inner = wide[:, :columns] + (wide[:, columns:] + times(low, near[:, :columns]))
        on_0, on_1 = outer[:, :columns], outer[:, columns:]
        parts.append(
            jnp.concatenate(
                [
                    middle[:, :columns] + jnp.where(upper == 0, inner, on_1),
                    middle[:, columns:] + jnp.where(upper == 0, on_0, inner),
                    jnp.where(upper == 0, on_1, on_0),
                ],
                axis=0,
            )
        )
    lane, row = iotas(3 * half, columns)
    left, middle, right = parts
    main = (
        middle
        + jnp.where(lane == 0, 0.0, pltpu.roll(left, 1, 1))
        + jnp.where(lane == columns - 1, 0.0, pltpu.roll(right, columns - 1, 1))
    )
    slot = lane - lax.rem(row, 8) - 8 * (row // half)
    edges = jnp.where(slot == 0, left[:, columns - 1 :], 0.0)
    edges = jnp.where(slot == 24, right[:, 0:1], edges)
    edges = edges[:half] + edges[half : 2 * half] + edges[2 * half :]
    for owner in range(half // 8):
        first = FORTH * owner
        for part in range(3):
            here = half * part + 8 * owner
            out_ref[first + 16 + 8 * part : first + 24 + 8 * part, :] = main[here : here + 8]
        out_ref[first + 48 : first + 49, :] = jnp.sum(
            edges[8 * owner : 8 * owner + 8], axis=0, keepdims=True
        )
    for owner in range(half // 8):
        first, here = FORTH * owner, half * core + 8 * owner
        out_ref[first : first + 8, :] = cots[0][here : here + 8, :]
        out_ref[first + 8 : first + 16, :] = cots[1][here : here + 8, :]
        out_ref[first + 40 : first + 48, :] = gain_ref[8 * owner : 8 * owner + 8, :]


def transform_8(x):
    s = [x[d] + x[d + 4] for d in range(4)]
    t = [x[d] - x[d + 4] for d in range(4)]
    plus, minus = ROOT_HALF * (t[1] + t[3]), ROOT_HALF * (t[1] - t[3])
    return [
        (s[0] + s[2] + (s[1] + s[3]), None),
        (t[0] + minus, -t[2] - plus),
        (s[0] - s[2], s[3] - s[1]),
        (t[0] - minus, t[2] - plus),
        (s[0] + s[2] - (s[1] + s[3]), None),
    ]


def spectral_kernel(in_ref, turn_ref, dft_ref, out_ref, work):
    rows, lon = 4, 8
    columns = in_ref.shape[-1]
    lane, sub = iotas(8, columns)
    me = rank(lax.axis_index("lat") // 2, lax.axis_index("lon"))

    def message(chip, place, first, count):
        start = FORTH * rank(chip, place) + first
        return in_ref[start : start + count, :]

    def edge(row, place, group):
        chip, part = row // 2, row % 2
        wanted = lane == sub + 8 * part + 24 * group
        line = jnp.where(wanted, message(chip, place, 48, 1), 0.0)
        if row in (1, 2):
            wanted = lane == sub + 16 + 24 * group
            line = line + jnp.where(wanted, message(1 - chip, place, 48, 1), 0.0)
        return jnp.sum(line, axis=1, keepdims=True)

    grid = []
    for place in range(lon):
        mixed = []
        for row in range(rows):
            tile = message(row // 2, place, 16 + 8 * (row % 2), 8)
            if row in (1, 2):
                tile = tile + message(1 - row // 2, place, 32, 8)
            left, right = edge(row, (place - 1) % lon, 0), edge(row, (place + 1) % lon, 1)
            outer = jnp.where(lane == columns - 1, right, 0.0)
            mixed.append(tile + jnp.where(lane == 0, left, outer))
        cot = [message(row // 2, place, 8 * (row % 2), 8) for row in range(rows)]
        grid.append(jnp.concatenate(mixed + cot, axis=0))
    pairs = transform_8(grid)
    height = 16 * rows
    for residue in range(lon):
        real, imag = pairs[min(residue, lon - residue)]
        cosine, sine = turn_ref[residue : residue + 1, :], turn_ref[8 + residue : 9 + residue, :]
        if imag is None:
            turned = (real * cosine, -real * sine)
        elif residue < 4:
            turned = (real * cosine + imag * sine, imag * cosine - real * sine)
        else:
            turned = (real * cosine - imag * sine, -imag * cosine - real * sine)
        span = pl.ds(residue * height, height)
        work[span, 0:columns] = turned[0]
        work[span, columns:] = turned[1]
    chunk = lon * height // 4
    pieces = [pl.ds(first, chunk) for first in range(0, lon * height, chunk)]
    table = high_low(dft_ref[...])
    spectra = jnp.concatenate(
        [tall_product(work[piece], *table) for piece in pieces], axis=0
    )
    scale = 1.0 / (lon * columns)
    half = 8 * rows
    gradients = []
    for residue in range(lon):
        place = reversed_bits(residue, 3)
        part = spectra[residue * height : (residue + 1) * height]
        mix_re, mix_im = part[:half, :columns], part[:half, columns:]
        cot_re, cot_im = part[half:, :columns], part[half:, columns:]
        gain_re = jnp.concatenate([message(0, place, 40, 8) * scale] * rows, axis=0)
        gain_im = jnp.concatenate([message(1, place, 40, 8) * scale] * rows, axis=0)
        top = pl.ds(residue * height, half)
        bottom = pl.ds(residue * height + half, half)
        work[top, 0:columns] = gain_re * mix_re - gain_im * mix_im
        work[top, columns:] = -(gain_re * mix_im + gain_im * mix_re)
        work[bottom, 0:columns] = gain_re * cot_re + gain_im * cot_im
        work[bottom, columns:] = gain_im * cot_re - gain_re * cot_im
        grad_re = (mix_re * cot_re + mix_im * cot_im) * scale
        grad_im = (mix_re * cot_im - mix_im * cot_re) * scale
        gradients.append(
            [
                grad[0:8] + grad[8:16] + (grad[16:24] + grad[24:32])
                for grad in (grad_re, grad_im)
            ]
        )
    back = jnp.concatenate(
        [tall_product(work[piece], *table) for piece in pieces], axis=0
    )
    turned = []
    for residue in range(lon):
        part = back[residue * height : (residue + 1) * height]
        real, imag = part[:, :columns], part[:, columns:]
        cosine, sine = turn_ref[residue : residue + 1, :], turn_ref[8 + residue : 9 + residue, :]
        turned.append((real * cosine + imag * sine, real * sine - imag * cosine))
    sums = [turned[r][0] + turned[lon - r][0] for r in (1, 2, 3)]
    gaps = [turned[r][1] - turned[lon - r][1] for r in (1, 2, 3)]
    first, fourth = turned[0][0], turned[4][0]
    even = [
        first + fourth + sums[1],
        first - fourth - gaps[1],
        first + fourth - sums[1],
        first - fourth + gaps[1],
    ]
    swing = [
        sums[0] + sums[2],
        ROOT_HALF * (sums[0] - gaps[0] - sums[2] - gaps[2]),
        gaps[2] - gaps[0],
        ROOT_HALF * (sums[2] - gaps[2] - sums[0] - gaps[0]),
    ]
    series = [even[d] + swing[d] for d in range(4)] + [even[d] - swing[d] for d in range(4)]
    slots = [lane == 8 * lax.rem(me + group, 16) + sub for group in range(6)]
    for place in range(lon):
        residue = reversed_bits(place, 3)
        before, after = series[(place - 1) % lon], series[(place + 1) % lon]
        for chip in range(2):
            start = BACK * rank(chip, place)
            rims = jnp.zeros((8, columns), jnp.float32)
            for step in range(3):
                here = half + 8 * (chip + step)
                span = slice(here, here + 8)
                rims = jnp.where(slots[2 * step], before[span, columns - 1 :], rims)
                rims = jnp.where(slots[2 * step + 1], after[span, 0:1], rims)
                first = start + 16 + 8 * step
                out_ref[first : first + 8, :] = series[place][span]
            out_ref[start : start + 16, :] = series[place][16 * chip : 16 * chip + 16]
            for part in range(2):
                first = start + 40 + 8 * part
                out_ref[first : first + 8, :] = gradients[residue][part]
            out_ref[start + 56 : start + 57, :] = jnp.sum(rims, axis=0, keepdims=True)


def partial_adjoint(message_ref, taps_ref, rows_ref, part):
    half, columns = rows_ref.shape[-1], message_ref.shape[-1]
    place = lax.axis_index("lat")
    index = place - place // 2
    owners = half // 8
    lines = message_ref[pl.ds(56, owners, stride=BACK), :]
    lane, owner = iotas(owners, columns)
    rows_ref[0] = jnp.zeros(rows_ref.shape[1:], jnp.float32)
    rows_ref[4] = jnp.zeros(rows_ref.shape[1:], jnp.float32)
    for step in range(3):
        pieces = [
            message_ref[BACK * j + 16 + 8 * step : BACK * j + 24 + 8 * step, :] for j in range(owners)
        ]
        rows_ref[1 + step, 8 : 8 + columns, :] = jnp.concatenate(pieces, axis=0).T
        for rim, target in ((2 * step, 7), (2 * step + 1, 8 + columns)):
            wanted = lane // 8 == lax.rem(owner + rim, owners)
            line = jnp.sum(jnp.where(wanted, lines, 0.0), axis=0, keepdims=True)
            line = jnp.broadcast_to(line, (8, columns))
            if rim:
                line = pltpu.roll(line, columns - 8 * rim, 1)
            rows_ref[1 + step, target : target + 1, :] = line[0:1]
    span = pl.ds(pl.multiple_of(part * half, half), half)
    windows, weights = [], []
    for tap_row in range(3):
        for tap_col in range(3):
            first = 9 - tap_col
            windows.append(rows_ref[index + 2 - tap_row, first : first + columns, :])
            weights.append(taps_ref[tap_row, tap_col, span])
    total = 0.0
    for pair in range(0, 9, 2):
        window = jnp.concatenate(windows[pair : pair + 2], axis=1)
        weight = jnp.concatenate(weights[pair : pair + 2], axis=0)
        total = total + tall_product(window, *high_low(weight))
    return total


def adjoint_kernel(mine_ref, taps_ref, total_ref, rows_ref):
    part = lax.rem(lax.axis_index("lat"), 2)
    total_ref[...] = partial_adjoint(mine_ref, taps_ref, rows_ref, part)


def last_kernel(
    mine_ref, other_ref, field_ref, cot_ref, taps_ref, total_ref, out_ref, grad_ref, gain_ref, rows_ref
):
    half = cot_ref.shape[0] // 2
    part = lax.rem(lax.axis_index("lat"), 2)
    for message_ref, side in ((mine_ref, part), (other_ref, 1 - part)):
        for owner in range(half // 8):
            here = pl.ds(pl.multiple_of(half * side + 8 * owner, 8), 8)
            start = BACK * owner
            first, second = message_ref[start : start + 8, :], message_ref[start + 8 : start + 16, :]
            out_ref[here, :] = field_ref[here, :] + jnp.where(part == 0, first, second)
            gain_ref[0, here, :] = message_ref[start + 40 : start + 48, :]
            gain_ref[1, here, :] = message_ref[start + 48 : start + 56, :]
    total = total_ref[...] + partial_adjoint(other_ref, taps_ref, rows_ref, 1 - part)
    grad_ref[...] = cot_ref[...] + total.T


def transform_tables(columns, lon):
    places = np.arange(columns)
    turn = 2.0 * np.pi * (np.arange(lon)[:, None] * places[None, :]) / (lon * columns)
    angle = 2.0 * np.pi * (places[:, None] * places[None, :] % columns) / columns
    cosine, sine = np.cos(angle), np.sin(angle)
    dft = np.block([[cosine, -sine], [sine, cosine]])
    turns = np.concatenate([np.cos(turn), np.sin(turn)], axis=0)
    return jnp.asarray(turns, jnp.float32), jnp.asarray(dft, jnp.float32)


def exchanged(flat, lat, lon):
    rows, columns = flat.shape
    members = [(chip, place) for chip in range(lat // 2) for place in range(lon)]
    members.sort(key=lambda member: rank(*member))
    groups = [[(2 * chip + core) * lon + place for chip, place in members] for core in range(2)]
    moved = lax.all_to_all(
        flat.reshape(rows, 1, columns),
        ("lat", "lon"),
        0,
        0,
        tiled=True,
        axis_index_groups=groups,
    )
    return moved.reshape(rows, columns)


def in_hbm(x):
    return pltpu.with_memory_space_constraint(x, pltpu.HBM)


def on_device(field, cotangent, conv_weight, spectral_filter):
    channels, _, columns = field.shape
    lat, lon = lax.axis_size("lat"), lax.axis_size("lon")
    owners = lat * lon // 2
    swap = [(i, i ^ 1) for i in range(lat)]
    own = field.reshape(channels, columns)
    cot = cotangent.reshape(channels, columns)
    vmem = pl.BlockSpec(memory_space=pltpu.VMEM)
    hbm = pl.BlockSpec(memory_space=pltpu.HBM)
    params = pltpu.CompilerParams(vmem_limit_bytes=16 * 1024 * 1024)
    flat = jax.ShapeDtypeStruct((channels, columns), jnp.float32)
    half_taps = jax.ShapeDtypeStruct((3, 3, channels // 2, channels), jnp.float32)
    forth = jax.ShapeDtypeStruct((owners * FORTH, columns), jnp.float32)
    back = jax.ShapeDtypeStruct((owners * BACK, columns), jnp.float32)
    other, other_cot = lax.ppermute((own, cot), "lat", swap)
    gain_half = jax.ShapeDtypeStruct((channels // 2, columns), jnp.float32)
    own_here, cot_here, gain, taps = pl.pallas_call(
        fetch_kernel,
        out_shape=(flat, flat, gain_half, half_taps),
        in_specs=[hbm] * 4,
        out_specs=(vmem,) * 4,
        scratch_shapes=[pltpu.SemaphoreType.DMA((4,))],
        compiler_params=params,
        name="fetch",
    )(*map(in_hbm, (own, cot, spectral_filter, conv_weight)))
    outgoing = pl.pallas_call(
        conv_kernel,
        out_shape=forth,
        in_specs=[vmem] * 6 + [hbm],
        out_specs=vmem,
        scratch_shapes=[
            pltpu.VMEM((9, channels // 2, channels), jnp.float32),
            pltpu.SemaphoreType.DMA((9,)),
        ],
        compiler_params=params,
        name="conv",
    )(own_here, other, cot_here, other_cot, gain, taps, in_hbm(conv_weight))
    turns, dft = transform_tables(columns, lon)
    returned = pl.pallas_call(
        spectral_kernel,
        out_shape=back,
        in_specs=[vmem] * 3,
        out_specs=vmem,
        scratch_shapes=[pltpu.VMEM((2 * 8 * lat * lon, 2 * columns), jnp.float32)],
        compiler_params=params,
        name="spectral",
    )(exchanged(outgoing, lat, lon), turns, dft)
    mine = exchanged(returned, lat, lon)
    other = lax.ppermute(mine, "lat", swap)
    rows_scratch = pltpu.VMEM((5, columns + 16, channels // 2), jnp.float32)
    total = pl.pallas_call(
        adjoint_kernel,
        out_shape=jax.ShapeDtypeStruct((columns, channels), jnp.float32),
        in_specs=[vmem] * 2,
        out_specs=vmem,
        scratch_shapes=[rows_scratch],
        compiler_params=params,
        name="adjoint",
    )(mine, conv_weight)
    output, input_grad, filter_grad = pl.pallas_call(
        last_kernel,
        out_shape=(flat, flat, jax.ShapeDtypeStruct(spectral_filter.shape, jnp.float32)),
        in_specs=[vmem] * 6,
        out_specs=(vmem, vmem, vmem),
        scratch_shapes=[rows_scratch],
        compiler_params=params,
        name="last",
    )(mine, other, own, cot, conv_weight, total)
    return (output.reshape(field.shape), input_grad.reshape(field.shape), filter_grad)


def solution(mesh):
    placed = (P(None, "lat", "lon"), P(None, "lat", "lon"), P(), P(None, None, "lon"))
    specs = (P(None, "lat", "lon"), P(None, "lat", "lon"), P(None, None, "lon"))

    def layer(field, cotangent, conv_weight, spectral_filter):
        lat, lon = mesh.shape["lat"], mesh.shape["lon"]
        channels, rows, length = field.shape
        owned = rows == lat == 4 and lon == 8 and channels == 8 * lat * lon and length == 128 * lon
        body = on_device if owned else on_device_any_mesh
        mapped = jax.shard_map(body, mesh=mesh, in_specs=placed, out_specs=specs, check_vma=False)
        return mapped(field, cotangent, conv_weight, spectral_filter)

    return layer
```

```python
from functools import partial

import jax
import jax.numpy as jnp
import numpy as np
from jax import lax
from jax.experimental import pallas as pl
from jax.experimental.pallas import tpu as pltpu
from jax.sharding import PartitionSpec as P

precise = lax.Precision.HIGHEST
three_pass = lax.Precision.HIGH
ROOT_HALF = 0.5**0.5


def padded_2(array, sides, width, wrap):
    for axis, dim in sides:
        peers, length = (lax.axis_size(axis), array.shape[dim])
        up = [(i, (i + 1) % peers) for i in range(peers if wrap else peers - 1)]
        down = [(j, i) for i, j in up]
        last = lax.slice_in_dim(array, length - width, length, axis=dim)
        leading = lax.slice_in_dim(array, 0, width, axis=dim)
        before = lax.ppermute(last, axis, up)
        after = lax.ppermute(leading, axis, down)
        array = jnp.concatenate([before, array, after], axis=dim)
    return array


def partner(array, axis, stride):
    return lax.ppermute(array, axis, [(i, i ^ 1 << stride) for i in range(lax.axis_size(axis))])


def angle_table(first, second, modulus):
    product = first[:, None] * second[None, :] % modulus
    return 2.0 * jnp.pi / modulus * product.astype(jnp.float32)


def apply_taps(padded, taps, lat_rows, columns):
    total = jnp.zeros((taps.shape[2], lat_rows, columns), jnp.float32)
    for tap_row in range(3):
        for tap_col in range(3):
            window = padded[:, tap_row : tap_row + lat_rows, tap_col : tap_col + columns]
            total = total + jnp.einsum(
                "oi,iab->oab", taps[tap_row, tap_col], window, precision=precise
            )
    return total


def with_rims(field):
    wider = padded_2(field, (("lon", 2),), 1, True)
    return padded_2(wider, (("lat", 1),), 1, False)


def local_forward(real_part, imag_part):
    columns = real_part.shape[-1]
    places = lax.iota(jnp.int32, columns)
    angles = angle_table(places, places, columns)
    cosine = jnp.cos(angles)
    sine = jnp.sin(angles)
    out_real = jnp.dot(real_part, cosine, precision=precise) + jnp.dot(
        imag_part, sine, precision=precise
    )
    out_imag = jnp.dot(imag_part, cosine, precision=precise) - jnp.dot(
        real_part, sine, precision=precise
    )
    return (out_real, out_imag)


def local_inverse(real_part, imag_part):
    columns = real_part.shape[-1]
    places = lax.iota(jnp.int32, columns)
    angles = angle_table(places, places, columns)
    cosine = jnp.cos(angles)
    sine = jnp.sin(angles)
    out_real = jnp.dot(real_part, cosine, precision=precise) - jnp.dot(
        imag_part, sine, precision=precise
    )
    out_imag = jnp.dot(imag_part, cosine, precision=precise) + jnp.dot(
        real_part, sine, precision=precise
    )
    return (out_real / columns, out_imag / columns)


def section_angles(place, bit_pos, columns):
    offsets = lax.iota(jnp.int32, columns)
    start = place % 2**bit_pos * columns
    span = 2 * columns * 2**bit_pos
    angles = 2.0 * jnp.pi / span * (start + offsets).astype(jnp.float32)
    upper = place // 2**bit_pos % 2 == 1
    return (jnp.cos(angles), jnp.sin(angles), upper)


def forward_pairs(field):
    extent = lax.axis_size("lon")
    width_bits = extent.bit_length() - 1
    place = lax.axis_index("lon")
    columns = field.shape[-1]
    data = jnp.stack([field, jnp.zeros_like(field)])
    for bit_pos in reversed(range(width_bits)):
        other = partner(data, "lon", bit_pos)
        cosine, sine, upper = section_angles(place, bit_pos, columns)
        differ = other - data
        turned = jnp.stack(
            [differ[0] * cosine + differ[1] * sine, differ[1] * cosine - differ[0] * sine]
        )
        data = jnp.where(upper, turned, data + other)
    out_real, out_imag = local_forward(data[0], data[1])
    return jnp.stack([out_real, out_imag])


def inverse_pairs(spectrum):
    extent = lax.axis_size("lon")
    width_bits = extent.bit_length() - 1
    place = lax.axis_index("lon")
    columns = spectrum.shape[-1]
    back_real, back_imag = local_inverse(spectrum[0], spectrum[1])
    data = jnp.stack([back_real, back_imag])
    for bit_pos in range(width_bits):
        cosine, sine, upper = section_angles(place, bit_pos, columns)
        turned = jnp.stack([data[0] * cosine - data[1] * sine, data[1] * cosine + data[0] * sine])
        outgoing = jnp.where(upper, turned, data)
        other = partner(outgoing, "lon", bit_pos)
        data = jnp.where(upper, other - outgoing, outgoing + other) * 0.5
    return data[0]


def on_device_any_mesh(field, cotangent, conv_weight, spectral_filter):
    lat_rows = field.shape[1]
    columns = field.shape[2]
    total_len = columns * lax.axis_size("lon")
    mixed = apply_taps(with_rims(field), conv_weight, lat_rows, columns)
    hidden_spec = forward_pairs(mixed)
    cot_spec = forward_pairs(cotangent)
    gain_real = spectral_filter[0][:, None, :]
    gain_imag = spectral_filter[1][:, None, :]
    filtered = jnp.stack(
        [
            gain_real * hidden_spec[0] - gain_imag * hidden_spec[1],
            gain_real * hidden_spec[1] + gain_imag * hidden_spec[0],
        ]
    )
    adjoint = jnp.stack(
        [
            gain_real * cot_spec[0] + gain_imag * cot_spec[1],
            gain_real * cot_spec[1] - gain_imag * cot_spec[0],
        ]
    )
    shaped = inverse_pairs(filtered)
    back_field = inverse_pairs(adjoint)
    output = field + shaped
    local_grad = (
        jnp.stack(
            [
                jnp.sum(hidden_spec[0] * cot_spec[0] + hidden_spec[1] * cot_spec[1], axis=1),
                jnp.sum(hidden_spec[0] * cot_spec[1] - hidden_spec[1] * cot_spec[0], axis=1),
            ]
        )
        / total_len
    )
    filter_grad = lax.psum(local_grad, "lat")
    flipped_taps = jnp.transpose(conv_weight[::-1, ::-1], (0, 1, 3, 2))
    input_grad = cotangent + apply_taps(with_rims(back_field), flipped_taps, lat_rows, columns)
    return (output, input_grad, filter_grad)


FORTH, BACK = 49, 57


def rank(chip, place):
    upper, odd, x = place // 4, place // 2 % 2, place % 2
    return 8 * ((upper + odd + 1) % 2) + 4 * (1 - x) + 2 * (1 - chip) + 1 - upper


def reversed_bits(value, width):
    return int(format(value, f"0{width}b")[::-1], 2)


def iotas(rows, columns):
    lane = lax.broadcasted_iota(jnp.int32, (rows, columns), 1)
    row = lax.broadcasted_iota(jnp.int32, (rows, columns), 0)
    return lane, row


def fetch_kernel(
    own_ref, cot_ref, filter_ref, taps_ref, own_out, cot_out, gain_out, taps_out, sems
):
    place = lax.axis_index("lat")
    odd, half = lax.rem(place, 2), gain_out.shape[0]
    span = pl.ds(pl.multiple_of(odd * half, half), half)
    copies = [
        pltpu.make_async_copy(own_ref, own_out, sems.at[0]),
        pltpu.make_async_copy(cot_ref, cot_out, sems.at[1]),
        pltpu.make_async_copy(filter_ref.at[place // 2, span], gain_out, sems.at[2]),
    ]

    @pl.when(odd == 1)
    def _():
        all_taps = [
            pltpu.make_async_copy(taps_ref.at[row, :, half:], taps_out.at[row], sems.at[3 + row])
            for row in range(3)
        ]
        for copy in all_taps + copies:
            copy.start()
        for copy in copies + all_taps:
            copy.wait()

    @pl.when(odd == 0)
    def _():
        for copy in copies:
            copy.start()
        for copy in copies:
            copy.wait()


def high_low(x):
    high = x.astype(jnp.bfloat16)
    return high, (x - high.astype(jnp.float32)).astype(jnp.bfloat16)


def tall_product(x, high, low):
    rows = x.shape[0]
    x_high, x_low = high_low(x)
    both = jnp.concatenate([x_high, x_low], axis=0)
    both = jnp.dot(both, high, preferred_element_type=jnp.float32)
    rest = jnp.dot(x_high, low, preferred_element_type=jnp.float32)
    return both[:rows] + (both[rows:] + rest)


def conv_kernel(
    own_ref, other_ref, cot_ref, other_cot_ref, gain_ref, half_ref, taps_ref, out_ref, taps, sems
):
    odd, upper = lax.rem(lax.axis_index("lat"), 2), lax.axis_index("lat") // 2
    half = gain_ref.shape[0]
    order = [(row, col) for col in range(3) for row in (1, 2 * upper, 2 - 2 * upper)]

    @pl.when(odd == 0)
    def _():
        copies = [
            pltpu.make_async_copy(taps_ref.at[row, col, :half], taps.at[index], sems.at[index])
            for index, (row, col) in enumerate(order)
        ]
        for copy in copies:
            copy.start()

        def weights(index):
            copies[index].wait()
            return high_low(taps[index])

        pack((own_ref, other_ref), (cot_ref, other_cot_ref), gain_ref, weights, 0, out_ref)

    @pl.when(odd == 1)
    def _():
        def weights(index):
            return high_low(half_ref[order[index]])

        pack((other_ref, own_ref), (other_cot_ref, cot_ref), gain_ref, weights, 1, out_ref)


def pack(fields, cots, gain_ref, weights, core, out_ref):
    upper = lax.axis_index("lat") // 2
    half, columns = gain_ref.shape
    for owner in range(half // 8):
        first, here = FORTH * owner, half * core + 8 * owner
        out_ref[first : first + 8, :] = cots[0][here : here + 8, :]
        out_ref[first + 8 : first + 16, :] = cots[1][here : here + 8, :]
        out_ref[first + 40 : first + 48, :] = gain_ref[8 * owner : 8 * owner + 8, :]
    row_0, row_1 = fields[0][...], fields[1][...]
    near = jnp.concatenate(high_low(jnp.where(upper == 0, row_1, row_0)), axis=1)
    both_high, both_low = high_low(jnp.concatenate([row_0, row_1], axis=1))

    def times(weights, values):
        return jnp.dot(weights, values, preferred_element_type=jnp.float32)

    parts = []
    for tap_col in range(3):
        high, low = weights(3 * tap_col)
        middle = times(high, both_high) + (times(high, both_low) + times(low, both_high))
        high, low = weights(3 * tap_col + 1)
        outer = times(high, both_high) + (times(high, both_low) + times(low, both_high))
        high, low = weights(3 * tap_col + 2)
        wide = times(high, near)
        inner = wide[:, :columns] + (wide[:, columns:] + times(low, near[:, :columns]))
        on_0, on_1 = outer[:, :columns], outer[:, columns:]
        parts.append(
            jnp.concatenate(
                [
                    middle[:, :columns] + jnp.where(upper == 0, inner, on_1),
                    middle[:, columns:] + jnp.where(upper == 0, on_0, inner),
                    jnp.where(upper == 0, on_1, on_0),
                ],
                axis=0,
            )
        )
    lane, row = iotas(3 * half, columns)
    left, middle, right = parts
    main = (
        middle
        + jnp.where(lane == 0, 0.0, pltpu.roll(left, 1, 1))
        + jnp.where(lane == columns - 1, 0.0, pltpu.roll(right, columns - 1, 1))
    )
    slot = lane - lax.rem(row, 8) - 8 * (row // half)
    edges = jnp.where(slot == 0, left[:, columns - 1 :], 0.0)
    edges = jnp.where(slot == 24, right[:, 0:1], edges)
    edges = edges[:half] + edges[half : 2 * half] + edges[2 * half :]
    for owner in range(half // 8):
        first = FORTH * owner
        for part in range(3):
            here = half * part + 8 * owner
            out_ref[first + 16 + 8 * part : first + 24 + 8 * part, :] = main[here : here + 8]
        out_ref[first + 48 : first + 49, :] = jnp.sum(
            edges[8 * owner : 8 * owner + 8], axis=0, keepdims=True
        )


def transform_8(x):
    s = [x[d] + x[d + 4] for d in range(4)]
    t = [x[d] - x[d + 4] for d in range(4)]
    plus, minus = ROOT_HALF * (t[1] + t[3]), ROOT_HALF * (t[1] - t[3])
    return [
        (s[0] + s[2] + (s[1] + s[3]), None),
        (t[0] + minus, -t[2] - plus),
        (s[0] - s[2], s[3] - s[1]),
        (t[0] - minus, t[2] - plus),
        (s[0] + s[2] - (s[1] + s[3]), None),
    ]


def spectral_kernel(in_ref, turn_ref, dft_ref, out_ref, work):
    rows, lon = 4, 8
    columns = in_ref.shape[-1]
    lane, sub = iotas(8, columns)
    me = rank(lax.axis_index("lat") // 2, lax.axis_index("lon"))

    def message(chip, place, first, count):
        start = FORTH * rank(chip, place) + first
        return in_ref[start : start + count, :]

    def edge(row, place, group):
        chip, part = row // 2, row % 2
        wanted = lane == sub + 8 * part + 24 * group
        line = jnp.where(wanted, message(chip, place, 48, 1), 0.0)
        if row in (1, 2):
            wanted = lane == sub + 16 + 24 * group
            line = line + jnp.where(wanted, message(1 - chip, place, 48, 1), 0.0)
        return jnp.sum(line, axis=1, keepdims=True)

    grid = []
    for place in range(lon):
        mixed = []
        for row in range(rows):
            tile = message(row // 2, place, 16 + 8 * (row % 2), 8)
            if row in (1, 2):
                tile = tile + message(1 - row // 2, place, 32, 8)
            tile = tile + jnp.where(lane == 0, edge(row, (place - 1) % lon, 0), 0.0)
            tile = tile + jnp.where(lane == columns - 1, edge(row, (place + 1) % lon, 1), 0.0)
            mixed.append(tile)
        cot = [message(row // 2, place, 8 * (row % 2), 8) for row in range(rows)]
        grid.append(jnp.concatenate(mixed + cot, axis=0))
    pairs = transform_8(grid)
    height = 16 * rows
    for residue in range(lon):
        real, imag = pairs[min(residue, lon - residue)]
        cosine, sine = turn_ref[residue : residue + 1, :], turn_ref[8 + residue : 9 + residue, :]
        if imag is None:
            turned = (real * cosine, -real * sine)
        elif residue < 4:
            turned = (real * cosine + imag * sine, imag * cosine - real * sine)
        else:
            turned = (real * cosine - imag * sine, -imag * cosine - real * sine)
        span = pl.ds(residue * height, height)
        work[span, 0:columns] = turned[0]
        work[span, columns:] = turned[1]
    chunk = lon * height // 4
    pieces = [pl.ds(first, chunk) for first in range(0, lon * height, chunk)]
    table = high_low(dft_ref[...])
    spectra = jnp.concatenate(
        [tall_product(work[piece], *table) for piece in pieces], axis=0
    )
    scale = 1.0 / (lon * columns)
    half = 8 * rows
    gradients = []
    for residue in range(lon):
        place = reversed_bits(residue, 3)
        part = spectra[residue * height : (residue + 1) * height]
        mix_re, mix_im = part[:half, :columns], part[:half, columns:]
        cot_re, cot_im = part[half:, :columns], part[half:, columns:]
        gain_re = jnp.concatenate([message(0, place, 40, 8) * scale] * rows, axis=0)
        gain_im = jnp.concatenate([message(1, place, 40, 8) * scale] * rows, axis=0)
        top = pl.ds(residue * height, half)
        bottom = pl.ds(residue * height + half, half)
        work[top, 0:columns] = gain_re * mix_re - gain_im * mix_im
        work[top, columns:] = -(gain_re * mix_im + gain_im * mix_re)
        work[bottom, 0:columns] = gain_re * cot_re + gain_im * cot_im
        work[bottom, columns:] = gain_im * cot_re - gain_re * cot_im
        grad_re = (mix_re * cot_re + mix_im * cot_im) * scale
        grad_im = (mix_re * cot_im - mix_im * cot_re) * scale
        gradients.append(
            [
                grad[0:8] + grad[8:16] + (grad[16:24] + grad[24:32])
                for grad in (grad_re, grad_im)
            ]
        )
    back = jnp.concatenate(
        [tall_product(work[piece], *table) for piece in pieces], axis=0
    )
    turned = []
    for residue in range(lon):
        part = back[residue * height : (residue + 1) * height]
        real, imag = part[:, :columns], part[:, columns:]
        cosine, sine = turn_ref[residue : residue + 1, :], turn_ref[8 + residue : 9 + residue, :]
        turned.append((real * cosine + imag * sine, real * sine - imag * cosine))
    sums = [turned[r][0] + turned[lon - r][0] for r in (1, 2, 3)]
    gaps = [turned[r][1] - turned[lon - r][1] for r in (1, 2, 3)]
    first, fourth = turned[0][0], turned[4][0]
    even = [
        first + fourth + sums[1],
        first - fourth - gaps[1],
        first + fourth - sums[1],
        first - fourth + gaps[1],
    ]
    swing = [
        sums[0] + sums[2],
        ROOT_HALF * (sums[0] - gaps[0] - sums[2] - gaps[2]),
        gaps[2] - gaps[0],
        ROOT_HALF * (sums[2] - gaps[2] - sums[0] - gaps[0]),
    ]
    series = [even[d] + swing[d] for d in range(4)] + [even[d] - swing[d] for d in range(4)]
    slots = [lane == 8 * lax.rem(me + group, 16) + sub for group in range(6)]
    for place in range(lon):
        residue = reversed_bits(place, 3)
        before, after = series[(place - 1) % lon], series[(place + 1) % lon]
        for chip in range(2):
            start = BACK * rank(chip, place)
            rims = jnp.zeros((8, columns), jnp.float32)
            for step in range(3):
                here = half + 8 * (chip + step)
                span = slice(here, here + 8)
                rims = jnp.where(slots[2 * step], before[span, columns - 1 :], rims)
                rims = jnp.where(slots[2 * step + 1], after[span, 0:1], rims)
                first = start + 16 + 8 * step
                out_ref[first : first + 8, :] = series[place][span]
            out_ref[start : start + 16, :] = series[place][16 * chip : 16 * chip + 16]
            for part in range(2):
                first = start + 40 + 8 * part
                out_ref[first : first + 8, :] = gradients[residue][part]
            out_ref[start + 56 : start + 57, :] = jnp.sum(rims, axis=0, keepdims=True)


def partial_adjoint(message_ref, taps_ref, rows_ref, part):
    half, columns = rows_ref.shape[-1], message_ref.shape[-1]
    place = lax.axis_index("lat")
    index = place - place // 2
    owners = half // 8
    lines = message_ref[pl.ds(56, owners, stride=BACK), :]
    lane, owner = iotas(owners, columns)
    rows_ref[0] = jnp.zeros(rows_ref.shape[1:], jnp.float32)
    rows_ref[4] = jnp.zeros(rows_ref.shape[1:], jnp.float32)
    for step in range(3):
        pieces = [
            message_ref[BACK * j + 16 + 8 * step : BACK * j + 24 + 8 * step, :] for j in range(owners)
        ]
        rows_ref[1 + step, 8 : 8 + columns, :] = jnp.concatenate(pieces, axis=0).T
        for rim, target in ((2 * step, 7), (2 * step + 1, 8 + columns)):
            wanted = lane // 8 == lax.rem(owner + rim, owners)
            line = jnp.sum(jnp.where(wanted, lines, 0.0), axis=0, keepdims=True)
            line = jnp.broadcast_to(line, (8, columns))
            if rim:
                line = pltpu.roll(line, columns - 8 * rim, 1)
            rows_ref[1 + step, target : target + 1, :] = line[0:1]
    span = pl.ds(pl.multiple_of(part * half, half), half)
    windows, weights = [], []
    for tap_row in range(3):
        for tap_col in range(3):
            first = 9 - tap_col
            windows.append(rows_ref[index + 2 - tap_row, first : first + columns, :])
            weights.append(taps_ref[tap_row, tap_col, span])
    window = jnp.concatenate(windows, axis=1)
    weight = jnp.concatenate(weights, axis=0)
    total = tall_product(window, *high_low(weight))
    return total


def adjoint_kernel(mine_ref, taps_ref, total_ref, rows_ref):
    part = lax.rem(lax.axis_index("lat"), 2)
    total_ref[...] = partial_adjoint(mine_ref, taps_ref, rows_ref, part)


def last_kernel(
    mine_ref, other_ref, field_ref, cot_ref, taps_ref, total_ref, out_ref, grad_ref, gain_ref, rows_ref
):
    half = cot_ref.shape[0] // 2
    part = lax.rem(lax.axis_index("lat"), 2)
    for message_ref, side in ((mine_ref, part), (other_ref, 1 - part)):
        for owner in range(half // 8):
            here = pl.ds(pl.multiple_of(half * side + 8 * owner, 8), 8)
            start = BACK * owner
            first, second = message_ref[start : start + 8, :], message_ref[start + 8 : start + 16, :]
            out_ref[here, :] = field_ref[here, :] + jnp.where(part == 0, first, second)
            gain_ref[0, here, :] = message_ref[start + 40 : start + 48, :]
            gain_ref[1, here, :] = message_ref[start + 48 : start + 56, :]
    total = total_ref[...] + partial_adjoint(other_ref, taps_ref, rows_ref, 1 - part)
    grad_ref[...] = cot_ref[...] + total.T


def transform_tables(columns, lon):
    places = np.arange(columns)
    turn = 2.0 * np.pi * (np.arange(lon)[:, None] * places[None, :]) / (lon * columns)
    angle = 2.0 * np.pi * (places[:, None] * places[None, :] % columns) / columns
    cosine, sine = np.cos(angle), np.sin(angle)
    dft = np.block([[cosine, -sine], [sine, cosine]])
    turns = np.concatenate([np.cos(turn), np.sin(turn)], axis=0)
    return jnp.asarray(turns, jnp.float32), jnp.asarray(dft, jnp.float32)


def exchanged(flat, lat, lon):
    rows, columns = flat.shape
    members = [(chip, place) for chip in range(lat // 2) for place in range(lon)]
    members.sort(key=lambda member: rank(*member))
    groups = [[(2 * chip + core) * lon + place for chip, place in members] for core in range(2)]
    moved = lax.all_to_all(
        flat.reshape(rows, 1, columns),
        ("lat", "lon"),
        0,
        0,
        tiled=True,
        axis_index_groups=groups,
    )
    return moved.reshape(rows, columns)


def in_hbm(x):
    return pltpu.with_memory_space_constraint(x, pltpu.HBM)


def on_device(field, cotangent, conv_weight, spectral_filter):
    channels, _, columns = field.shape
    lat, lon = lax.axis_size("lat"), lax.axis_size("lon")
    owners = lat * lon // 2
    swap = [(i, i ^ 1) for i in range(lat)]
    own = field.reshape(channels, columns)
    cot = cotangent.reshape(channels, columns)
    vmem = pl.BlockSpec(memory_space=pltpu.VMEM)
    hbm = pl.BlockSpec(memory_space=pltpu.HBM)
    params = pltpu.CompilerParams(vmem_limit_bytes=16 * 1024 * 1024)
    flat = jax.ShapeDtypeStruct((channels, columns), jnp.float32)
    half_taps = jax.ShapeDtypeStruct((3, 3, channels // 2, channels), jnp.float32)
    forth = jax.ShapeDtypeStruct((owners * FORTH, columns), jnp.float32)
    back = jax.ShapeDtypeStruct((owners * BACK, columns), jnp.float32)
    other, other_cot = lax.ppermute((own, cot), "lat", swap)
    gain_half = jax.ShapeDtypeStruct((channels // 2, columns), jnp.float32)
    own_here, cot_here, gain, taps = pl.pallas_call(
        fetch_kernel,
        out_shape=(flat, flat, gain_half, half_taps),
        in_specs=[hbm] * 4,
        out_specs=(vmem,) * 4,
        scratch_shapes=[pltpu.SemaphoreType.DMA((6,))],
        compiler_params=params,
        name="fetch",
    )(*map(in_hbm, (own, cot, spectral_filter, conv_weight)))
    outgoing = pl.pallas_call(
        conv_kernel,
        out_shape=forth,
        in_specs=[vmem] * 6 + [hbm],
        out_specs=vmem,
        scratch_shapes=[
            pltpu.VMEM((9, channels // 2, channels), jnp.float32),
            pltpu.SemaphoreType.DMA((9,)),
        ],
        compiler_params=params,
        name="conv",
    )(own_here, other, cot_here, other_cot, gain, taps, in_hbm(conv_weight))
    turns, dft = transform_tables(columns, lon)
    returned = pl.pallas_call(
        spectral_kernel,
        out_shape=back,
        in_specs=[vmem] * 3,
        out_specs=vmem,
        scratch_shapes=[pltpu.VMEM((2 * 8 * lat * lon, 2 * columns), jnp.float32)],
        compiler_params=params,
        name="spectral",
    )(exchanged(outgoing, lat, lon), turns, dft)
    mine = exchanged(returned, lat, lon)
    other = lax.ppermute(mine, "lat", swap)
    rows_scratch = pltpu.VMEM((5, columns + 16, channels // 2), jnp.float32)
    total = pl.pallas_call(
        adjoint_kernel,
        out_shape=jax.ShapeDtypeStruct((columns, channels), jnp.float32),
        in_specs=[vmem] * 2,
        out_specs=vmem,
        scratch_shapes=[rows_scratch],
        compiler_params=params,
        name="adjoint",
    )(mine, conv_weight)
    output, input_grad, filter_grad = pl.pallas_call(
        last_kernel,
        out_shape=(flat, flat, jax.ShapeDtypeStruct(spectral_filter.shape, jnp.float32)),
        in_specs=[vmem] * 6,
        out_specs=(vmem, vmem, vmem),
        scratch_shapes=[rows_scratch],
        compiler_params=params,
        name="last",
    )(mine, other, own, cot, conv_weight, total)
    return (output.reshape(field.shape), input_grad.reshape(field.shape), filter_grad)


def solution(mesh):
    placed = (P(None, "lat", "lon"), P(None, "lat", "lon"), P(), P(None, None, "lon"))
    specs = (P(None, "lat", "lon"), P(None, "lat", "lon"), P(None, None, "lon"))

    def layer(field, cotangent, conv_weight, spectral_filter):
        lat, lon = mesh.shape["lat"], mesh.shape["lon"]
        channels, rows, length = field.shape
        owned = rows == lat == 4 and lon == 8 and channels == 8 * lat * lon and length == 128 * lon
        body = on_device if owned else on_device_any_mesh
        mapped = jax.shard_map(body, mesh=mesh, in_specs=placed, out_specs=specs, check_vma=False)
        return mapped(field, cotangent, conv_weight, spectral_filter)

    return layer
```

```python
from functools import partial

import jax
import jax.numpy as jnp
import numpy as np
from jax import lax
from jax.experimental import pallas as pl
from jax.experimental.pallas import tpu as pltpu
from jax.sharding import PartitionSpec as P

precise = lax.Precision.HIGHEST
three_pass = lax.Precision.HIGH
ROOT_HALF = 0.5**0.5


def padded_2(array, sides, width, wrap):
    for axis, dim in sides:
        peers, length = (lax.axis_size(axis), array.shape[dim])
        up = [(i, (i + 1) % peers) for i in range(peers if wrap else peers - 1)]
        down = [(j, i) for i, j in up]
        last = lax.slice_in_dim(array, length - width, length, axis=dim)
        leading = lax.slice_in_dim(array, 0, width, axis=dim)
        before = lax.ppermute(last, axis, up)
        after = lax.ppermute(leading, axis, down)
        array = jnp.concatenate([before, array, after], axis=dim)
    return array


def partner(array, axis, stride):
    return lax.ppermute(array, axis, [(i, i ^ 1 << stride) for i in range(lax.axis_size(axis))])


def angle_table(first, second, modulus):
    product = first[:, None] * second[None, :] % modulus
    return 2.0 * jnp.pi / modulus * product.astype(jnp.float32)


def apply_taps(padded, taps, lat_rows, columns):
    total = jnp.zeros((taps.shape[2], lat_rows, columns), jnp.float32)
    for tap_row in range(3):
        for tap_col in range(3):
            window = padded[:, tap_row : tap_row + lat_rows, tap_col : tap_col + columns]
            total = total + jnp.einsum(
                "oi,iab->oab", taps[tap_row, tap_col], window, precision=precise
            )
    return total


def with_rims(field):
    wider = padded_2(field, (("lon", 2),), 1, True)
    return padded_2(wider, (("lat", 1),), 1, False)


def local_forward(real_part, imag_part):
    columns = real_part.shape[-1]
    places = lax.iota(jnp.int32, columns)
    angles = angle_table(places, places, columns)
    cosine = jnp.cos(angles)
    sine = jnp.sin(angles)
    out_real = jnp.dot(real_part, cosine, precision=precise) + jnp.dot(
        imag_part, sine, precision=precise
    )
    out_imag = jnp.dot(imag_part, cosine, precision=precise) - jnp.dot(
        real_part, sine, precision=precise
    )
    return (out_real, out_imag)


def local_inverse(real_part, imag_part):
    columns = real_part.shape[-1]
    places = lax.iota(jnp.int32, columns)
    angles = angle_table(places, places, columns)
    cosine = jnp.cos(angles)
    sine = jnp.sin(angles)
    out_real = jnp.dot(real_part, cosine, precision=precise) - jnp.dot(
        imag_part, sine, precision=precise
    )
    out_imag = jnp.dot(imag_part, cosine, precision=precise) + jnp.dot(
        real_part, sine, precision=precise
    )
    return (out_real / columns, out_imag / columns)


def section_angles(place, bit_pos, columns):
    offsets = lax.iota(jnp.int32, columns)
    start = place % 2**bit_pos * columns
    span = 2 * columns * 2**bit_pos
    angles = 2.0 * jnp.pi / span * (start + offsets).astype(jnp.float32)
    upper = place // 2**bit_pos % 2 == 1
    return (jnp.cos(angles), jnp.sin(angles), upper)


def forward_pairs(field):
    extent = lax.axis_size("lon")
    width_bits = extent.bit_length() - 1
    place = lax.axis_index("lon")
    columns = field.shape[-1]
    data = jnp.stack([field, jnp.zeros_like(field)])
    for bit_pos in reversed(range(width_bits)):
        other = partner(data, "lon", bit_pos)
        cosine, sine, upper = section_angles(place, bit_pos, columns)
        differ = other - data
        turned = jnp.stack(
            [differ[0] * cosine + differ[1] * sine, differ[1] * cosine - differ[0] * sine]
        )
        data = jnp.where(upper, turned, data + other)
    out_real, out_imag = local_forward(data[0], data[1])
    return jnp.stack([out_real, out_imag])


def inverse_pairs(spectrum):
    extent = lax.axis_size("lon")
    width_bits = extent.bit_length() - 1
    place = lax.axis_index("lon")
    columns = spectrum.shape[-1]
    back_real, back_imag = local_inverse(spectrum[0], spectrum[1])
    data = jnp.stack([back_real, back_imag])
    for bit_pos in range(width_bits):
        cosine, sine, upper = section_angles(place, bit_pos, columns)
        turned = jnp.stack([data[0] * cosine - data[1] * sine, data[1] * cosine + data[0] * sine])
        outgoing = jnp.where(upper, turned, data)
        other = partner(outgoing, "lon", bit_pos)
        data = jnp.where(upper, other - outgoing, outgoing + other) * 0.5
    return data[0]


def on_device_any_mesh(field, cotangent, conv_weight, spectral_filter):
    lat_rows = field.shape[1]
    columns = field.shape[2]
    total_len = columns * lax.axis_size("lon")
    mixed = apply_taps(with_rims(field), conv_weight, lat_rows, columns)
    hidden_spec = forward_pairs(mixed)
    cot_spec = forward_pairs(cotangent)
    gain_real = spectral_filter[0][:, None, :]
    gain_imag = spectral_filter[1][:, None, :]
    filtered = jnp.stack(
        [
            gain_real * hidden_spec[0] - gain_imag * hidden_spec[1],
            gain_real * hidden_spec[1] + gain_imag * hidden_spec[0],
        ]
    )
    adjoint = jnp.stack(
        [
            gain_real * cot_spec[0] + gain_imag * cot_spec[1],
            gain_real * cot_spec[1] - gain_imag * cot_spec[0],
        ]
    )
    shaped = inverse_pairs(filtered)
    back_field = inverse_pairs(adjoint)
    output = field + shaped
    local_grad = (
        jnp.stack(
            [
                jnp.sum(hidden_spec[0] * cot_spec[0] + hidden_spec[1] * cot_spec[1], axis=1),
                jnp.sum(hidden_spec[0] * cot_spec[1] - hidden_spec[1] * cot_spec[0], axis=1),
            ]
        )
        / total_len
    )
    filter_grad = lax.psum(local_grad, "lat")
    flipped_taps = jnp.transpose(conv_weight[::-1, ::-1], (0, 1, 3, 2))
    input_grad = cotangent + apply_taps(with_rims(back_field), flipped_taps, lat_rows, columns)
    return (output, input_grad, filter_grad)


FORTH, BACK = 49, 57


def rank(chip, place):
    upper, odd, x = place // 4, place // 2 % 2, place % 2
    return 8 * ((upper + odd + 1) % 2) + 4 * (1 - x) + 2 * (1 - chip) + 1 - upper


def reversed_bits(value, width):
    return int(format(value, f"0{width}b")[::-1], 2)


def iotas(rows, columns):
    lane = lax.broadcasted_iota(jnp.int32, (rows, columns), 1)
    row = lax.broadcasted_iota(jnp.int32, (rows, columns), 0)
    return lane, row


def fetch_kernel(
    own_ref, cot_ref, filter_ref, taps_ref, own_out, cot_out, gain_out, taps_out, sems
):
    place = lax.axis_index("lat")
    odd, half = lax.rem(place, 2), gain_out.shape[0]
    span = pl.ds(pl.multiple_of(odd * half, half), half)
    copies = [
        pltpu.make_async_copy(own_ref, own_out, sems.at[0]),
        pltpu.make_async_copy(cot_ref, cot_out, sems.at[1]),
        pltpu.make_async_copy(filter_ref.at[place // 2, span], gain_out, sems.at[2]),
    ]

    @pl.when(odd == 1)
    def _():
        half_taps = pltpu.make_async_copy(taps_ref.at[:, :, half:], taps_out, sems.at[3])
        for copy in [half_taps] + copies:
            copy.start()
        for copy in [half_taps] + copies:
            copy.wait()

    @pl.when(odd == 0)
    def _():
        for copy in copies:
            copy.start()
        for copy in copies:
            copy.wait()


def high_low(x):
    high = x.astype(jnp.bfloat16)
    return high, (x - high.astype(jnp.float32)).astype(jnp.bfloat16)


def tall_product(x, high, low):
    rows = x.shape[0]
    x_high, x_low = high_low(x)
    both = jnp.concatenate([x_high, x_low], axis=0)
    both = jnp.dot(both, high, preferred_element_type=jnp.float32)
    rest = jnp.dot(x_high, low, preferred_element_type=jnp.float32)
    return both[:rows] + (both[rows:] + rest)


def conv_kernel(
    own_ref, other_ref, cot_ref, other_cot_ref, gain_ref, half_ref, taps_ref, out_ref, taps, sems
):
    odd, upper = lax.rem(lax.axis_index("lat"), 2), lax.axis_index("lat") // 2
    half = gain_ref.shape[0]
    order = [(row, col) for col in range(3) for row in (1, 2 * upper, 2 - 2 * upper)]

    @pl.when(odd == 0)
    def _():
        copies = [
            pltpu.make_async_copy(taps_ref.at[row, col, :half], taps.at[index], sems.at[index])
            for index, (row, col) in enumerate(order)
        ]
        for copy in copies:
            copy.start()

        def weights(index):
            copies[index].wait()
            return high_low(taps[index])

        pack((own_ref, other_ref), (cot_ref, other_cot_ref), gain_ref, weights, 0, out_ref)

    @pl.when(odd == 1)
    def _():
        def weights(index):
            return high_low(half_ref[order[index]])

        pack((other_ref, own_ref), (other_cot_ref, cot_ref), gain_ref, weights, 1, out_ref)


def pack(fields, cots, gain_ref, weights, core, out_ref):
    upper = lax.axis_index("lat") // 2
    half, columns = gain_ref.shape
    for owner in range(half // 8):
        first, here = FORTH * owner, half * core + 8 * owner
        out_ref[first : first + 8, :] = cots[0][here : here + 8, :]
        out_ref[first + 8 : first + 16, :] = cots[1][here : here + 8, :]
        out_ref[first + 40 : first + 48, :] = gain_ref[8 * owner : 8 * owner + 8, :]
    row_0, row_1 = fields[0][...], fields[1][...]
    near = jnp.concatenate(high_low(jnp.where(upper == 0, row_1, row_0)), axis=1)
    both_high, both_low = high_low(jnp.concatenate([row_0, row_1], axis=1))

    def times(weights, values):
        return jnp.dot(weights, values, preferred_element_type=jnp.float32)

    parts = []
    for tap_col in range(3):
        high, low = weights(3 * tap_col)
        middle = times(high, both_high) + (times(high, both_low) + times(low, both_high))
        high, low = weights(3 * tap_col + 1)
        outer = times(high, both_high) + (times(high, both_low) + times(low, both_high))
        high, low = weights(3 * tap_col + 2)
        wide = times(high, near)
        inner = wide[:, :columns] + (wide[:, columns:] + times(low, near[:, :columns]))
        on_0, on_1 = outer[:, :columns], outer[:, columns:]
        parts.append(
            jnp.concatenate(
                [
                    middle[:, :columns] + jnp.where(upper == 0, inner, on_1),
                    middle[:, columns:] + jnp.where(upper == 0, on_0, inner),
                    jnp.where(upper == 0, on_1, on_0),
                ],
                axis=0,
            )
        )
    lane, row = iotas(3 * half, columns)
    left, middle, right = parts
    main = (
        middle
        + jnp.where(lane == 0, 0.0, pltpu.roll(left, 1, 1))
        + jnp.where(lane == columns - 1, 0.0, pltpu.roll(right, columns - 1, 1))
    )
    slot = lane - lax.rem(row, 8) - 8 * (row // half)
    edges = jnp.where(slot == 0, left[:, columns - 1 :], 0.0)
    edges = jnp.where(slot == 24, right[:, 0:1], edges)
    edges = edges[:half] + edges[half : 2 * half] + edges[2 * half :]
    for owner in range(half // 8):
        first = FORTH * owner
        for part in range(3):
            here = half * part + 8 * owner
            out_ref[first + 16 + 8 * part : first + 24 + 8 * part, :] = main[here : here + 8]
        out_ref[first + 48 : first + 49, :] = jnp.sum(
            edges[8 * owner : 8 * owner + 8], axis=0, keepdims=True
        )


def transform_8(x):
    s = [x[d] + x[d + 4] for d in range(4)]
    t = [x[d] - x[d + 4] for d in range(4)]
    plus, minus = ROOT_HALF * (t[1] + t[3]), ROOT_HALF * (t[1] - t[3])
    return [
        (s[0] + s[2] + (s[1] + s[3]), None),
        (t[0] + minus, -t[2] - plus),
        (s[0] - s[2], s[3] - s[1]),
        (t[0] - minus, t[2] - plus),
        (s[0] + s[2] - (s[1] + s[3]), None),
    ]


def spectral_kernel(in_ref, turn_ref, dft_ref, out_ref, work):
    rows, lon = 4, 8
    columns = in_ref.shape[-1]
    lane, sub = iotas(8, columns)
    me = rank(lax.axis_index("lat") // 2, lax.axis_index("lon"))

    def message(chip, place, first, count):
        start = FORTH * rank(chip, place) + first
        return in_ref[start : start + count, :]

    def edge(row, place, group):
        chip, part = row // 2, row % 2
        wanted = lane == sub + 8 * part + 24 * group
        line = jnp.where(wanted, message(chip, place, 48, 1), 0.0)
        if row in (1, 2):
            wanted = lane == sub + 16 + 24 * group
            line = line + jnp.where(wanted, message(1 - chip, place, 48, 1), 0.0)
        return jnp.sum(line, axis=1, keepdims=True)

    grid = []
    for place in range(lon):
        mixed = []
        for row in range(rows):
            tile = message(row // 2, place, 16 + 8 * (row % 2), 8)
            if row in (1, 2):
                tile = tile + message(1 - row // 2, place, 32, 8)
            tile = tile + jnp.where(lane == 0, edge(row, (place - 1) % lon, 0), 0.0)
            tile = tile + jnp.where(lane == columns - 1, edge(row, (place + 1) % lon, 1), 0.0)
            mixed.append(tile)
        cot = [message(row // 2, place, 8 * (row % 2), 8) for row in range(rows)]
        grid.append(jnp.concatenate(mixed + cot, axis=0))
    pairs = transform_8(grid)
    height = 16 * rows
    for residue in range(lon):
        real, imag = pairs[min(residue, lon - residue)]
        cosine, sine = turn_ref[residue : residue + 1, :], turn_ref[8 + residue : 9 + residue, :]
        if imag is None:
            turned = (real * cosine, -real * sine)
        elif residue < 4:
            turned = (real * cosine + imag * sine, imag * cosine - real * sine)
        else:
            turned = (real * cosine - imag * sine, -imag * cosine - real * sine)
        span = pl.ds(residue * height, height)
        work[span, 0:columns] = turned[0]
        work[span, columns:] = turned[1]
    chunk = lon * height // 4
    pieces = [pl.ds(first, chunk) for first in range(0, lon * height, chunk)]
    table = dft_ref[...]
    spectra = jnp.concatenate(
        [jnp.dot(work[piece], table, precision=three_pass) for piece in pieces], axis=0
    )
    scale = 1.0 / (lon * columns)
    half = 8 * rows
    gradients = []
    for residue in range(lon):
        place = reversed_bits(residue, 3)
        part = spectra[residue * height : (residue + 1) * height]
        mix_re, mix_im = part[:half, :columns], part[:half, columns:]
        cot_re, cot_im = part[half:, :columns], part[half:, columns:]
        gain_re = jnp.concatenate([message(0, place, 40, 8) * scale] * rows, axis=0)
        gain_im = jnp.concatenate([message(1, place, 40, 8) * scale] * rows, axis=0)
        top = pl.ds(residue * height, half)
        bottom = pl.ds(residue * height + half, half)
        work[top, 0:columns] = gain_re * mix_re - gain_im * mix_im
        work[top, columns:] = -(gain_re * mix_im + gain_im * mix_re)
        work[bottom, 0:columns] = gain_re * cot_re + gain_im * cot_im
        work[bottom, columns:] = gain_im * cot_re - gain_re * cot_im
        grad_re = (mix_re * cot_re + mix_im * cot_im) * scale
        grad_im = (mix_re * cot_im - mix_im * cot_re) * scale
        gradients.append(
            [
                grad[0:8] + grad[8:16] + (grad[16:24] + grad[24:32])
                for grad in (grad_re, grad_im)
            ]
        )
    back = jnp.concatenate(
        [jnp.dot(work[piece], table, precision=three_pass) for piece in pieces], axis=0
    )
    turned = []
    for residue in range(lon):
        part = back[residue * height : (residue + 1) * height]
        real, imag = part[:, :columns], part[:, columns:]
        cosine, sine = turn_ref[residue : residue + 1, :], turn_ref[8 + residue : 9 + residue, :]
        turned.append((real * cosine + imag * sine, real * sine - imag * cosine))
    sums = [turned[r][0] + turned[lon - r][0] for r in (1, 2, 3)]
    gaps = [turned[r][1] - turned[lon - r][1] for r in (1, 2, 3)]
    first, fourth = turned[0][0], turned[4][0]
    even = [
        first + fourth + sums[1],
        first - fourth - gaps[1],
        first + fourth - sums[1],
        first - fourth + gaps[1],
    ]
    swing = [
        sums[0] + sums[2],
        ROOT_HALF * (sums[0] - gaps[0] - sums[2] - gaps[2]),
        gaps[2] - gaps[0],
        ROOT_HALF * (sums[2] - gaps[2] - sums[0] - gaps[0]),
    ]
    series = [even[d] + swing[d] for d in range(4)] + [even[d] - swing[d] for d in range(4)]
    slots = [lane == 8 * lax.rem(me + group, 16) + sub for group in range(6)]
    for place in range(lon):
        residue = reversed_bits(place, 3)
        before, after = series[(place - 1) % lon], series[(place + 1) % lon]
        for chip in range(2):
            start = BACK * rank(chip, place)
            rims = jnp.zeros((8, columns), jnp.float32)
            for step in range(3):
                here = half + 8 * (chip + step)
                span = slice(here, here + 8)
                rims = jnp.where(slots[2 * step], before[span, columns - 1 :], rims)
                rims = jnp.where(slots[2 * step + 1], after[span, 0:1], rims)
                first = start + 16 + 8 * step
                out_ref[first : first + 8, :] = series[place][span]
            out_ref[start : start + 16, :] = series[place][16 * chip : 16 * chip + 16]
            for part in range(2):
                first = start + 40 + 8 * part
                out_ref[first : first + 8, :] = gradients[residue][part]
            out_ref[start + 56 : start + 57, :] = jnp.sum(rims, axis=0, keepdims=True)


def partial_adjoint(message_ref, taps_ref, rows_ref, part):
    half, columns = rows_ref.shape[-1], message_ref.shape[-1]
    place = lax.axis_index("lat")
    index = place - place // 2
    owners = half // 8
    lines = message_ref[pl.ds(56, owners, stride=BACK), :]
    lane, owner = iotas(owners, columns)
    rows_ref[0] = jnp.zeros(rows_ref.shape[1:], jnp.float32)
    rows_ref[4] = jnp.zeros(rows_ref.shape[1:], jnp.float32)
    for step in range(3):
        pieces = [
            message_ref[BACK * j + 16 + 8 * step : BACK * j + 24 + 8 * step, :] for j in range(owners)
        ]
        rows_ref[1 + step, 8 : 8 + columns, :] = jnp.concatenate(pieces, axis=0).T
        for rim, target in ((2 * step, 7), (2 * step + 1, 8 + columns)):
            wanted = lane // 8 == lax.rem(owner + rim, owners)
            line = jnp.sum(jnp.where(wanted, lines, 0.0), axis=0, keepdims=True)
            line = jnp.broadcast_to(line, (8, columns))
            if rim:
                line = pltpu.roll(line, columns - 8 * rim, 1)
            rows_ref[1 + step, target : target + 1, :] = line[0:1]
    span = pl.ds(pl.multiple_of(part * half, half), half)
    windows, weights = [], []
    for tap_row in range(3):
        for tap_col in range(3):
            first = 9 - tap_col
            windows.append(rows_ref[index + 2 - tap_row, first : first + columns, :])
            weights.append(taps_ref[tap_row, tap_col, span])
    total = 0.0
    for pair in range(0, 9, 2):
        window = jnp.concatenate(windows[pair : pair + 2], axis=1)
        weight = jnp.concatenate(weights[pair : pair + 2], axis=0)
        total = total + tall_product(window, *high_low(weight))
    return total


def adjoint_kernel(mine_ref, taps_ref, total_ref, rows_ref):
    part = lax.rem(lax.axis_index("lat"), 2)
    total_ref[...] = partial_adjoint(mine_ref, taps_ref, rows_ref, part)


def last_kernel(
    mine_ref, other_ref, field_ref, cot_ref, taps_ref, total_ref, out_ref, grad_ref, gain_ref, rows_ref
):
    half = cot_ref.shape[0] // 2
    part = lax.rem(lax.axis_index("lat"), 2)
    for message_ref, side in ((mine_ref, part), (other_ref, 1 - part)):
        for owner in range(half // 8):
            here = pl.ds(pl.multiple_of(half * side + 8 * owner, 8), 8)
            start = BACK * owner
            first, second = message_ref[start : start + 8, :], message_ref[start + 8 : start + 16, :]
            out_ref[here, :] = field_ref[here, :] + jnp.where(part == 0, first, second)
            gain_ref[0, here, :] = message_ref[start + 40 : start + 48, :]
            gain_ref[1, here, :] = message_ref[start + 48 : start + 56, :]
    total = total_ref[...] + partial_adjoint(other_ref, taps_ref, rows_ref, 1 - part)
    grad_ref[...] = cot_ref[...] + total.T


def transform_tables(columns, lon):
    places = np.arange(columns)
    turn = 2.0 * np.pi * (np.arange(lon)[:, None] * places[None, :]) / (lon * columns)
    angle = 2.0 * np.pi * (places[:, None] * places[None, :] % columns) / columns
    cosine, sine = np.cos(angle), np.sin(angle)
    dft = np.block([[cosine, -sine], [sine, cosine]])
    turns = np.concatenate([np.cos(turn), np.sin(turn)], axis=0)
    return jnp.asarray(turns, jnp.float32), jnp.asarray(dft, jnp.float32)


def exchanged(flat, lat, lon):
    rows, columns = flat.shape
    members = [(chip, place) for chip in range(lat // 2) for place in range(lon)]
    members.sort(key=lambda member: rank(*member))
    groups = [[(2 * chip + core) * lon + place for chip, place in members] for core in range(2)]
    moved = lax.all_to_all(
        flat.reshape(rows, 1, columns),
        ("lat", "lon"),
        0,
        0,
        tiled=True,
        axis_index_groups=groups,
    )
    return moved.reshape(rows, columns)


def in_hbm(x):
    return pltpu.with_memory_space_constraint(x, pltpu.HBM)


def on_device(field, cotangent, conv_weight, spectral_filter):
    channels, _, columns = field.shape
    lat, lon = lax.axis_size("lat"), lax.axis_size("lon")
    owners = lat * lon // 2
    swap = [(i, i ^ 1) for i in range(lat)]
    own = field.reshape(channels, columns)
    cot = cotangent.reshape(channels, columns)
    vmem = pl.BlockSpec(memory_space=pltpu.VMEM)
    hbm = pl.BlockSpec(memory_space=pltpu.HBM)
    params = pltpu.CompilerParams(vmem_limit_bytes=16 * 1024 * 1024)
    flat = jax.ShapeDtypeStruct((channels, columns), jnp.float32)
    half_taps = jax.ShapeDtypeStruct((3, 3, channels // 2, channels), jnp.float32)
    forth = jax.ShapeDtypeStruct((owners * FORTH, columns), jnp.float32)
    back = jax.ShapeDtypeStruct((owners * BACK, columns), jnp.float32)
    other, other_cot = lax.ppermute((own, cot), "lat", swap)
    gain_half = jax.ShapeDtypeStruct((channels // 2, columns), jnp.float32)
    own_here, cot_here, gain, taps = pl.pallas_call(
        fetch_kernel,
        out_shape=(flat, flat, gain_half, half_taps),
        in_specs=[hbm] * 4,
        out_specs=(vmem,) * 4,
        scratch_shapes=[pltpu.SemaphoreType.DMA((4,))],
        compiler_params=params,
        name="fetch",
    )(*map(in_hbm, (own, cot, spectral_filter, conv_weight)))
    outgoing = pl.pallas_call(
        conv_kernel,
        out_shape=forth,
        in_specs=[vmem] * 6 + [hbm],
        out_specs=vmem,
        scratch_shapes=[
            pltpu.VMEM((9, channels // 2, channels), jnp.float32),
            pltpu.SemaphoreType.DMA((9,)),
        ],
        compiler_params=params,
        name="conv",
    )(own_here, other, cot_here, other_cot, gain, taps, in_hbm(conv_weight))
    turns, dft = transform_tables(columns, lon)
    returned = pl.pallas_call(
        spectral_kernel,
        out_shape=back,
        in_specs=[vmem] * 3,
        out_specs=vmem,
        scratch_shapes=[pltpu.VMEM((2 * 8 * lat * lon, 2 * columns), jnp.float32)],
        compiler_params=params,
        name="spectral",
    )(exchanged(outgoing, lat, lon), turns, dft)
    mine = exchanged(returned, lat, lon)
    other = lax.ppermute(mine, "lat", swap)
    rows_scratch = pltpu.VMEM((5, columns + 16, channels // 2), jnp.float32)
    total = pl.pallas_call(
        adjoint_kernel,
        out_shape=jax.ShapeDtypeStruct((columns, channels), jnp.float32),
        in_specs=[vmem] * 2,
        out_specs=vmem,
        scratch_shapes=[rows_scratch],
        compiler_params=params,
        name="adjoint",
    )(mine, conv_weight)
    output, input_grad, filter_grad = pl.pallas_call(
        last_kernel,
        out_shape=(flat, flat, jax.ShapeDtypeStruct(spectral_filter.shape, jnp.float32)),
        in_specs=[vmem] * 6,
        out_specs=(vmem, vmem, vmem),
        scratch_shapes=[rows_scratch],
        compiler_params=params,
        name="last",
    )(mine, other, own, cot, conv_weight, total)
    return (output.reshape(field.shape), input_grad.reshape(field.shape), filter_grad)


def solution(mesh):
    placed = (P(None, "lat", "lon"), P(None, "lat", "lon"), P(), P(None, None, "lon"))
    specs = (P(None, "lat", "lon"), P(None, "lat", "lon"), P(None, None, "lon"))

    def layer(field, cotangent, conv_weight, spectral_filter):
        lat, lon = mesh.shape["lat"], mesh.shape["lon"]
        channels, rows, length = field.shape
        owned = rows == lat == 4 and lon == 8 and channels == 8 * lat * lon and length == 128 * lon
        body = on_device if owned else on_device_any_mesh
        mapped = jax.shard_map(body, mesh=mesh, in_specs=placed, out_specs=specs, check_vma=False)
        return mapped(field, cotangent, conv_weight, spectral_filter)

    return layer
```
